32 devices in a mesh: groups: 2 (over y), expert: 4 (over z), dp: 4 (over x, core).
Axes of the slice: x: 2, y: 2, z: 4, core: 2. Of those that a mesh axis runs over, the one named last changes fastest.
Arguments:
- tokens: bfloat16 [1024, 2560], P(('groups', 'expert'), 'dp'), parts along dimension 0, may hold values from -6 to 6
- out_grad: bfloat16 [1024, 2560], P(('groups', 'expert'), 'dp'), parts along dimension 0, may hold values from -6 to 6
- gate_weights: float32 [1024, 2], P(('groups', 'expert')), parts along dimension 0, may hold values from 0.1 to 0.5
- expert_ids: int32 [1024, 2], P(('groups', 'expert')), parts along dimension 0, may hold values from 0 to 3, as said below
- replica_plan: int32 [4, 2], P('groups'), parts along dimension 0, may hold values from 0 to 3, as said below
- cap_blocks: int32 [8], P('groups'), parts along dimension 0, may hold values from 1 to 2, as said below
- gate_weight: bfloat16 [4, 2560, 768], P('expert', 'dp'), may hold values from -0.125 to 0.125
- up_weight: bfloat16 [4, 2560, 768], P('expert', 'dp'), may hold values from -0.125 to 0.125
- down_weight: bfloat16 [4, 768, 2560], P('expert', None, 'dp'), may hold values from -0.21875 to 0.21875
Outputs:
- mixed: bfloat16 [1024, 2560], P(('groups', 'expert'), 'dp'), parts along dimension 0
- token_grad: bfloat16 [1024, 2560], P(('groups', 'expert'), 'dp'), parts along dimension 0
- gate_grad: bfloat16 [8, 2560, 768], P(('groups', 'expert'), 'dp'), parts along dimension 0
- up_grad: bfloat16 [8, 2560, 768], P(('groups', 'expert'), 'dp'), parts along dimension 0
- down_grad: bfloat16 [8, 768, 2560], P(('groups', 'expert'), None, 'dp'), parts along dimension 0
The draws below stay inside these ranges and needn't reach their ends.
There are 2 independent parts, one for each index of `groups`. The reference program is written for one: setup_inputs(seed, part) draws one part's arguments, and reference() takes and returns one part's arrays. A program takes and returns all parts, laid end to end along the dimension named above; an argument that names none is the same for every part. Nothing has to cross between parts.
Inputs may be any that keep to these rules, and one draw needn't show every extreme that they name: `expert_ids`: each row names 2 different experts. `replica_plan`: every number 0 to 3 appears once; entry [i, 0] is the i-th hot expert and the rest of row i are the expert devices that hold its replicas. `cap_blocks`: capacity of expert device d for rows of its own expert from one source, in blocks of 4 rows.
All inputs are finite; a program needn't handle non-finite values.
Results may differ from the reference program's by a relative error of at most 0.018.
Values may be sent and summed in bfloat16 or wider, within the bound.
No kernel may reach another device: no remote copies, remote signals or barrier semaphores. Data moves between devices by JAX's collectives and lax.ppermute only.
A program may use at most 128 MiB of HBM per device.

```python
import jax
import jax.numpy as jnp
from jax import lax

D = 2560
FF = 768
TOK_DEV = 128
BLK = 4
MAXB = 2
SPARE = 2
EXPERTS = 4
TOP = 2
HOT_HOST_DEVICES = 2
CAPM = 8
TOKEN_TOTAL = 512
N_DP = 4


def hot_order(key):
    return jax.random.permutation(key, EXPERTS).astype(jnp.int32)


def draw_replica_plan(key, part):
    sorted_index = hot_order(key)
    return sorted_index.reshape(2, HOT_HOST_DEVICES).astype(jnp.int32)


def draw_expert_ids(key, part):
    sorted_index = hot_order(key)
    key = jax.random.fold_in(key, 7)
    ranking_key, reward_key = jax.random.split(key)
    column_indices = jnp.arange(EXPERTS, dtype=jnp.int32)
    router_logits = jax.random.randint(ranking_key, (TOKEN_TOTAL, EXPERTS), 0, 2 ** 20, dtype=jnp.int32) * EXPERTS + column_indices[None, :]
    match_count = jax.random.randint(reward_key, (TOKEN_TOTAL, 2), 0, 2, dtype=jnp.int32)
    extra_reward = match_count[:, 0:1] * (column_indices == sorted_index[0]).astype(jnp.int32)[None, :]
    extra_reward = extra_reward + match_count[:, 1:2] * (column_indices == sorted_index[HOT_HOST_DEVICES]).astype(jnp.int32)[None, :]
    router_logits = router_logits + extra_reward * 2 ** 26
    unused, picked = lax.top_k(router_logits, TOP)
    return picked.astype(jnp.int32)


def draw_cap_blocks(key, part):
    key = jax.random.fold_in(key, 5)
    value_key, first_key, step_key = jax.random.split(key, 3)
    blocks = jax.random.randint(value_key, (EXPERTS,), 1, MAXB + 1, dtype=jnp.int32)
    first = jax.random.randint(first_key, (), 0, EXPERTS, dtype=jnp.int32)
    stride = jax.random.randint(step_key, (), 1, EXPERTS, dtype=jnp.int32)
    blocks = blocks.at[first].set(MAXB)
    blocks = blocks.at[(first + stride) % EXPERTS].set(1)
    return blocks.astype(jnp.int32)


def levels(own_key, extent, pieces, least, largest):
    level, own = 1.0, jax.random.fold_in(own_key, 6)
    for axis_at, blocks in pieces:
        draws = jnp.exp(jax.random.uniform(jax.random.fold_in(own, axis_at), (blocks,), jnp.float32, least / len(pieces), largest / len(pieces)))
        level = level * jnp.repeat(draws, extent[axis_at] // blocks).reshape([-1 if axis == axis_at else 1 for axis in range(len(extent))])
    return level


def noise(rng, extent, scale, most, shards=(), kind=jnp.bfloat16):
    level = levels(rng, extent, shards, -0.22, 0.18) if shards else 1.0
    drawn = jax.random.normal(rng, extent, jnp.float32) * scale * level
    return jnp.minimum(jnp.maximum(drawn, -most), most).astype(kind)


def setup_inputs(seed: int = 0, part: int = 0) -> dict:
    streams_of = jax.random.split(jax.random.key(seed), 10)
    own_keys = jax.random.split(jax.random.fold_in(streams_of[9], part), 10)
    return {
        "tokens": noise(own_keys[0], (TOKEN_TOTAL, D), 1.0, 6.0, ((0, 4), (1, 4))),
        "out_grad": noise(own_keys[1], (TOKEN_TOTAL, D), 1.0, 6.0, ((0, 4), (1, 4))),
        "gate_weights": jnp.clip(0.1 + 0.4 * jax.random.uniform(own_keys[2], (TOKEN_TOTAL, TOP), jnp.float32) ** levels(own_keys[2], (TOKEN_TOTAL, TOP), ((0, 4),), -0.2, 0.2), 0.1, 0.5),
        "expert_ids": draw_expert_ids(jax.random.fold_in(jax.random.fold_in(streams_of[9], part), 71), part),
        "replica_plan": draw_replica_plan(jax.random.fold_in(jax.random.fold_in(streams_of[9], part), 71), part),
        "cap_blocks": draw_cap_blocks(jax.random.fold_in(jax.random.fold_in(streams_of[9], part), 71), part),
        "gate_weight": noise(streams_of[6], (EXPERTS, D, FF), D ** -0.5, 0.125, ((0, 4), (1, 4))),
        "up_weight": noise(streams_of[7], (EXPERTS, D, FF), D ** -0.5, 0.125, ((0, 4), (1, 4))),
        "down_weight": noise(streams_of[8], (EXPERTS, FF, D), FF ** -0.5, 0.21875, ((0, 4), (2, 4))),
    }


def routing(expert_ids, replica_plan, cap_blocks, token_index):
    host_count = replica_plan.shape[1]
    experts = cap_blocks.shape[0]
    host_slot = (token_index % host_count).astype(jnp.int32)
    is_first = expert_ids == replica_plan[0, 0]
    is_second = expert_ids == replica_plan[1, 0]
    first_host = replica_plan[0][host_slot][:, None]
    second_host = replica_plan[1][host_slot][:, None]
    target = jnp.where(is_first, first_host, jnp.where(is_second, second_host, expert_ids)).astype(jnp.int32)
    spare_kind = ((is_first | is_second) & (host_slot[:, None] > 0)).astype(jnp.int32)
    bucket = (target * 2 + spare_kind).reshape(-1)
    onehot = (bucket[:, None] == jnp.arange(2 * experts, dtype=jnp.int32)[None, :]).astype(jnp.int32)
    before = jnp.cumsum(onehot, axis=0) - onehot
    position = jnp.sum(before * onehot, axis=1).reshape(target.shape).astype(jnp.int32)
    capacity = jnp.where(spare_kind == 1, SPARE, cap_blocks[target] * BLK)
    accepted = position < capacity
    return target, spare_kind, position, accepted


def silu_parts(preact):
    sigma = jax.nn.sigmoid(preact)
    return preact * sigma, sigma * (1.0 + preact * (1.0 - sigma))


def block_sum(partials):
    return jnp.sum(lax.optimization_barrier(partials.astype(jnp.bfloat16)).astype(jnp.float32), axis=0)


def expert_pass(rows, cotangent, gate_mat, up_mat, down_mat):
    count = rows.shape[0]
    piece = D // N_DP
    rows_blocks = rows.reshape(count, N_DP, piece).astype(jnp.float32)
    gate_pre = block_sum(jnp.einsum("rqp,qpf->qrf", rows_blocks, gate_mat.reshape(N_DP, piece, FF).astype(jnp.float32)))
    up_pre = block_sum(jnp.einsum("rqp,qpf->qrf", rows_blocks, up_mat.reshape(N_DP, piece, FF).astype(jnp.float32)))
    active, slope = silu_parts(gate_pre)
    hidden = (active * up_pre).astype(jnp.bfloat16)
    pair_out = jnp.dot(hidden, down_mat, preferred_element_type=jnp.float32).astype(jnp.bfloat16)
    cot_blocks = cotangent.reshape(count, N_DP, piece).astype(jnp.float32)
    hidden_grad = block_sum(jnp.einsum("rqp,fqp->qrf", cot_blocks, down_mat.reshape(FF, N_DP, piece).astype(jnp.float32)))
    gate_pre_grad = (hidden_grad * up_pre * slope).astype(jnp.bfloat16)
    up_pre_grad = (hidden_grad * active).astype(jnp.bfloat16)
    pair_in = jnp.dot(gate_pre_grad, gate_mat.T, preferred_element_type=jnp.float32)
    pair_in = (pair_in + jnp.dot(up_pre_grad, up_mat.T, preferred_element_type=jnp.float32)).astype(jnp.bfloat16)
    gate_part = jnp.dot(rows.T, gate_pre_grad, preferred_element_type=jnp.float32)
    up_part = jnp.dot(rows.T, up_pre_grad, preferred_element_type=jnp.float32)
    down_part = jnp.dot(hidden.T, cotangent, preferred_element_type=jnp.float32)
    return pair_out, pair_in, gate_part, up_part, down_part


def rounded(value):
    return lax.optimization_barrier(value.astype(jnp.bfloat16)).astype(jnp.float32)


def reference(tokens, out_grad, gate_weights, expert_ids, replica_plan, cap_blocks, gate_weight, up_weight, down_weight):
    token_index = jnp.arange(TOKEN_TOTAL, dtype=jnp.int32).reshape(EXPERTS, TOK_DEV)
    target, spare_kind, position, accepted = jax.vmap(routing, in_axes=(0, None, None, 0))(
        expert_ids.reshape(EXPERTS, TOK_DEV, TOP), replica_plan, cap_blocks, token_index)
    pair_ids = jnp.arange(TOKEN_TOTAL * TOP, dtype=jnp.int32).reshape(EXPERTS, TOK_DEV, TOP)
    source = jnp.broadcast_to(jnp.arange(EXPERTS, dtype=jnp.int32)[:, None, None], pair_ids.shape)
    sentinel = TOKEN_TOTAL * TOP
    own_dest = jnp.where(accepted & (spare_kind == 0), target, EXPERTS).astype(jnp.int32)
    spare_dest = jnp.where(accepted & (spare_kind == 1), target, EXPERTS).astype(jnp.int32)
    own_table = jnp.full((EXPERTS, EXPERTS, CAPM), sentinel, jnp.int32).at[own_dest, source, position].set(pair_ids, mode="drop")
    spare_table = jnp.full((EXPERTS, EXPERTS, SPARE), sentinel, jnp.int32).at[spare_dest, source, position].set(pair_ids, mode="drop")
    padded_tokens = jnp.concatenate([tokens, jnp.zeros((1, D), jnp.bfloat16)], axis=0)
    padded_grads = jnp.concatenate([out_grad, jnp.zeros((1, D), jnp.bfloat16)], axis=0)
    padded_gates = jnp.concatenate([gate_weights.reshape(-1), jnp.zeros((1,), jnp.float32)], axis=0)
    in_first = jnp.any(replica_plan[0][None, :] == jnp.arange(EXPERTS, dtype=jnp.int32)[:, None], axis=1)
    hot_of = jnp.where(in_first, replica_plan[0, 0], replica_plan[1, 0]).astype(jnp.int32)

    def gather_pairs(table):
        token_rows = (table // TOP).astype(jnp.int32)
        rows = padded_tokens[token_rows]
        cotangent = (padded_gates[table][:, None] * padded_grads[token_rows].astype(jnp.float32)).astype(jnp.bfloat16)
        return token_rows, rows, cotangent

    def device_step(carry, device):
        mixed_sum, grad_sum, hot_gate, hot_up, hot_down = carry
        own_ids = own_table[device].reshape(-1)
        spare_ids = spare_table[device].reshape(-1)
        own_tok, own_rows, own_cot = gather_pairs(own_ids)
        spare_tok, spare_rows, spare_cot = gather_pairs(spare_ids)
        own_res = expert_pass(own_rows, own_cot, gate_weight[device], up_weight[device], down_weight[device])
        spare_expert = hot_of[device]
        spare_res = expert_pass(spare_rows, spare_cot, gate_weight[spare_expert], up_weight[spare_expert], down_weight[spare_expert])
        mixed_sum = mixed_sum.at[own_tok].add(padded_gates[own_ids][:, None] * own_res[0].astype(jnp.float32))
        mixed_sum = mixed_sum.at[spare_tok].add(padded_gates[spare_ids][:, None] * spare_res[0].astype(jnp.float32))
        grad_sum = grad_sum.at[own_tok].add(own_res[1].astype(jnp.float32))
        grad_sum = grad_sum.at[spare_tok].add(spare_res[1].astype(jnp.float32))
        place = jnp.where(in_first[device], 0, 1).astype(jnp.int32)
        hot_gate = hot_gate.at[place].add(rounded(spare_res[2]))
        hot_up = hot_up.at[place].add(rounded(spare_res[3]))
        hot_down = hot_down.at[place].add(rounded(spare_res[4]))
        return (mixed_sum, grad_sum, hot_gate, hot_up, hot_down), (own_res[2], own_res[3], own_res[4])

    start = (jnp.zeros((TOKEN_TOTAL + 1, D), jnp.float32), jnp.zeros((TOKEN_TOTAL + 1, D), jnp.float32),
             jnp.zeros((2, D, FF), jnp.float32), jnp.zeros((2, D, FF), jnp.float32), jnp.zeros((2, FF, D), jnp.float32))
    carry, own_grads = lax.scan(device_step, start, jnp.arange(EXPERTS, dtype=jnp.int32))
    mixed_sum, grad_sum, hot_gate, hot_up, hot_down = carry
    is_hot_one = (jnp.arange(EXPERTS, dtype=jnp.int32) == replica_plan[0, 0])[:, None, None]
    is_hot_two = (jnp.arange(EXPERTS, dtype=jnp.int32) == replica_plan[1, 0])[:, None, None]

    def finish(own_part, hot_part):
        total = own_part + jnp.where(is_hot_one, hot_part[0][None], 0.0) + jnp.where(is_hot_two, hot_part[1][None], 0.0)
        return total.astype(jnp.bfloat16)

    mixed = mixed_sum[:TOKEN_TOTAL].astype(jnp.bfloat16)
    token_grad = grad_sum[:TOKEN_TOTAL].astype(jnp.bfloat16)
    return mixed, token_grad, finish(own_grads[0], hot_gate), finish(own_grads[1], hot_up), finish(own_grads[2], hot_down)
```

```python
import functools

import jax
import jax.numpy as jnp
from jax import lax
from jax.experimental import pallas as pl
from jax.experimental.pallas import tpu as pltpu
from jax.sharding import PartitionSpec as P

BLK = 4
MAXB = 2
SPARE = 2
OWN = BLK * MAXB
GROUP = 4
TILE = 256
VMEM_LIMIT = 32 * 1024 * 1024

BF16 = jnp.bfloat16
F32 = jnp.float32
I32 = jnp.int32


def matmul(left, right, left_dim, right_dim):
    return lax.dot_general(
        left, right, (((left_dim,), (right_dim,)), ((), ())), preferred_element_type=F32
    )


def params():
    return pltpu.CompilerParams(vmem_limit_bytes=VMEM_LIMIT)


def dispatch_kernel(
    experts, hosts, slots, block, plan_ref, caps_ref, ids_ref, gates_ref, tok_ref, grad_ref, send_ref, pick_ref
):
    choose, count = ids_ref.shape
    row = lax.broadcasted_iota(I32, (block, count), 0)
    col = lax.broadcasted_iota(I32, (block, count), 1)
    is_cot = row >= slots
    slot = jnp.where(is_cot, row - slots, row)
    valid = row < 2 * slots
    is_spare = slot >= OWN
    spare_slot = jnp.maximum(slot - OWN, 0)
    replica = jnp.where(is_spare, 1 + lax.div(spare_slot, SPARE), 0)
    position = jnp.where(is_spare, lax.rem(spare_slot, SPARE), slot)
    token_slot = lax.rem(col, hosts)
    members, weights, limits = [], [], []
    for expert in range(experts):
        hot = (plan_ref[0, 0] == expert) | (plan_ref[1, 0] == expert)
        wanted = token_slot * hot.astype(I32)
        here = jnp.zeros((1, count), F32)
        weight = jnp.zeros((1, count), F32)
        for k in range(choose):
            chosen = ids_ref[k : k + 1, :] == expert
            here = jnp.where(chosen, 1.0, here)
            weight = jnp.where(chosen, gates_ref[k : k + 1, :], weight)
        fits = valid & (replica == wanted)
        members.append(jnp.where(fits, jnp.broadcast_to(here, fits.shape), 0.0))
        weights.append(jnp.broadcast_to(weight, fits.shape))
        room = jnp.where(is_spare, SPARE, caps_ref[expert] * BLK)
        limits.append(jnp.where(position < room, position, -1))
    member = jnp.concatenate(members, axis=0)
    weight = jnp.concatenate(weights, axis=0)
    limit = jnp.concatenate(limits, axis=0).astype(F32)
    cots = jnp.concatenate([is_cot.astype(F32)] * experts, axis=0)
    earlier = (
        lax.broadcasted_iota(I32, (count, count), 0) < lax.broadcasted_iota(I32, (count, count), 1)
    )
    before = matmul(member.astype(BF16), earlier.astype(F32).astype(BF16), 1, 0)
    taken = jnp.where(before == limit, member, 0.0)
    pick_cot = taken * cots
    pick_tok = taken - pick_cot
    gate = jnp.sum(taken * weight, axis=1, keepdims=True)
    pick_cot = pick_cot.astype(BF16)
    rows = matmul(pick_tok.astype(BF16), tok_ref[...], 1, 0)
    cotangents = gate * matmul(pick_cot, grad_ref[...], 1, 0)
    send_ref[...] = (rows + cotangents).astype(BF16)
    scaled = pick_tok * weight
    high = scaled.astype(BF16)
    pick_ref[0] = high
    pick_ref[1] = (scaled - high.astype(F32)).astype(BF16)
    pick_ref[2] = pick_cot


def dispatch(plan, caps, ids, gates, tokens, grads, experts, slots, block):
    count, feature = tokens.shape
    smem = pl.BlockSpec(memory_space=pltpu.SMEM)
    vmem = pl.BlockSpec(memory_space=pltpu.VMEM)
    return pl.pallas_call(
        functools.partial(dispatch_kernel, experts, plan.shape[1], slots, block),
        out_shape=(
            jax.ShapeDtypeStruct((experts * block, feature), BF16),
            jax.ShapeDtypeStruct((3, experts * block, count), BF16),
        ),
        in_specs=[smem, smem, vmem, vmem, vmem, vmem],
        out_specs=(vmem, vmem),
        compiler_params=params(),
        name="dispatch",
    )(plan, caps, ids, gates, tokens, grads)


def partial_kernel(
    group, slots, block, recv_ref, gate_ref, up_ref, down_ref, rows_ref, cots_ref, part_ref, wide, flat
):
    wide[...] = recv_ref[...].astype(F32)
    for s in range(group):
        flat[0, s * slots : (s + 1) * slots, :] = wide[s * block : s * block + slots, :]
        flat[1, s * slots : (s + 1) * slots, :] = wide[s * block + slots : s * block + 2 * slots, :]
    rows = flat[0].astype(BF16)
    cots = flat[1].astype(BF16)
    rows_ref[...] = rows
    cots_ref[...] = cots
    hidden = gate_ref.shape[1]
    part_ref[:, :hidden] = matmul(rows, gate_ref[...], 1, 0).astype(BF16)
    part_ref[:, hidden : 2 * hidden] = matmul(rows, up_ref[...], 1, 0).astype(BF16)
    part_ref[:, 2 * hidden :] = matmul(cots, down_ref[...], 1, 1).astype(BF16)


def partials(recv, gate, up, down, experts, slots, block):
    feature, hidden = gate.shape
    tile, big = GROUP * slots, GROUP * block
    total = experts * slots

    def whole(shape):
        return pl.BlockSpec(shape, lambda i: (0, 0))

    def by_rows(rows, width):
        return pl.BlockSpec((rows, width), lambda i: (i, 0))

    return pl.pallas_call(
        functools.partial(partial_kernel, GROUP, slots, block),
        grid=(experts // GROUP,),
        out_shape=(
            jax.ShapeDtypeStruct((total, feature), BF16),
            jax.ShapeDtypeStruct((total, feature), BF16),
            jax.ShapeDtypeStruct((total, 3 * hidden), BF16),
        ),
        in_specs=[
            by_rows(big, feature),
            whole((feature, hidden)),
            whole((feature, hidden)),
            whole((hidden, feature)),
        ],
        out_specs=(by_rows(tile, feature), by_rows(tile, feature), by_rows(tile, 3 * hidden)),
        scratch_shapes=[pltpu.VMEM((big, feature), F32), pltpu.VMEM((2, tile, feature), F32)],
        compiler_params=params(),
        name="partials",
    )(recv, gate, up, down)


def middle_kernel(
    group, slots, block, parts_ref, gate_ref, up_ref, down_ref, back_ref, hidden_ref, gg_ref, ug_ref, flat, wide
):
    width = gate_ref.shape[1]
    total = parts_ref[0].astype(F32)
    for j in range(1, parts_ref.shape[0]):
        total = total + parts_ref[j].astype(F32)
    gate_pre, up_pre, hidden_grad = (total[:, i * width : (i + 1) * width] for i in range(3))
    sigma = jax.nn.sigmoid(gate_pre)
    active = gate_pre * sigma
    slope = sigma * (1.0 + gate_pre * (1.0 - sigma))
    hidden = (active * up_pre).astype(BF16)
    gg = (hidden_grad * up_pre * slope).astype(BF16)
    ug = (hidden_grad * active).astype(BF16)
    hidden_ref[...] = hidden
    gg_ref[...] = gg
    ug_ref[...] = ug
    flat[0] = matmul(hidden, down_ref[...], 1, 0)
    flat[1] = matmul(gg, gate_ref[...], 1, 1) + matmul(ug, up_ref[...], 1, 1)
    wide[...] = jnp.zeros_like(wide)
    for s in range(group):
        wide[s * block : s * block + slots, :] = flat[0, s * slots : (s + 1) * slots, :]
        wide[s * block + slots : s * block + 2 * slots, :] = flat[1, s * slots : (s + 1) * slots, :]
    back_ref[...] = wide[...].astype(BF16)


def middle(parts, gate, up, down, experts, slots, block):
    feature, hidden = gate.shape
    tile, big = GROUP * slots, GROUP * block
    total = experts * slots

    def whole(shape):
        return pl.BlockSpec(shape, lambda i: (0, 0))

    def by_rows(rows, width):
        return pl.BlockSpec((rows, width), lambda i: (i, 0))

    return pl.pallas_call(
        functools.partial(middle_kernel, GROUP, slots, block),
        grid=(experts // GROUP,),
        out_shape=(
            jax.ShapeDtypeStruct((experts * block, feature), BF16),
            jax.ShapeDtypeStruct((total, hidden), BF16),
            jax.ShapeDtypeStruct((total, hidden), BF16),
            jax.ShapeDtypeStruct((total, hidden), BF16),
        ),
        in_specs=[
            pl.BlockSpec((parts.shape[0], tile, 3 * hidden), lambda i: (0, i, 0)),
            whole((feature, hidden)),
            whole((feature, hidden)),
            whole((hidden, feature)),
        ],
        out_specs=(
            by_rows(big, feature),
            by_rows(tile, hidden),
            by_rows(tile, hidden),
            by_rows(tile, hidden),
        ),
        scratch_shapes=[pltpu.VMEM((2, tile, feature), F32), pltpu.VMEM((big, feature), F32)],
        compiler_params=params(),
        name="middle",
    )(parts, gate, up, down)


def grads_kernel(rows_ref, cots_ref, hidden_ref, gg_ref, ug_ref, gate_ref, up_ref, down_ref):
    gate_ref[...] = matmul(rows_ref[...], gg_ref[...], 0, 0).astype(BF16)
    up_ref[...] = matmul(rows_ref[...], ug_ref[...], 0, 0).astype(BF16)
    down_ref[...] = matmul(hidden_ref[...], cots_ref[...], 0, 0).astype(BF16)


def weight_grads(rows, cots, hidden, gg, ug):
    total, feature = rows.shape
    width = hidden.shape[1]
    tile = TILE if width % TILE == 0 else width

    def whole(shape):
        return pl.BlockSpec(shape, lambda i: (0, 0))

    def by_columns(count):
        return pl.BlockSpec((count, tile), lambda i: (0, i))

    return pl.pallas_call(
        grads_kernel,
        grid=(width // tile,),
        out_shape=(
            jax.ShapeDtypeStruct((feature, width), BF16),
            jax.ShapeDtypeStruct((feature, width), BF16),
            jax.ShapeDtypeStruct((width, feature), BF16),
        ),
        in_specs=[
            whole((total, feature)),
            whole((total, feature)),
            by_columns(total),
            by_columns(total),
            by_columns(total),
        ],
        out_specs=(
            by_columns(feature),
            by_columns(feature),
            pl.BlockSpec((tile, feature), lambda i: (i, 0)),
        ),
        compiler_params=params(),
        cost_estimate=pl.CostEstimate(
            flops=6 * total * feature * width,
            bytes_accessed=6 * feature * width,
            transcendentals=0,
        ),
        name="weight_grads",
    )(rows, cots, hidden, gg, ug)


def combine_kernel(back_ref, pick_ref, mixed_ref, token_ref):
    back = back_ref[...]
    mixed = matmul(pick_ref[0], back, 0, 0) + matmul(pick_ref[1], back, 0, 0)
    mixed_ref[...] = mixed.astype(BF16)
    token_ref[...] = matmul(pick_ref[2], back, 0, 0).astype(BF16)


def combine(back, pick):
    feature, count = back.shape[1], pick.shape[2]
    vmem = pl.BlockSpec(memory_space=pltpu.VMEM)
    shape = jax.ShapeDtypeStruct((count, feature), BF16)
    return pl.pallas_call(
        combine_kernel,
        out_shape=(shape, shape),
        in_specs=[vmem, vmem],
        out_specs=(vmem, vmem),
        compiler_params=params(),
        name="combine",
    )(back, pick)


def over_experts(array, experts):
    blocks = array.reshape(experts, -1, array.shape[1])
    return lax.all_to_all(blocks, "expert", split_axis=0, concat_axis=0, tiled=True).reshape(array.shape)


def shards(
    tokens,
    out_grad,
    gate_weights,
    expert_ids,
    replica_plan,
    cap_blocks,
    gate_weight,
    up_weight,
    down_weight,
):
    experts = lax.axis_size("expert")
    hosts = replica_plan.shape[1]
    assert tokens.shape[0] % hosts == 0 and experts % GROUP == 0
    slots = OWN + SPARE * (hosts - 1)
    block = -(-2 * slots // 8) * 8
    gate, up, down = gate_weight[0], up_weight[0], down_weight[0]
    send, pick = dispatch(
        replica_plan, cap_blocks, expert_ids.T, gate_weights.T, tokens, out_grad, experts, slots, block
    )
    recv = over_experts(send, experts)
    rows, cots, part = partials(recv, gate, up, down, experts, slots, block)
    parts = lax.all_gather(part, "dp")
    back, hidden, gg, ug = middle(parts, gate, up, down, experts, slots, block)
    returned = over_experts(back, experts)
    gate_grad, up_grad, down_grad = weight_grads(rows, cots, hidden, gg, ug)
    mixed, token_grad = combine(returned, pick)
    return mixed, token_grad, gate_grad[None], up_grad[None], down_grad[None]


def solution(mesh):
    return jax.shard_map(
        shards,
        mesh=mesh,
        in_specs=(
            P(("groups", "expert"), "dp"),
            P(("groups", "expert"), "dp"),
            P(("groups", "expert"), None),
            P(("groups", "expert"), None),
            P("groups", None),
            P("groups"),
            P("expert", "dp", None),
            P("expert", "dp", None),
            P("expert", None, "dp"),
        ),
        out_specs=(
            P(("groups", "expert"), "dp"),
            P(("groups", "expert"), "dp"),
            P(("groups", "expert"), "dp", None),
            P(("groups", "expert"), "dp", None),
            P(("groups", "expert"), None, "dp"),
        ),
        check_vma=False,
    )
```

```python
import functools

import jax
import jax.numpy as jnp
from jax import lax
from jax.experimental import pallas as pl
from jax.experimental.pallas import tpu as pltpu
from jax.sharding import PartitionSpec as P

BLK = 4
MAXB = 2
SPARE = 2
OWN = BLK * MAXB
GROUP = 4
TILE = 256
VMEM_LIMIT = 32 * 1024 * 1024

BF16 = jnp.bfloat16
F32 = jnp.float32
I32 = jnp.int32


def matmul(left, right, left_dim, right_dim):
    return lax.dot_general(
        left, right, (((left_dim,), (right_dim,)), ((), ())), preferred_element_type=F32
    )


def params():
    return pltpu.CompilerParams(vmem_limit_bytes=VMEM_LIMIT)


def dispatch_kernel(experts, hosts, slots, block, pieces, *refs):
    plan_hbm, caps_hbm, ids_hbm, gates_hbm, tok_hbm, grad_hbm = refs[:6]
    send_refs, pick_ref = refs[6 : 6 + pieces], refs[6 + pieces]
    plan_ref, caps_ref, ids_ref, gates_ref, tok_ref, grad_ref, sems = refs[7 + pieces :]
    copies = [
        pltpu.make_async_copy(source, target, sems.at[i])
        for i, (source, target) in enumerate(
            (
                (ids_hbm, ids_ref),
                (plan_hbm, plan_ref),
                (caps_hbm, caps_ref),
                (gates_hbm, gates_ref),
                (tok_hbm, tok_ref),
                (grad_hbm, grad_ref),
            )
        )
    ]
    for copy in copies:
        copy.start()
    me = lax.axis_index("expert")
    choose, count = ids_ref.shape
    row = lax.broadcasted_iota(I32, (block, count), 0)
    col = lax.broadcasted_iota(I32, (block, count), 1)
    is_cot = row >= slots
    slot = jnp.where(is_cot, row - slots, row)
    valid = row < 2 * slots
    is_spare = slot >= OWN
    spare_slot = jnp.maximum(slot - OWN, 0)
    replica = jnp.where(is_spare, 1 + lax.div(spare_slot, SPARE), 0)
    position = jnp.where(is_spare, lax.rem(spare_slot, SPARE), slot)
    token_slot = lax.rem(col, hosts)
    earlier = (
        lax.broadcasted_iota(I32, (count, count), 0) < lax.broadcasted_iota(I32, (count, count), 1)
    )
    earlier = earlier.astype(F32).astype(BF16)
    cots = jnp.concatenate([is_cot.astype(F32)] * experts, axis=0)
    for copy in copies[:4]:
        copy.wait()
    members, weights, limits = [], [], []
    for index in range(experts):
        expert = index if pieces == 1 else lax.rem(me + index, experts)
        hot = (plan_ref[0, 0] == expert) | (plan_ref[1, 0] == expert)
        wanted = token_slot * hot.astype(I32)
        here = jnp.zeros((1, count), F32)
        weight = jnp.zeros((1, count), F32)
        for k in range(choose):
            chosen = ids_ref[k : k + 1, :] == expert
            here = jnp.where(chosen, 1.0, here)
            weight = jnp.where(chosen, gates_ref[k : k + 1, :], weight)
        fits = valid & (replica == wanted)
        members.append(jnp.where(fits, jnp.broadcast_to(here, fits.shape), 0.0))
        weights.append(jnp.broadcast_to(weight, fits.shape))
        room = jnp.where(is_spare, SPARE, caps_ref[expert] * BLK)
        limits.append(jnp.where(position < room, position, -1))
    member = jnp.concatenate(members, axis=0)
    weight = jnp.concatenate(weights, axis=0)
    limit = jnp.concatenate(limits, axis=0).astype(F32)
    before = matmul(member.astype(BF16), earlier, 1, 0)
    taken = jnp.where(before == limit, member, 0.0)
    pick_cot = taken * cots
    pick_tok = taken - pick_cot
    gate = jnp.sum(taken * weight, axis=1, keepdims=True)
    scaled = pick_tok * weight
    high = scaled.astype(BF16)
    pick_cot = pick_cot.astype(BF16)
    pick_ref[0] = high
    pick_ref[1] = (scaled - high.astype(F32)).astype(BF16)
    pick_ref[2] = pick_cot
    for copy in copies[4:]:
        copy.wait()
    rows = matmul(pick_tok.astype(BF16), tok_ref[...], 1, 0)
    cotangents = gate * matmul(pick_cot, grad_ref[...], 1, 0)
    send = (rows + cotangents).astype(BF16)
    size = send.shape[0] // pieces
    for i, send_ref in enumerate(send_refs):
        send_ref[...] = send[i * size : (i + 1) * size]


def dispatch(plan, caps, ids, gates, tokens, grads, experts, slots, block, pieces):
    count, feature = tokens.shape
    vmem = pl.BlockSpec(memory_space=pltpu.VMEM)
    size = experts * block // pieces
    outs = pl.pallas_call(
        functools.partial(dispatch_kernel, experts, plan.shape[1], slots, block, pieces),
        out_shape=(jax.ShapeDtypeStruct((size, feature), BF16),) * pieces
        + (jax.ShapeDtypeStruct((3, experts * block, count), BF16),),
        in_specs=[pl.BlockSpec(memory_space=pltpu.HBM)] * 6,
        out_specs=(vmem,) * (pieces + 1),
        scratch_shapes=[
            pltpu.SMEM(plan.shape, I32),
            pltpu.SMEM(caps.shape, I32),
            pltpu.VMEM(ids.shape, I32),
            pltpu.VMEM(gates.shape, F32),
            pltpu.VMEM(tokens.shape, BF16),
            pltpu.VMEM(grads.shape, BF16),
            pltpu.SemaphoreType.DMA((6,)),
        ],
        compiler_params=params(),
        name="dispatch",
    )(plan, caps, ids, gates, tokens, grads)
    return outs[:pieces], outs[pieces]


def load_kernel(gate_hbm, up_hbm, down_hbm, pick_ref, gate_ref, up_ref, down_ref, sems):
    copies = [
        pltpu.make_async_copy(source, target, sems.at[i])
        for i, (source, target) in enumerate(
            ((gate_hbm, gate_ref), (up_hbm, up_ref), (down_hbm, down_ref))
        )
    ]
    for copy in copies:
        copy.start()
    for copy in copies:
        copy.wait()


def load_weights(gate, up, down, pick):
    hbm = pl.BlockSpec(memory_space=pltpu.HBM)
    vmem = pl.BlockSpec(memory_space=pltpu.VMEM)
    return pl.pallas_call(
        load_kernel,
        out_shape=tuple(pltpu.VMEM(w.shape, BF16) for w in (gate, up, down)),
        in_specs=[hbm, hbm, hbm, pl.BlockSpec(memory_space=pl.ANY)],
        out_specs=(vmem, vmem, vmem),
        scratch_shapes=[pltpu.SemaphoreType.DMA((3,))],
        compiler_params=params(),
        cost_estimate=pl.CostEstimate(
            flops=0, bytes_accessed=2 * 3 * gate.size * 2, transcendentals=0
        ),
        name="load_weights",
    )(gate, up, down, pick)


def partial_kernel(group, slots, block, pieces, *refs):
    recv_refs = refs[:pieces]
    gate_ref, up_ref, down_ref, rows_ref, cots_ref, part_ref, wide, flat = refs[pieces:]
    size = group * block // pieces
    for i, recv_ref in enumerate(recv_refs):
        wide[i * size : (i + 1) * size, :] = recv_ref[...].astype(F32)
    for s in range(group):
        flat[0, s * slots : (s + 1) * slots, :] = wide[s * block : s * block + slots, :]
        flat[1, s * slots : (s + 1) * slots, :] = wide[s * block + slots : s * block + 2 * slots, :]
    rows = flat[0].astype(BF16)
    cots = flat[1].astype(BF16)
    rows_ref[...] = rows
    cots_ref[...] = cots
    hidden = gate_ref.shape[1]
    part_ref[:, :hidden] = matmul(rows, gate_ref[...], 1, 0).astype(BF16)
    part_ref[:, hidden : 2 * hidden] = matmul(rows, up_ref[...], 1, 0).astype(BF16)
    part_ref[:, 2 * hidden :] = matmul(cots, down_ref[...], 1, 1).astype(BF16)


def partials(recvs, gate, up, down, experts, slots, block):
    pieces = len(recvs)
    feature, hidden = gate.shape
    tile, big = GROUP * slots, GROUP * block
    total = experts * slots

    def whole(shape):
        return pl.BlockSpec(shape, lambda i: (0, 0))

    def by_rows(rows, width):
        return pl.BlockSpec((rows, width), lambda i: (i, 0))

    return pl.pallas_call(
        functools.partial(partial_kernel, GROUP, slots, block, pieces),
        grid=(experts // GROUP,),
        out_shape=(
            jax.ShapeDtypeStruct((total, feature), BF16),
            jax.ShapeDtypeStruct((total, feature), BF16),
            jax.ShapeDtypeStruct((total, 3 * hidden), BF16),
        ),
        in_specs=[by_rows(big // pieces, feature)] * pieces
        + [
            whole((feature, hidden)),
            whole((feature, hidden)),
            whole((hidden, feature)),
        ],
        out_specs=(by_rows(tile, feature), by_rows(tile, feature), by_rows(tile, 3 * hidden)),
        scratch_shapes=[pltpu.VMEM((big, feature), F32), pltpu.VMEM((2, tile, feature), F32)],
        compiler_params=params(),
        name="partials",
    )(*recvs, gate, up, down)


def middle_kernel(group, slots, block, pieces, *refs):
    parts_ref, gate_ref, up_ref, down_ref = refs[:4]
    back_refs = refs[4 : 4 + pieces]
    hidden_ref, gg_ref, ug_ref, flat, wide = refs[4 + pieces :]
    width = gate_ref.shape[1]
    total = parts_ref[0].astype(F32)
    for j in range(1, parts_ref.shape[0]):
        total = total + parts_ref[j].astype(F32)
    gate_pre, up_pre, hidden_grad = (total[:, i * width : (i + 1) * width] for i in range(3))
    sigma = jax.nn.sigmoid(gate_pre)
    active = gate_pre * sigma
    slope = sigma * (1.0 + gate_pre * (1.0 - sigma))
    hidden = (active * up_pre).astype(BF16)
    gg = (hidden_grad * up_pre * slope).astype(BF16)
    ug = (hidden_grad * active).astype(BF16)
    hidden_ref[...] = hidden
    gg_ref[...] = gg
    ug_ref[...] = ug
    flat[0] = matmul(hidden, down_ref[...], 1, 0)
    flat[1] = matmul(gg, gate_ref[...], 1, 1) + matmul(ug, up_ref[...], 1, 1)
    wide[...] = jnp.zeros_like(wide)
    for s in range(group):
        wide[s * block : s * block + slots, :] = flat[0, s * slots : (s + 1) * slots, :]
        wide[s * block + slots : s * block + 2 * slots, :] = flat[1, s * slots : (s + 1) * slots, :]
    size = group * block // pieces
    for i, back_ref in enumerate(back_refs):
        back_ref[...] = wide[i * size : (i + 1) * size, :].astype(BF16)


def middle(parts, gate, up, down, experts, slots, block, pieces):
    feature, hidden = gate.shape
    tile, big = GROUP * slots, GROUP * block
    total = experts * slots

    def whole(shape):
        return pl.BlockSpec(shape, lambda i: (0, 0))

    def by_rows(rows, width):
        return pl.BlockSpec((rows, width), lambda i: (i, 0))

    outs = pl.pallas_call(
        functools.partial(middle_kernel, GROUP, slots, block, pieces),
        grid=(experts // GROUP,),
        out_shape=(jax.ShapeDtypeStruct((experts * block // pieces, feature), BF16),) * pieces
        + (jax.ShapeDtypeStruct((total, hidden), BF16),) * 3,
        in_specs=[
            pl.BlockSpec((parts.shape[0], tile, 3 * hidden), lambda i: (0, i, 0)),
            whole((feature, hidden)),
            whole((feature, hidden)),
            whole((hidden, feature)),
        ],
        out_specs=(by_rows(big // pieces, feature),) * pieces + (by_rows(tile, hidden),) * 3,
        scratch_shapes=[pltpu.VMEM((2, tile, feature), F32), pltpu.VMEM((big, feature), F32)],
        compiler_params=params(),
        name="middle",
    )(parts, gate, up, down)
    return outs[:pieces], *outs[pieces:]


def grads_kernel(rows_ref, cots_ref, hidden_ref, gg_ref, ug_ref, gate_ref, up_ref, down_ref):
    gate_ref[...] = matmul(rows_ref[...], gg_ref[...], 0, 0).astype(BF16)
    up_ref[...] = matmul(rows_ref[...], ug_ref[...], 0, 0).astype(BF16)
    down_ref[...] = matmul(hidden_ref[...], cots_ref[...], 0, 0).astype(BF16)


def weight_grads(rows, cots, hidden, gg, ug):
    total, feature = rows.shape
    width = hidden.shape[1]
    tile = TILE if width % TILE == 0 else width

    def whole(shape):
        return pl.BlockSpec(shape, lambda i: (0, 0))

    def by_columns(count):
        return pl.BlockSpec((count, tile), lambda i: (0, i))

    return pl.pallas_call(
        grads_kernel,
        grid=(width // tile,),
        out_shape=(
            jax.ShapeDtypeStruct((feature, width), BF16),
            jax.ShapeDtypeStruct((feature, width), BF16),
            jax.ShapeDtypeStruct((width, feature), BF16),
        ),
        in_specs=[
            whole((total, feature)),
            whole((total, feature)),
            by_columns(total),
            by_columns(total),
            by_columns(total),
        ],
        out_specs=(
            by_columns(feature),
            by_columns(feature),
            pl.BlockSpec((tile, feature), lambda i: (i, 0)),
        ),
        compiler_params=params(),
        cost_estimate=pl.CostEstimate(
            flops=6 * total * feature * width,
            bytes_accessed=6 * feature * width,
            transcendentals=0,
        ),
        name="weight_grads",
    )(rows, cots, hidden, gg, ug)


def combine_kernel(pieces, *refs):
    back_refs = refs[:pieces]
    pick_ref, mixed_ref, token_ref = refs[pieces:]
    back = jnp.concatenate([back_ref[...] for back_ref in back_refs], axis=0)
    mixed = matmul(pick_ref[0], back, 0, 0) + matmul(pick_ref[1], back, 0, 0)
    mixed_ref[...] = mixed.astype(BF16)
    token_ref[...] = matmul(pick_ref[2], back, 0, 0).astype(BF16)


def combine(backs, pick):
    feature, count = backs[0].shape[1], pick.shape[2]
    vmem = pl.BlockSpec(memory_space=pltpu.VMEM)
    shape = jax.ShapeDtypeStruct((count, feature), BF16)
    return pl.pallas_call(
        functools.partial(combine_kernel, len(backs)),
        out_shape=(shape, shape),
        in_specs=[vmem] * (len(backs) + 1),
        out_specs=(vmem, vmem),
        compiler_params=params(),
        name="combine",
    )(*backs, pick)


def over_experts(arrays, experts, sign):
    if len(arrays) == 1:
        array = arrays[0]
        blocks = array.reshape(experts, -1, array.shape[1])
        moved = lax.all_to_all(blocks, "expert", split_axis=0, concat_axis=0, tiled=True)
        return [moved.reshape(array.shape)]
    return [arrays[0]] + [
        lax.ppermute(
            arrays[shift], "expert", [(i, (i + sign * shift) % experts) for i in range(experts)]
        )
        for shift in range(1, experts)
    ]


def shards(
    tokens,
    out_grad,
    gate_weights,
    expert_ids,
    replica_plan,
    cap_blocks,
    gate_weight,
    up_weight,
    down_weight,
):
    experts = lax.axis_size("expert")
    hosts = replica_plan.shape[1]
    assert tokens.shape[0] % hosts == 0 and experts % GROUP == 0
    slots = OWN + SPARE * (hosts - 1)
    block = -(-2 * slots // 8) * 8
    pieces = experts if experts <= GROUP else 1
    gate, up, down = gate_weight[0], up_weight[0], down_weight[0]
    sends, pick = dispatch(
        replica_plan,
        cap_blocks,
        expert_ids.T,
        gate_weights.T,
        tokens,
        out_grad,
        experts,
        slots,
        block,
        pieces,
    )
    recvs = over_experts(sends, experts, 1)
    gate, up, down = load_weights(gate, up, down, pick)
    rows, cots, part = partials(recvs, gate, up, down, experts, slots, block)
    parts = lax.all_gather(part, "dp")
    backs, hidden, gg, ug = middle(parts, gate, up, down, experts, slots, block, pieces)
    returned = over_experts(backs, experts, -1)
    gate_grad, up_grad, down_grad = weight_grads(rows, cots, hidden, gg, ug)
    mixed, token_grad = combine(returned, pick)
    return mixed, token_grad, gate_grad[None], up_grad[None], down_grad[None]


def solution(mesh):
    return jax.shard_map(
        shards,
        mesh=mesh,
        in_specs=(
            P(("groups", "expert"), "dp"),
            P(("groups", "expert"), "dp"),
            P(("groups", "expert"), None),
            P(("groups", "expert"), None),
            P("groups", None),
            P("groups"),
            P("expert", "dp", None),
            P("expert", "dp", None),
            P("expert", None, "dp"),
        ),
        out_specs=(
            P(("groups", "expert"), "dp"),
            P(("groups", "expert"), "dp"),
            P(("groups", "expert"), "dp", None),
            P(("groups", "expert"), "dp", None),
            P(("groups", "expert"), None, "dp"),
        ),
        check_vma=False,
    )
```

```python
import functools

import jax
import jax.numpy as jnp
from jax import lax
from jax.experimental import pallas as pl
from jax.experimental.pallas import tpu as pltpu
from jax.sharding import PartitionSpec as P

BLK = 4
MAXB = 2
SPARE = 2
OWN = BLK * MAXB
GROUP = 4
CHUNK = 128
LOADS = 4
VMEM_LIMIT = 32 * 1024 * 1024

BF16 = jnp.bfloat16
F32 = jnp.float32
I32 = jnp.int32


def matmul(left, right, left_dim, right_dim):
    return lax.dot_general(
        left, right, (((left_dim,), (right_dim,)), ((), ())), preferred_element_type=F32
    )


def params():
    return pltpu.CompilerParams(vmem_limit_bytes=VMEM_LIMIT)


def in_hbm(array):
    return pltpu.with_memory_space_constraint(array, pltpu.HBM)


def spans(extent, size):
    return [(start, min(size, extent - start)) for start in range(0, extent, size)]


def dispatch_kernel(experts, hosts, slots, block, pieces, *refs):
    plan_hbm, caps_hbm, ids_hbm, gates_hbm, tok_hbm, grad_hbm = refs[:6]
    send_refs, pick_ref = refs[6 : 6 + pieces], refs[6 + pieces]
    plan_ref, caps_ref, ids_ref, gates_ref, tok_ref, grad_ref, sems = refs[7 + pieces :]
    copies = [
        pltpu.make_async_copy(source, target, sems.at[i])
        for i, (source, target) in enumerate(
            (
                (ids_hbm, ids_ref),
                (plan_hbm, plan_ref),
                (caps_hbm, caps_ref),
                (gates_hbm, gates_ref),
                (tok_hbm, tok_ref),
                (grad_hbm, grad_ref),
            )
        )
    ]
    for copy in copies:
        copy.start()
    me = lax.axis_index("expert")
    choose, count = ids_ref.shape
    row = lax.broadcasted_iota(I32, (block, count), 0)
    col = lax.broadcasted_iota(I32, (block, count), 1)
    is_cot = row >= slots
    slot = jnp.where(is_cot, row - slots, row)
    valid = row < 2 * slots
    is_spare = slot >= OWN
    spare_slot = jnp.maximum(slot - OWN, 0)
    replica = jnp.where(is_spare, 1 + lax.div(spare_slot, SPARE), 0)
    position = jnp.where(is_spare, lax.rem(spare_slot, SPARE), slot)
    token_slot = lax.rem(col, hosts)
    earlier = (
        lax.broadcasted_iota(I32, (count, count), 0) < lax.broadcasted_iota(I32, (count, count), 1)
    )
    earlier = earlier.astype(F32).astype(BF16)
    cots = jnp.concatenate([is_cot.astype(F32)] * experts, axis=0)
    for copy in copies[:4]:
        copy.wait()
    members, weights, limits = [], [], []
    for index in range(experts):
        expert = index if pieces == 1 else lax.rem(me + index, experts)
        hot = (plan_ref[0, 0] == expert) | (plan_ref[1, 0] == expert)
        wanted = token_slot * hot.astype(I32)
        here = jnp.zeros((1, count), F32)
        weight = jnp.zeros((1, count), F32)
        for k in range(choose):
            chosen = ids_ref[k : k + 1, :] == expert
            here = jnp.where(chosen, 1.0, here)
            weight = jnp.where(chosen, gates_ref[k : k + 1, :], weight)
        fits = valid & (replica == wanted)
        members.append(jnp.where(fits, jnp.broadcast_to(here, fits.shape), 0.0))
        weights.append(jnp.broadcast_to(weight, fits.shape))
        room = jnp.where(is_spare, SPARE, caps_ref[expert] * BLK)
        limits.append(jnp.where(position < room, position, -1))
    member = jnp.concatenate(members, axis=0)
    weight = jnp.concatenate(weights, axis=0)
    limit = jnp.concatenate(limits, axis=0).astype(F32)
    before = matmul(member.astype(BF16), earlier, 1, 0)
    taken = jnp.where(before == limit, member, 0.0)
    pick_cot = taken * cots
    pick_tok = taken - pick_cot
    gate = jnp.sum(taken * weight, axis=1, keepdims=True)
    scaled = pick_tok * weight
    high = scaled.astype(BF16)
    pick_cot = pick_cot.astype(BF16)
    pick_ref[0] = high
    pick_ref[1] = (scaled - high.astype(F32)).astype(BF16)
    pick_ref[2] = pick_cot
    for copy in copies[4:]:
        copy.wait()
    rows = matmul(pick_tok.astype(BF16), tok_ref[...], 1, 0)
    cotangents = gate * matmul(pick_cot, grad_ref[...], 1, 0)
    send = (rows + cotangents).astype(BF16)
    size = send.shape[0] // pieces
    for i, send_ref in enumerate(send_refs):
        send_ref[...] = send[i * size : (i + 1) * size]


def dispatch(plan, caps, ids, gates, tokens, grads, experts, slots, block, pieces):
    count, feature = tokens.shape
    vmem = pl.BlockSpec(memory_space=pltpu.VMEM)
    size = experts * block // pieces
    outs = pl.pallas_call(
        functools.partial(dispatch_kernel, experts, plan.shape[1], slots, block, pieces),
        out_shape=(jax.ShapeDtypeStruct((size, feature), BF16),) * pieces
        + (jax.ShapeDtypeStruct((3, experts * block, count), BF16),),
        in_specs=[pl.BlockSpec(memory_space=pltpu.HBM)] * 6,
        out_specs=(vmem,) * (pieces + 1),
        scratch_shapes=[
            pltpu.SMEM(plan.shape, I32),
            pltpu.SMEM(caps.shape, I32),
            pltpu.VMEM(ids.shape, I32),
            pltpu.VMEM(gates.shape, F32),
            pltpu.VMEM(tokens.shape, BF16),
            pltpu.VMEM(grads.shape, BF16),
            pltpu.SemaphoreType.DMA((6,)),
        ],
        compiler_params=params(),
        name="dispatch",
    )(*(in_hbm(array) for array in (plan, caps, ids, gates, tokens, grads)))
    return outs[:pieces], outs[pieces]


def load_kernel(gate_hbm, up_hbm, down_hbm, pick_ref, gate_ref, up_ref, down_ref, sems):
    copies = []
    for source, target in ((gate_hbm, gate_ref), (up_hbm, up_ref), (down_hbm, down_ref)):
        for start, size in spans(source.shape[0], source.shape[0] // LOADS):
            rows = pl.ds(start, size)
            copies.append(
                pltpu.make_async_copy(source.at[rows], target.at[rows], sems.at[len(copies)])
            )
    for copy in copies:
        copy.start()
    for copy in copies:
        copy.wait()


def load_weights(gate, up, down, pick):
    hbm = pl.BlockSpec(memory_space=pltpu.HBM)
    vmem = pl.BlockSpec(memory_space=pltpu.VMEM)
    assert all(w.shape[0] % (16 * LOADS) == 0 for w in (gate, up, down))
    return pl.pallas_call(
        load_kernel,
        out_shape=tuple(pltpu.VMEM(w.shape, BF16) for w in (gate, up, down)),
        in_specs=[hbm, hbm, hbm, pl.BlockSpec(memory_space=pl.ANY)],
        out_specs=(vmem, vmem, vmem),
        scratch_shapes=[pltpu.SemaphoreType.DMA((3 * LOADS,))],
        compiler_params=params(),
        cost_estimate=pl.CostEstimate(
            flops=0, bytes_accessed=2 * 3 * gate.size * 2, transcendentals=0
        ),
        name="load_weights",
    )(in_hbm(gate), in_hbm(up), in_hbm(down), pick)


def partial_kernel(group, slots, block, pieces, *refs):
    recv_refs = refs[:pieces]
    gate_ref, up_ref, down_ref, rows_ref, cots_ref, part_ref, wide, flat = refs[pieces:]
    size = group * block // pieces
    for i, recv_ref in enumerate(recv_refs):
        wide[i * size : (i + 1) * size, :] = recv_ref[...].astype(F32)
    for s in range(group):
        flat[0, s * slots : (s + 1) * slots, :] = wide[s * block : s * block + slots, :]
        flat[1, s * slots : (s + 1) * slots, :] = wide[s * block + slots : s * block + 2 * slots, :]
    rows = flat[0].astype(BF16)
    cots = flat[1].astype(BF16)
    rows_ref[...] = rows
    cots_ref[...] = cots
    hidden = gate_ref.shape[1]
    part_ref[:, :hidden] = matmul(rows, gate_ref[...], 1, 0).astype(BF16)
    part_ref[:, hidden : 2 * hidden] = matmul(rows, up_ref[...], 1, 0).astype(BF16)
    part_ref[:, 2 * hidden :] = matmul(cots, down_ref[...], 1, 1).astype(BF16)


def partials(recvs, gate, up, down, experts, slots, block):
    pieces = len(recvs)
    feature, hidden = gate.shape
    tile, big = GROUP * slots, GROUP * block
    total = experts * slots

    def whole(shape):
        return pl.BlockSpec(shape, lambda i: (0, 0))

    def by_rows(rows, width):
        return pl.BlockSpec((rows, width), lambda i: (i, 0))

    return pl.pallas_call(
        functools.partial(partial_kernel, GROUP, slots, block, pieces),
        grid=(experts // GROUP,),
        out_shape=(
            jax.ShapeDtypeStruct((total, feature), BF16),
            jax.ShapeDtypeStruct((total, feature), BF16),
            jax.ShapeDtypeStruct((total, 3 * hidden), BF16),
        ),
        in_specs=[by_rows(big // pieces, feature)] * pieces
        + [
            whole((feature, hidden)),
            whole((feature, hidden)),
            whole((hidden, feature)),
        ],
        out_specs=(by_rows(tile, feature), by_rows(tile, feature), by_rows(tile, 3 * hidden)),
        scratch_shapes=[pltpu.VMEM((big, feature), F32), pltpu.VMEM((2, tile, feature), F32)],
        compiler_params=params(),
        name="partials",
    )(*recvs, gate, up, down)


def middle_kernel(group, slots, block, pieces, *refs):
    parts_ref, gate_ref, up_ref, down_ref = refs[:4]
    back_refs = refs[4 : 4 + pieces]
    hidden_ref, gg_ref, ug_ref, flat, wide = refs[4 + pieces :]
    width = gate_ref.shape[1]
    total = parts_ref[0].astype(F32)
    for j in range(1, parts_ref.shape[0]):
        total = total + parts_ref[j].astype(F32)
    gate_pre, up_pre, hidden_grad = (total[:, i * width : (i + 1) * width] for i in range(3))
    sigma = jax.nn.sigmoid(gate_pre)
    active = gate_pre * sigma
    slope = sigma * (1.0 + gate_pre * (1.0 - sigma))
    hidden = (active * up_pre).astype(BF16)
    gg = (hidden_grad * up_pre * slope).astype(BF16)
    ug = (hidden_grad * active).astype(BF16)
    hidden_ref[...] = hidden
    gg_ref[...] = gg
    ug_ref[...] = ug
    flat[0] = matmul(hidden, down_ref[...], 1, 0)
    flat[1] = matmul(gg, gate_ref[...], 1, 1) + matmul(ug, up_ref[...], 1, 1)
    wide[...] = jnp.zeros_like(wide)
    for s in range(group):
        wide[s * block : s * block + slots, :] = flat[0, s * slots : (s + 1) * slots, :]
        wide[s * block + slots : s * block + 2 * slots, :] = flat[1, s * slots : (s + 1) * slots, :]
    size = group * block // pieces
    for i, back_ref in enumerate(back_refs):
        back_ref[...] = wide[i * size : (i + 1) * size, :].astype(BF16)


def middle(parts, gate, up, down, experts, slots, block, pieces):
    feature, hidden = gate.shape
    tile, big = GROUP * slots, GROUP * block
    total = experts * slots

    def whole(shape):
        return pl.BlockSpec(shape, lambda i: (0, 0))

    def by_rows(rows, width):
        return pl.BlockSpec((rows, width), lambda i: (i, 0))

    outs = pl.pallas_call(
        functools.partial(middle_kernel, GROUP, slots, block, pieces),
        grid=(experts // GROUP,),
        out_shape=(jax.ShapeDtypeStruct((experts * block // pieces, feature), BF16),) * pieces
        + (jax.ShapeDtypeStruct((total, hidden), BF16),) * 3,
        in_specs=[
            pl.BlockSpec((parts.shape[0], tile, 3 * hidden), lambda i: (0, i, 0)),
            whole((feature, hidden)),
            whole((feature, hidden)),
            whole((hidden, feature)),
        ],
        out_specs=(by_rows(big // pieces, feature),) * pieces + (by_rows(tile, hidden),) * 3,
        scratch_shapes=[pltpu.VMEM((2, tile, feature), F32), pltpu.VMEM((big, feature), F32)],
        compiler_params=params(),
        name="middle",
    )(parts, gate, up, down)
    return outs[:pieces], *outs[pieces:]


def grads_kernel(
    rows_ref, cots_ref, hidden_ref, gg_ref, ug_ref, gate_hbm, up_hbm, down_hbm, gate_ref, up_ref, down_ref, sems
):
    copies = []
    for left_ref, right_ref, out_ref, out_hbm in (
        (rows_ref, gg_ref, gate_ref, gate_hbm),
        (rows_ref, ug_ref, up_ref, up_hbm),
        (hidden_ref, cots_ref, down_ref, down_hbm),
    ):
        for start, size in spans(out_ref.shape[0], CHUNK):
            rows = pl.ds(start, size)
            out_ref[rows, :] = matmul(left_ref[:, rows], right_ref[...], 0, 0).astype(BF16)
            copies.append(
                pltpu.make_async_copy(out_ref.at[rows], out_hbm.at[rows], sems.at[len(copies)])
            )
            copies[-1].start()
    for copy in copies:
        copy.wait()


def weight_grads(rows, cots, hidden, gg, ug):
    total, feature = rows.shape
    width = hidden.shape[1]
    vmem = pl.BlockSpec(memory_space=pltpu.VMEM)
    hbm = pl.BlockSpec(memory_space=pltpu.HBM)
    shapes = ((feature, width), (feature, width), (width, feature))
    return pl.pallas_call(
        grads_kernel,
        out_shape=tuple(jax.ShapeDtypeStruct(shape, BF16) for shape in shapes),
        in_specs=[vmem] * 5,
        out_specs=(hbm,) * 3,
        scratch_shapes=[pltpu.VMEM(shape, BF16) for shape in shapes]
        + [pltpu.SemaphoreType.DMA((sum(len(spans(shape[0], CHUNK)) for shape in shapes),))],
        compiler_params=params(),
        cost_estimate=pl.CostEstimate(
            flops=6 * total * feature * width,
            bytes_accessed=6 * feature * width,
            transcendentals=0,
        ),
        name="weight_grads",
    )(rows, cots, hidden, gg, ug)


def combine_kernel(pieces, *refs):
    back_refs = refs[:pieces]
    pick_ref, mixed_hbm, token_hbm, mixed_ref, token_ref, sems = refs[pieces:]
    back = jnp.concatenate([back_ref[...] for back_ref in back_refs], axis=0)
    token_ref[...] = matmul(pick_ref[2], back, 0, 0).astype(BF16)
    token_copy = pltpu.make_async_copy(token_ref, token_hbm, sems.at[0])
    token_copy.start()
    mixed = matmul(pick_ref[0], back, 0, 0) + matmul(pick_ref[1], back, 0, 0)
    mixed_ref[...] = mixed.astype(BF16)
    mixed_copy = pltpu.make_async_copy(mixed_ref, mixed_hbm, sems.at[1])
    mixed_copy.start()
    token_copy.wait()
    mixed_copy.wait()


def combine(backs, pick):
    feature, count = backs[0].shape[1], pick.shape[2]
    vmem = pl.BlockSpec(memory_space=pltpu.VMEM)
    hbm = pl.BlockSpec(memory_space=pltpu.HBM)
    shape = (count, feature)
    return pl.pallas_call(
        functools.partial(combine_kernel, len(backs)),
        out_shape=(jax.ShapeDtypeStruct(shape, BF16),) * 2,
        in_specs=[vmem] * (len(backs) + 1),
        out_specs=(hbm, hbm),
        scratch_shapes=[
            pltpu.VMEM(shape, BF16),
            pltpu.VMEM(shape, BF16),
            pltpu.SemaphoreType.DMA((2,)),
        ],
        compiler_params=params(),
        name="combine",
    )(*backs, pick)


def over_experts(arrays, experts, sign):
    if len(arrays) == 1:
        array = arrays[0]
        blocks = array.reshape(experts, -1, array.shape[1])
        moved = lax.all_to_all(blocks, "expert", split_axis=0, concat_axis=0, tiled=True)
        return [moved.reshape(array.shape)]
    return [arrays[0]] + [
        lax.ppermute(
            arrays[shift], "expert", [(i, (i + sign * shift) % experts) for i in range(experts)]
        )
        for shift in range(1, experts)
    ]


def shards(
    tokens,
    out_grad,
    gate_weights,
    expert_ids,
    replica_plan,
    cap_blocks,
    gate_weight,
    up_weight,
    down_weight,
):
    experts = lax.axis_size("expert")
    hosts = replica_plan.shape[1]
    assert tokens.shape[0] % hosts == 0 and experts % GROUP == 0
    slots = OWN + SPARE * (hosts - 1)
    block = -(-2 * slots // 8) * 8
    pieces = experts if experts <= GROUP else 1
    gate, up, down = gate_weight[0], up_weight[0], down_weight[0]
    sends, pick = dispatch(
        replica_plan,
        cap_blocks,
        expert_ids.T,
        gate_weights.T,
        tokens,
        out_grad,
        experts,
        slots,
        block,
        pieces,
    )
    recvs = over_experts(sends, experts, 1)
    gate, up, down = load_weights(gate, up, down, pick)
    rows, cots, part = partials(recvs, gate, up, down, experts, slots, block)
    parts = lax.all_gather(part, "dp")
    backs, hidden, gg, ug = middle(parts, gate, up, down, experts, slots, block, pieces)
    returned = over_experts(backs, experts, -1)
    gate_grad, up_grad, down_grad = weight_grads(rows, cots, hidden, gg, ug)
    mixed, token_grad = combine(returned, pick)
    return mixed, token_grad, gate_grad[None], up_grad[None], down_grad[None]


def solution(mesh):
    return jax.shard_map(
        shards,
        mesh=mesh,
        in_specs=(
            P(("groups", "expert"), "dp"),
            P(("groups", "expert"), "dp"),
            P(("groups", "expert"), None),
            P(("groups", "expert"), None),
            P("groups", None),
            P("groups"),
            P("expert", "dp", None),
            P("expert", "dp", None),
            P("expert", None, "dp"),
        ),
        out_specs=(
            P(("groups", "expert"), "dp"),
            P(("groups", "expert"), "dp"),
            P(("groups", "expert"), "dp", None),
            P(("groups", "expert"), "dp", None),
            P(("groups", "expert"), None, "dp"),
        ),
        check_vma=False,
    )
```

```python
import functools

import jax
import jax.numpy as jnp
from jax import lax
from jax.experimental import pallas as pl
from jax.experimental.pallas import tpu as pltpu
from jax.sharding import PartitionSpec as P

BLK = 4
MAXB = 2
SPARE = 2
OWN = BLK * MAXB
GROUP = 4
CHUNK = 128
LOADS = 4
VMEM_LIMIT = 32 * 1024 * 1024

BF16 = jnp.bfloat16
F32 = jnp.float32
I32 = jnp.int32


def matmul(left, right, left_dim, right_dim):
    return lax.dot_general(
        left, right, (((left_dim,), (right_dim,)), ((), ())), preferred_element_type=F32
    )


def params():
    return pltpu.CompilerParams(vmem_limit_bytes=VMEM_LIMIT)


def in_hbm(array):
    return pltpu.with_memory_space_constraint(array, pltpu.HBM)


def spans(extent, size):
    return [(start, min(size, extent - start)) for start in range(0, extent, size)]


def dispatch_kernel(experts, hosts, slots, block, pieces, *refs):
    plan_hbm, caps_hbm, ids_hbm, gates_hbm, tok_hbm, grad_hbm = refs[:6]
    send_refs, pick_ref = refs[6 : 6 + pieces], refs[6 + pieces]
    plan_ref, caps_ref, ids_ref, gates_ref, tok_ref, grad_ref, sems = refs[7 + pieces :]
    copies = [
        pltpu.make_async_copy(source, target, sems.at[i])
        for i, (source, target) in enumerate(
            (
                (ids_hbm, ids_ref),
                (plan_hbm, plan_ref),
                (caps_hbm, caps_ref),
                (gates_hbm, gates_ref),
                (tok_hbm, tok_ref),
                (grad_hbm, grad_ref),
            )
        )
    ]
    for copy in copies:
        copy.start()
    me = lax.axis_index("expert")
    choose, count = ids_ref.shape
    row = lax.broadcasted_iota(I32, (block, count), 0)
    col = lax.broadcasted_iota(I32, (block, count), 1)
    is_cot = row >= slots
    slot = jnp.where(is_cot, row - slots, row)
    valid = row < 2 * slots
    is_spare = slot >= OWN
    spare_slot = jnp.maximum(slot - OWN, 0)
    replica = jnp.where(is_spare, 1 + lax.div(spare_slot, SPARE), 0)
    position = jnp.where(is_spare, lax.rem(spare_slot, SPARE), slot)
    token_slot = lax.rem(col, hosts)
    earlier = (
        lax.broadcasted_iota(I32, (count, count), 0) < lax.broadcasted_iota(I32, (count, count), 1)
    )
    earlier = earlier.astype(F32).astype(BF16)
    cots = jnp.concatenate([is_cot.astype(F32)] * experts, axis=0)
    for copy in copies[:4]:
        copy.wait()
    members, weights, limits = [], [], []
    for index in range(experts):
        expert = index if pieces == 1 else me ^ index
        hot = (plan_ref[0, 0] == expert) | (plan_ref[1, 0] == expert)
        wanted = token_slot * hot.astype(I32)
        here = jnp.zeros((1, count), F32)
        weight = jnp.zeros((1, count), F32)
        for k in range(choose):
            chosen = ids_ref[k : k + 1, :] == expert
            here = jnp.where(chosen, 1.0, here)
            weight = jnp.where(chosen, gates_ref[k : k + 1, :], weight)
        fits = valid & (replica == wanted)
        members.append(jnp.where(fits, jnp.broadcast_to(here, fits.shape), 0.0))
        weights.append(jnp.broadcast_to(weight, fits.shape))
        room = jnp.where(is_spare, SPARE, caps_ref[expert] * BLK)
        limits.append(jnp.where(position < room, position, -1))
    member = jnp.concatenate(members, axis=0)
    weight = jnp.concatenate(weights, axis=0)
    limit = jnp.concatenate(limits, axis=0).astype(F32)
    before = matmul(member.astype(BF16), earlier, 1, 0)
    taken = jnp.where(before == limit, member, 0.0)
    pick_cot = taken * cots
    pick_tok = taken - pick_cot
    gate = jnp.sum(taken * weight, axis=1, keepdims=True)
    scaled = pick_tok * weight
    high = scaled.astype(BF16)
    pick_cot = pick_cot.astype(BF16)
    pick_ref[0] = high
    pick_ref[1] = (scaled - high.astype(F32)).astype(BF16)
    pick_ref[2] = pick_cot
    for copy in copies[4:]:
        copy.wait()
    rows = matmul(pick_tok.astype(BF16), tok_ref[...], 1, 0)
    cotangents = gate * matmul(pick_cot, grad_ref[...], 1, 0)
    send = (rows + cotangents).astype(BF16)
    size = send.shape[0] // pieces
    for i, send_ref in enumerate(send_refs):
        send_ref[...] = send[i * size : (i + 1) * size]


def dispatch(plan, caps, ids, gates, tokens, grads, experts, slots, block, pieces):
    count, feature = tokens.shape
    vmem = pl.BlockSpec(memory_space=pltpu.VMEM)
    size = experts * block // pieces
    outs = pl.pallas_call(
        functools.partial(dispatch_kernel, experts, plan.shape[1], slots, block, pieces),
        out_shape=(jax.ShapeDtypeStruct((size, feature), BF16),) * pieces
        + (jax.ShapeDtypeStruct((3, experts * block, count), BF16),),
        in_specs=[pl.BlockSpec(memory_space=pltpu.HBM)] * 6,
        out_specs=(vmem,) * (pieces + 1),
        scratch_shapes=[
            pltpu.SMEM(plan.shape, I32),
            pltpu.SMEM(caps.shape, I32),
            pltpu.VMEM(ids.shape, I32),
            pltpu.VMEM(gates.shape, F32),
            pltpu.VMEM(tokens.shape, BF16),
            pltpu.VMEM(grads.shape, BF16),
            pltpu.SemaphoreType.DMA((6,)),
        ],
        compiler_params=params(),
        name="dispatch",
    )(*(in_hbm(array) for array in (plan, caps, ids, gates, tokens, grads)))
    return outs[:pieces], outs[pieces]


def load_kernel(gate_hbm, up_hbm, down_hbm, pick_ref, gate_ref, up_ref, down_ref, sems):
    copies = []
    for source, target in ((gate_hbm, gate_ref), (up_hbm, up_ref), (down_hbm, down_ref)):
        for start, size in spans(source.shape[0], source.shape[0] // LOADS):
            rows = pl.ds(start, size)
            copies.append(
                pltpu.make_async_copy(source.at[rows], target.at[rows], sems.at[len(copies)])
            )
    for copy in copies:
        copy.start()
    for copy in copies:
        copy.wait()


def load_weights(gate, up, down, pick):
    hbm = pl.BlockSpec(memory_space=pltpu.HBM)
    vmem = pl.BlockSpec(memory_space=pltpu.VMEM)
    assert all(w.shape[0] % (16 * LOADS) == 0 for w in (gate, up, down))
    return pl.pallas_call(
        load_kernel,
        out_shape=tuple(pltpu.VMEM(w.shape, BF16) for w in (gate, up, down)),
        in_specs=[hbm, hbm, hbm, pl.BlockSpec(memory_space=pl.ANY)],
        out_specs=(vmem, vmem, vmem),
        scratch_shapes=[pltpu.SemaphoreType.DMA((3 * LOADS,))],
        compiler_params=params(),
        cost_estimate=pl.CostEstimate(
            flops=0, bytes_accessed=2 * 3 * gate.size * 2, transcendentals=0
        ),
        name="load_weights",
    )(in_hbm(gate), in_hbm(up), in_hbm(down), pick)


def partial_kernel(group, slots, block, pieces, *refs):
    recv_refs = refs[:pieces]
    gate_ref, up_ref, down_ref, rows_ref, cots_ref, part_ref, wide, flat = refs[pieces:]
    size = group * block // pieces
    for i, recv_ref in enumerate(recv_refs):
        wide[i * size : (i + 1) * size, :] = recv_ref[...].astype(F32)
    for s in range(group):
        flat[0, s * slots : (s + 1) * slots, :] = wide[s * block : s * block + slots, :]
        flat[1, s * slots : (s + 1) * slots, :] = wide[s * block + slots : s * block + 2 * slots, :]
    rows = flat[0].astype(BF16)
    cots = flat[1].astype(BF16)
    rows_ref[...] = rows
    cots_ref[...] = cots
    hidden = gate_ref.shape[1]
    part_ref[:, :hidden] = matmul(rows, gate_ref[...], 1, 0).astype(BF16)
    part_ref[:, hidden : 2 * hidden] = matmul(rows, up_ref[...], 1, 0).astype(BF16)
    part_ref[:, 2 * hidden :] = matmul(cots, down_ref[...], 1, 1).astype(BF16)


def partials(recvs, gate, up, down, experts, slots, block):
    pieces = len(recvs)
    feature, hidden = gate.shape
    tile, big = GROUP * slots, GROUP * block
    total = experts * slots

    def whole(shape):
        return pl.BlockSpec(shape, lambda i: (0, 0))

    def by_rows(rows, width):
        return pl.BlockSpec((rows, width), lambda i: (i, 0))

    return pl.pallas_call(
        functools.partial(partial_kernel, GROUP, slots, block, pieces),
        grid=(experts // GROUP,),
        out_shape=(
            jax.ShapeDtypeStruct((total, feature), BF16),
            jax.ShapeDtypeStruct((total, feature), BF16),
            jax.ShapeDtypeStruct((total, 3 * hidden), BF16),
        ),
        in_specs=[by_rows(big // pieces, feature)] * pieces
        + [
            whole((feature, hidden)),
            whole((feature, hidden)),
            whole((hidden, feature)),
        ],
        out_specs=(by_rows(tile, feature), by_rows(tile, feature), by_rows(tile, 3 * hidden)),
        scratch_shapes=[pltpu.VMEM((big, feature), F32), pltpu.VMEM((2, tile, feature), F32)],
        compiler_params=params(),
        name="partials",
    )(*recvs, gate, up, down)


def middle_kernel(group, slots, block, pieces, *refs):
    near_ref, far_ref, gate_ref, up_ref, down_ref = refs[:5]
    back_refs = refs[5 : 5 + pieces]
    hidden_ref, gg_ref, ug_ref, flat, wide = refs[5 + pieces :]
    width = gate_ref.shape[1]
    total = near_ref[...].astype(F32) + far_ref[...].astype(F32)
    gate_pre, up_pre, hidden_grad = (total[:, i * width : (i + 1) * width] for i in range(3))
    sigma = jax.nn.sigmoid(gate_pre)
    active = gate_pre * sigma
    slope = sigma * (1.0 + gate_pre * (1.0 - sigma))
    hidden = (active * up_pre).astype(BF16)
    gg = (hidden_grad * up_pre * slope).astype(BF16)
    ug = (hidden_grad * active).astype(BF16)
    hidden_ref[...] = hidden
    gg_ref[...] = gg
    ug_ref[...] = ug
    flat[0] = matmul(hidden, down_ref[...], 1, 0)
    flat[1] = matmul(gg, gate_ref[...], 1, 1) + matmul(ug, up_ref[...], 1, 1)
    wide[...] = jnp.zeros_like(wide)
    for s in range(group):
        wide[s * block : s * block + slots, :] = flat[0, s * slots : (s + 1) * slots, :]
        wide[s * block + slots : s * block + 2 * slots, :] = flat[1, s * slots : (s + 1) * slots, :]
    size = group * block // pieces
    for i, back_ref in enumerate(back_refs):
        back_ref[...] = wide[i * size : (i + 1) * size, :].astype(BF16)


def middle(parts, gate, up, down, experts, slots, block, pieces):
    feature, hidden = gate.shape
    tile, big = GROUP * slots, GROUP * block
    total = experts * slots

    def whole(shape):
        return pl.BlockSpec(shape, lambda i: (0, 0))

    def by_rows(rows, width):
        return pl.BlockSpec((rows, width), lambda i: (i, 0))

    outs = pl.pallas_call(
        functools.partial(middle_kernel, GROUP, slots, block, pieces),
        grid=(experts // GROUP,),
        out_shape=(jax.ShapeDtypeStruct((experts * block // pieces, feature), BF16),) * pieces
        + (jax.ShapeDtypeStruct((total, hidden), BF16),) * 3,
        in_specs=[
            by_rows(tile, 3 * hidden),
            by_rows(tile, 3 * hidden),
            whole((feature, hidden)),
            whole((feature, hidden)),
            whole((hidden, feature)),
        ],
        out_specs=(by_rows(big // pieces, feature),) * pieces + (by_rows(tile, hidden),) * 3,
        scratch_shapes=[pltpu.VMEM((2, tile, feature), F32), pltpu.VMEM((big, feature), F32)],
        compiler_params=params(),
        name="middle",
    )(*parts, gate, up, down)
    return outs[:pieces], *outs[pieces:]


def grads_kernel(
    rows_ref, cots_ref, hidden_ref, gg_ref, ug_ref, gate_hbm, up_hbm, down_hbm, gate_ref, up_ref, down_ref, sems
):
    copies = []
    for left_ref, right_ref, out_ref, out_hbm in (
        (rows_ref, gg_ref, gate_ref, gate_hbm),
        (rows_ref, ug_ref, up_ref, up_hbm),
        (hidden_ref, cots_ref, down_ref, down_hbm),
    ):
        for start, size in spans(out_ref.shape[0], CHUNK):
            rows = pl.ds(start, size)
            out_ref[rows, :] = matmul(left_ref[:, rows], right_ref[...], 0, 0).astype(BF16)
            copies.append(
                pltpu.make_async_copy(out_ref.at[rows], out_hbm.at[rows], sems.at[len(copies)])
            )
            copies[-1].start()
    for copy in copies:
        copy.wait()


def weight_grads(rows, cots, hidden, gg, ug):
    total, feature = rows.shape
    width = hidden.shape[1]
    vmem = pl.BlockSpec(memory_space=pltpu.VMEM)
    hbm = pl.BlockSpec(memory_space=pltpu.HBM)
    shapes = ((feature, width), (feature, width), (width, feature))
    return pl.pallas_call(
        grads_kernel,
        out_shape=tuple(jax.ShapeDtypeStruct(shape, BF16) for shape in shapes),
        in_specs=[vmem] * 5,
        out_specs=(hbm,) * 3,
        scratch_shapes=[pltpu.VMEM(shape, BF16) for shape in shapes]
        + [pltpu.SemaphoreType.DMA((sum(len(spans(shape[0], CHUNK)) for shape in shapes),))],
        compiler_params=params(),
        cost_estimate=pl.CostEstimate(
            flops=6 * total * feature * width,
            bytes_accessed=6 * feature * width,
            transcendentals=0,
        ),
        name="weight_grads",
    )(rows, cots, hidden, gg, ug)


def combine_kernel(pieces, *refs):
    back_refs = refs[:pieces]
    pick_ref, mixed_hbm, token_hbm, mixed_ref, token_ref, sems = refs[pieces:]
    back = jnp.concatenate([back_ref[...] for back_ref in back_refs], axis=0)
    token_ref[...] = matmul(pick_ref[2], back, 0, 0).astype(BF16)
    token_copy = pltpu.make_async_copy(token_ref, token_hbm, sems.at[0])
    token_copy.start()
    mixed = matmul(pick_ref[0], back, 0, 0) + matmul(pick_ref[1], back, 0, 0)
    mixed_ref[...] = mixed.astype(BF16)
    mixed_copy = pltpu.make_async_copy(mixed_ref, mixed_hbm, sems.at[1])
    mixed_copy.start()
    token_copy.wait()
    mixed_copy.wait()


def combine(backs, pick):
    feature, count = backs[0].shape[1], pick.shape[2]
    vmem = pl.BlockSpec(memory_space=pltpu.VMEM)
    hbm = pl.BlockSpec(memory_space=pltpu.HBM)
    shape = (count, feature)
    return pl.pallas_call(
        functools.partial(combine_kernel, len(backs)),
        out_shape=(jax.ShapeDtypeStruct(shape, BF16),) * 2,
        in_specs=[vmem] * (len(backs) + 1),
        out_specs=(hbm, hbm),
        scratch_shapes=[
            pltpu.VMEM(shape, BF16),
            pltpu.VMEM(shape, BF16),
            pltpu.SemaphoreType.DMA((2,)),
        ],
        compiler_params=params(),
        name="combine",
    )(*backs, pick)


def swapped(array, axis, distance):
    return lax.ppermute(array, axis, [(i, i ^ distance) for i in range(lax.axis_size(axis))])


def over_experts(arrays, experts):
    if len(arrays) == 1:
        array = arrays[0]
        blocks = array.reshape(experts, -1, array.shape[1])
        moved = lax.all_to_all(blocks, "expert", split_axis=0, concat_axis=0, tiled=True)
        return [moved.reshape(array.shape)]
    return [arrays[0]] + [swapped(arrays[d], "expert", d) for d in range(1, experts)]


def add_kernel(left_ref, right_ref, sum_ref):
    sum_ref[...] = (left_ref[...].astype(F32) + right_ref[...].astype(F32)).astype(BF16)


def add(left, right, tile):
    spec = pl.BlockSpec((tile, left.shape[1]), lambda i: (i, 0))
    return pl.pallas_call(
        add_kernel,
        grid=(left.shape[0] // tile,),
        out_shape=jax.ShapeDtypeStruct(left.shape, BF16),
        in_specs=[spec, spec],
        out_specs=spec,
        compiler_params=params(),
        name="add",
    )(left, right)


def halves_over_dp(part, tile):
    last = lax.axis_size("dp") // 2
    distance = 1
    while distance < last:
        part = add(part, swapped(part, "dp", distance), tile)
        distance *= 2
    return part, swapped(part, "dp", last)


def shards(
    tokens,
    out_grad,
    gate_weights,
    expert_ids,
    replica_plan,
    cap_blocks,
    gate_weight,
    up_weight,
    down_weight,
):
    experts = lax.axis_size("expert")
    hosts = replica_plan.shape[1]
    assert tokens.shape[0] % hosts == 0 and experts % GROUP == 0
    assert all(n & (n - 1) == 0 for n in (experts, lax.axis_size("dp")))
    slots = OWN + SPARE * (hosts - 1)
    block = -(-2 * slots // 8) * 8
    pieces = experts if experts <= GROUP else 1
    gate, up, down = gate_weight[0], up_weight[0], down_weight[0]
    sends, pick = dispatch(
        replica_plan,
        cap_blocks,
        expert_ids.T,
        gate_weights.T,
        tokens,
        out_grad,
        experts,
        slots,
        block,
        pieces,
    )
    recvs = over_experts(sends, experts)
    gate, up, down = load_weights(gate, up, down, pick)
    rows, cots, part = partials(recvs, gate, up, down, experts, slots, block)
    parts = halves_over_dp(part, GROUP * slots)
    backs, hidden, gg, ug = middle(parts, gate, up, down, experts, slots, block, pieces)
    returned = over_experts(backs, experts)
    gate_grad, up_grad, down_grad = weight_grads(rows, cots, hidden, gg, ug)
    mixed, token_grad = combine(returned, pick)
    return mixed, token_grad, gate_grad[None], up_grad[None], down_grad[None]


def solution(mesh):
    return jax.shard_map(
        shards,
        mesh=mesh,
        in_specs=(
            P(("groups", "expert"), "dp"),
            P(("groups", "expert"), "dp"),
            P(("groups", "expert"), None),
            P(("groups", "expert"), None),
            P("groups", None),
            P("groups"),
            P("expert", "dp", None),
            P("expert", "dp", None),
            P("expert", None, "dp"),
        ),
        out_specs=(
            P(("groups", "expert"), "dp"),
            P(("groups", "expert"), "dp"),
            P(("groups", "expert"), "dp", None),
            P(("groups", "expert"), "dp", None),
            P(("groups", "expert"), None, "dp"),
        ),
        check_vma=False,
    )
```

```python
import functools

import jax
import jax.numpy as jnp
from jax import lax
from jax.experimental import pallas as pl
from jax.experimental.pallas import tpu as pltpu
from jax.sharding import PartitionSpec as P

BLK = 4
MAXB = 2
SPARE = 2
OWN = BLK * MAXB
GROUP = 4
CHUNK = 128
LOADS = 4
VMEM_LIMIT = 32 * 1024 * 1024

BF16 = jnp.bfloat16
F32 = jnp.float32
I32 = jnp.int32


def matmul(left, right, left_dim, right_dim):
    return lax.dot_general(
        left, right, (((left_dim,), (right_dim,)), ((), ())), preferred_element_type=F32
    )


def params():
    return pltpu.CompilerParams(vmem_limit_bytes=VMEM_LIMIT)


def in_hbm(array):
    return pltpu.with_memory_space_constraint(array, pltpu.HBM)


def spans(extent, size):
    return [(start, min(size, extent - start)) for start in range(0, extent, size)]


def dispatch_kernel(experts, hosts, slots, block, pieces, *refs):
    plan_hbm, caps_hbm, ids_hbm, gates_hbm, tok_hbm, grad_hbm = refs[:6]
    send_refs, pick_ref = refs[6 : 6 + pieces], refs[6 + pieces]
    plan_ref, caps_ref, ids_ref, gates_ref, tok_ref, grad_ref, sems = refs[7 + pieces :]
    copies = [
        pltpu.make_async_copy(source, target, sems.at[i])
        for i, (source, target) in enumerate(
            (
                (ids_hbm, ids_ref),
                (plan_hbm, plan_ref),
                (caps_hbm, caps_ref),
                (gates_hbm, gates_ref),
                (tok_hbm, tok_ref),
                (grad_hbm, grad_ref),
            )
        )
    ]
    for copy in copies:
        copy.start()
    me = lax.axis_index("expert")
    choose, count = ids_ref.shape
    row = lax.broadcasted_iota(I32, (block, count), 0)
    col = lax.broadcasted_iota(I32, (block, count), 1)
    is_cot = row >= slots
    slot = jnp.where(is_cot, row - slots, row)
    valid = row < 2 * slots
    is_spare = slot >= OWN
    spare_slot = jnp.maximum(slot - OWN, 0)
    replica = jnp.where(is_spare, 1 + lax.div(spare_slot, SPARE), 0)
    position = jnp.where(is_spare, lax.rem(spare_slot, SPARE), slot)
    token_slot = lax.rem(col, hosts)
    earlier = (
        lax.broadcasted_iota(I32, (count, count), 0) < lax.broadcasted_iota(I32, (count, count), 1)
    )
    earlier = earlier.astype(F32).astype(BF16)
    cots = jnp.concatenate([is_cot.astype(F32)] * experts, axis=0)
    for copy in copies[:4]:
        copy.wait()
    members, weights, limits = [], [], []
    for index in range(experts):
        expert = index if pieces == 1 else me ^ index
        hot = (plan_ref[0, 0] == expert) | (plan_ref[1, 0] == expert)
        wanted = token_slot * hot.astype(I32)
        here = jnp.zeros((1, count), F32)
        weight = jnp.zeros((1, count), F32)
        for k in range(choose):
            chosen = ids_ref[k : k + 1, :] == expert
            here = jnp.where(chosen, 1.0, here)
            weight = jnp.where(chosen, gates_ref[k : k + 1, :], weight)
        fits = valid & (replica == wanted)
        members.append(jnp.where(fits, jnp.broadcast_to(here, fits.shape), 0.0))
        weights.append(jnp.broadcast_to(weight, fits.shape))
        room = jnp.where(is_spare, SPARE, caps_ref[expert] * BLK)
        limits.append(jnp.where(position < room, position, -1))
    member = jnp.concatenate(members, axis=0)
    weight = jnp.concatenate(weights, axis=0)
    limit = jnp.concatenate(limits, axis=0).astype(F32)
    before = matmul(member.astype(BF16), earlier, 1, 0)
    taken = jnp.where(before == limit, member, 0.0)
    pick_cot = taken * cots
    pick_tok = taken - pick_cot
    gate = jnp.sum(taken * weight, axis=1, keepdims=True)
    scaled = pick_tok * weight
    high = scaled.astype(BF16)
    pick_cot = pick_cot.astype(BF16)
    pick_ref[0] = high
    pick_ref[1] = (scaled - high.astype(F32)).astype(BF16)
    pick_ref[2] = pick_cot
    for copy in copies[4:]:
        copy.wait()
    rows = matmul(pick_tok.astype(BF16), tok_ref[...], 1, 0)
    cotangents = gate * matmul(pick_cot, grad_ref[...], 1, 0)
    send = (rows + cotangents).astype(BF16)
    size = send.shape[0] // pieces
    for i, send_ref in enumerate(send_refs):
        send_ref[...] = send[i * size : (i + 1) * size]


def dispatch(plan, caps, ids, gates, tokens, grads, experts, slots, block, pieces):
    count, feature = tokens.shape
    vmem = pl.BlockSpec(memory_space=pltpu.VMEM)
    size = experts * block // pieces
    outs = pl.pallas_call(
        functools.partial(dispatch_kernel, experts, plan.shape[1], slots, block, pieces),
        out_shape=(jax.ShapeDtypeStruct((size, feature), BF16),) * pieces
        + (jax.ShapeDtypeStruct((3, experts * block, count), BF16),),
        in_specs=[pl.BlockSpec(memory_space=pltpu.HBM)] * 6,
        out_specs=(vmem,) * (pieces + 1),
        scratch_shapes=[
            pltpu.SMEM(plan.shape, I32),
            pltpu.SMEM(caps.shape, I32),
            pltpu.VMEM(ids.shape, I32),
            pltpu.VMEM(gates.shape, F32),
            pltpu.VMEM(tokens.shape, BF16),
            pltpu.VMEM(grads.shape, BF16),
            pltpu.SemaphoreType.DMA((6,)),
        ],
        compiler_params=params(),
        name="dispatch",
    )(*(in_hbm(array) for array in (plan, caps, ids, gates, tokens, grads)))
    return outs[:pieces], outs[pieces]


def load_kernel(gate_hbm, up_hbm, down_hbm, pick_ref, gate_ref, up_ref, down_ref, sems):
    copies = []
    for source, target in ((gate_hbm, gate_ref), (up_hbm, up_ref), (down_hbm, down_ref)):
        for start, size in spans(source.shape[0], source.shape[0] // LOADS):
            rows = pl.ds(start, size)
            copies.append(
                pltpu.make_async_copy(source.at[rows], target.at[rows], sems.at[len(copies)])
            )
    for copy in copies:
        copy.start()
    for copy in copies:
        copy.wait()


def load_weights(gate, up, down, pick):
    hbm = pl.BlockSpec(memory_space=pltpu.HBM)
    vmem = pl.BlockSpec(memory_space=pltpu.VMEM)
    assert all(w.shape[0] % (16 * LOADS) == 0 for w in (gate, up, down))
    return pl.pallas_call(
        load_kernel,
        out_shape=tuple(pltpu.VMEM(w.shape, BF16) for w in (gate, up, down)),
        in_specs=[hbm, hbm, hbm, pl.BlockSpec(memory_space=pl.ANY)],
        out_specs=(vmem, vmem, vmem),
        scratch_shapes=[pltpu.SemaphoreType.DMA((3 * LOADS,))],
        compiler_params=params(),
        cost_estimate=pl.CostEstimate(
            flops=0, bytes_accessed=2 * 3 * gate.size * 2, transcendentals=0
        ),
        name="load_weights",
    )(in_hbm(gate), in_hbm(up), in_hbm(down), pick)


def half_columns(which, width):
    half = width // 2
    side = lax.rem(lax.axis_index("dp") + which, 2)
    return pl.ds(pl.multiple_of(side * half, half), half)


def half_partials(which, rows, cots, gate_ref, up_ref, down_ref, part_ref):
    width = gate_ref.shape[1]
    half = width // 2
    units = half_columns(which, width)
    part_ref[:, :half] = matmul(rows, gate_ref[:, units], 1, 0).astype(BF16)
    part_ref[:, half : 2 * half] = matmul(rows, up_ref[:, units], 1, 0).astype(BF16)
    part_ref[:, 2 * half :] = matmul(cots, down_ref[units, :], 1, 1).astype(BF16)


def give_kernel(group, slots, block, pieces, *refs):
    recv_refs = refs[:pieces]
    gate_ref, up_ref, down_ref, rows_ref, cots_ref, give_ref, wide, flat = refs[pieces:]
    size = group * block // pieces
    for i, recv_ref in enumerate(recv_refs):
        wide[i * size : (i + 1) * size, :] = recv_ref[...].astype(F32)
    for s in range(group):
        flat[0, s * slots : (s + 1) * slots, :] = wide[s * block : s * block + slots, :]
        flat[1, s * slots : (s + 1) * slots, :] = wide[s * block + slots : s * block + 2 * slots, :]
    rows = flat[0].astype(BF16)
    cots = flat[1].astype(BF16)
    rows_ref[...] = rows
    cots_ref[...] = cots
    half_partials(1, rows, cots, gate_ref, up_ref, down_ref, give_ref)


def keep_kernel(rows_ref, cots_ref, gate_ref, up_ref, down_ref, keep_ref):
    half_partials(0, rows_ref[...], cots_ref[...], gate_ref, up_ref, down_ref, keep_ref)


def add_kernel(left_ref, right_ref, sum_ref):
    sum_ref[...] = (left_ref[...].astype(F32) + right_ref[...].astype(F32)).astype(BF16)


def activate_kernel(near_ref, far_ref, mine_ref):
    half = mine_ref.shape[1] // 3
    total = near_ref[...].astype(F32) + far_ref[...].astype(F32)
    gate_pre, up_pre, hidden_grad = (total[:, i * half : (i + 1) * half] for i in range(3))
    sigma = jax.nn.sigmoid(gate_pre)
    active = gate_pre * sigma
    slope = sigma * (1.0 + gate_pre * (1.0 - sigma))
    mine_ref[:, :half] = (active * up_pre).astype(BF16)
    mine_ref[:, half : 2 * half] = (hidden_grad * up_pre * slope).astype(BF16)
    mine_ref[:, 2 * half :] = (hidden_grad * active).astype(BF16)


def half_outputs(which, acts_ref, gate_ref, up_ref, down_ref):
    width = gate_ref.shape[1]
    half = width // 2
    units = half_columns(which, width)
    outs = matmul(acts_ref[:, :half], down_ref[units, :], 1, 0)
    ins = matmul(acts_ref[:, half : 2 * half], gate_ref[:, units], 1, 1)
    return outs, ins + matmul(acts_ref[:, 2 * half :], up_ref[:, units], 1, 1)


def own_kernel(mine_ref, gate_ref, up_ref, down_ref, outs_ref, ins_ref):
    outs_ref[...], ins_ref[...] = half_outputs(0, mine_ref, gate_ref, up_ref, down_ref)


def back_kernel(group, slots, block, pieces, *refs):
    theirs_ref, outs_ref, ins_ref, gate_ref, up_ref, down_ref = refs[:6]
    back_refs = refs[6 : 6 + pieces]
    flat, wide = refs[6 + pieces :]
    outs, ins = half_outputs(1, theirs_ref, gate_ref, up_ref, down_ref)
    flat[0] = outs_ref[...] + outs
    flat[1] = ins_ref[...] + ins
    wide[...] = jnp.zeros_like(wide)
    for s in range(group):
        wide[s * block : s * block + slots, :] = flat[0, s * slots : (s + 1) * slots, :]
        wide[s * block + slots : s * block + 2 * slots, :] = flat[1, s * slots : (s + 1) * slots, :]
    size = group * block // pieces
    for i, back_ref in enumerate(back_refs):
        back_ref[...] = wide[i * size : (i + 1) * size, :].astype(BF16)


def by_rows(kernel, name, steps, arrays, weights, outs, scratch=(), flops=0):
    def tiled(shape):
        return pl.BlockSpec((shape[0] // steps, shape[1]), lambda i: (i, 0))

    def whole(shape):
        return pl.BlockSpec(shape, lambda i: (0, 0))

    moved = sum(array.size * array.dtype.itemsize for array in (*arrays, *weights))
    results = pl.pallas_call(
        kernel,
        grid=(steps,),
        out_shape=tuple(jax.ShapeDtypeStruct(shape, dtype) for shape, dtype in outs),
        in_specs=[tiled(array.shape) for array in arrays] + [whole(w.shape) for w in weights],
        out_specs=tuple(tiled(shape) for shape, _ in outs),
        scratch_shapes=list(scratch),
        compiler_params=params(),
        cost_estimate=pl.CostEstimate(flops=flops, bytes_accessed=moved, transcendentals=0),
        name=name,
    )(*arrays, *weights)
    return results if len(outs) > 1 else results[0]


def grads_kernel(
    rows_ref, cots_ref, mine_ref, theirs_ref, gate_hbm, up_hbm, down_hbm, gate_ref, up_ref, down_ref, sems
):
    width = gate_ref.shape[1]
    half = width // 2
    copies = []

    def send(source, target, rows):
        copies.append(
            pltpu.make_async_copy(source.at[rows], target.at[rows], sems.at[len(copies)])
        )
        copies[-1].start()

    sides = [(mine_ref, half_columns(0, width)), (theirs_ref, half_columns(1, width))]
    for acts_ref, units in sides:
        for start, size in spans(half, CHUNK):
            rows = pl.ds(pl.multiple_of(units.start + start, 16), size)
            hidden = acts_ref[:, start : start + size]
            down_ref[rows, :] = matmul(hidden, cots_ref[...], 0, 0).astype(BF16)
            send(down_ref, down_hbm, rows)
    for place, out_ref, out_hbm in ((1, gate_ref, gate_hbm), (2, up_ref, up_hbm)):
        for start, size in spans(out_ref.shape[0], CHUNK):
            rows = pl.ds(start, size)
            for acts_ref, units in sides:
                grad = acts_ref[:, place * half : (place + 1) * half]
                out_ref[rows, units] = matmul(rows_ref[:, rows], grad, 0, 0).astype(BF16)
            send(out_ref, out_hbm, rows)
    for copy in copies:
        copy.wait()


def weight_grads(rows, cots, mine, theirs):
    total, feature = rows.shape
    width = 2 * mine.shape[1] // 3
    vmem = pl.BlockSpec(memory_space=pltpu.VMEM)
    hbm = pl.BlockSpec(memory_space=pltpu.HBM)
    shapes = ((feature, width), (feature, width), (width, feature))
    pieces = 2 * len(spans(feature, CHUNK)) + 2 * len(spans(width // 2, CHUNK))
    return pl.pallas_call(
        grads_kernel,
        out_shape=tuple(jax.ShapeDtypeStruct(shape, BF16) for shape in shapes),
        in_specs=[vmem] * 4,
        out_specs=(hbm,) * 3,
        scratch_shapes=[pltpu.VMEM(shape, BF16) for shape in shapes]
        + [pltpu.SemaphoreType.DMA((pieces,))],
        compiler_params=params(),
        cost_estimate=pl.CostEstimate(
            flops=6 * total * feature * width,
            bytes_accessed=6 * feature * width,
            transcendentals=0,
        ),
        name="weight_grads",
    )(rows, cots, mine, theirs)


def combine_kernel(pieces, *refs):
    back_refs = refs[:pieces]
    pick_ref, mixed_hbm, token_hbm, mixed_ref, token_ref, sems = refs[pieces:]
    back = jnp.concatenate([back_ref[...] for back_ref in back_refs], axis=0)
    token_ref[...] = matmul(pick_ref[2], back, 0, 0).astype(BF16)
    token_copy = pltpu.make_async_copy(token_ref, token_hbm, sems.at[0])
    token_copy.start()
    mixed = matmul(pick_ref[0], back, 0, 0) + matmul(pick_ref[1], back, 0, 0)
    mixed_ref[...] = mixed.astype(BF16)
    mixed_copy = pltpu.make_async_copy(mixed_ref, mixed_hbm, sems.at[1])
    mixed_copy.start()
    token_copy.wait()
    mixed_copy.wait()


def combine(backs, pick):
    feature, count = backs[0].shape[1], pick.shape[2]
    vmem = pl.BlockSpec(memory_space=pltpu.VMEM)
    hbm = pl.BlockSpec(memory_space=pltpu.HBM)
    shape = (count, feature)
    return pl.pallas_call(
        functools.partial(combine_kernel, len(backs)),
        out_shape=(jax.ShapeDtypeStruct(shape, BF16),) * 2,
        in_specs=[vmem] * (len(backs) + 1),
        out_specs=(hbm, hbm),
        scratch_shapes=[
            pltpu.VMEM(shape, BF16),
            pltpu.VMEM(shape, BF16),
            pltpu.SemaphoreType.DMA((2,)),
        ],
        compiler_params=params(),
        name="combine",
    )(*backs, pick)


def swapped(array, axis, distance):
    return lax.ppermute(array, axis, [(i, i ^ distance) for i in range(lax.axis_size(axis))])


def over_experts(arrays, experts):
    if len(arrays) == 1:
        array = arrays[0]
        blocks = array.reshape(experts, -1, array.shape[1])
        moved = lax.all_to_all(blocks, "expert", split_axis=0, concat_axis=0, tiled=True)
        return [moved.reshape(array.shape)]
    return [arrays[0]] + [swapped(arrays[d], "expert", d) for d in range(1, experts)]


def shards(
    tokens,
    out_grad,
    gate_weights,
    expert_ids,
    replica_plan,
    cap_blocks,
    gate_weight,
    up_weight,
    down_weight,
):
    experts = lax.axis_size("expert")
    hosts = replica_plan.shape[1]
    assert tokens.shape[0] % hosts == 0 and experts % GROUP == 0
    assert all(n >= 4 and n & (n - 1) == 0 for n in (experts, lax.axis_size("dp")))
    slots = OWN + SPARE * (hosts - 1)
    block = -(-2 * slots // 8) * 8
    pieces = experts if experts <= GROUP else 1
    gate, up, down = gate_weight[0], up_weight[0], down_weight[0]
    sends, pick = dispatch(
        replica_plan,
        cap_blocks,
        expert_ids.T,
        gate_weights.T,
        tokens,
        out_grad,
        experts,
        slots,
        block,
        pieces,
    )
    recvs = over_experts(sends, experts)
    weights = load_weights(gate, up, down, pick)
    feature, width = gate.shape
    tile, big = GROUP * slots, GROUP * block
    steps, total, half = experts // GROUP, experts * slots, 3 * width // 2
    layout = (GROUP, slots, block, pieces)
    flops = 3 * total * feature * width
    scratch = [pltpu.VMEM((big, feature), F32), pltpu.VMEM((2, tile, feature), F32)]
    rows, cots, give = by_rows(
        functools.partial(give_kernel, *layout),
        "give",
        steps,
        recvs,
        weights,
        [((total, feature), BF16), ((total, feature), BF16), ((total, half), BF16)],
        scratch,
        flops,
    )
    got = swapped(give, "dp", 1)
    keep = by_rows(
        keep_kernel, "keep", steps, [rows, cots], weights, [((total, half), BF16)], (), flops
    )
    near = by_rows(add_kernel, "add", steps, [keep, got], [], [((total, half), BF16)])
    distance, last = 2, lax.axis_size("dp") // 2
    while distance < last:
        far = swapped(near, "dp", distance)
        near = by_rows(add_kernel, "add", steps, [near, far], [], [((total, half), BF16)])
        distance *= 2
    far = swapped(near, "dp", last)
    mine = by_rows(activate_kernel, "activate", steps, [near, far], [], [((total, half), BF16)])
    theirs = swapped(mine, "dp", 1)
    outs, ins = by_rows(
        own_kernel, "own", steps, [mine], weights, [((total, feature), F32)] * 2, (), flops
    )
    backs = by_rows(
        functools.partial(back_kernel, *layout),
        "back",
        steps,
        [theirs, outs, ins],
        weights,
        [((experts * block // pieces, feature), BF16)] * pieces,
        scratch[::-1],
        flops,
    )
    returned = over_experts(backs if pieces > 1 else [backs], experts)
    gate_grad, up_grad, down_grad = weight_grads(rows, cots, mine, theirs)
    mixed, token_grad = combine(returned, pick)
    return mixed, token_grad, gate_grad[None], up_grad[None], down_grad[None]


def solution(mesh):
    return jax.shard_map(
        shards,
        mesh=mesh,
        in_specs=(
            P(("groups", "expert"), "dp"),
            P(("groups", "expert"), "dp"),
            P(("groups", "expert"), None),
            P(("groups", "expert"), None),
            P("groups", None),
            P("groups"),
            P("expert", "dp", None),
            P("expert", "dp", None),
            P("expert", None, "dp"),
        ),
        out_specs=(
            P(("groups", "expert"), "dp"),
            P(("groups", "expert"), "dp"),
            P(("groups", "expert"), "dp", None),
            P(("groups", "expert"), "dp", None),
            P(("groups", "expert"), None, "dp"),
        ),
        check_vma=False,
    )
```

```python
import functools

import jax
import jax.numpy as jnp
from jax import lax
from jax.experimental import pallas as pl
from jax.experimental.pallas import tpu as pltpu
from jax.sharding import PartitionSpec as P

BLK = 4
MAXB = 2
SPARE = 2
OWN = BLK * MAXB
GROUP = 4
CHUNK = 128
LOADS = 4
VMEM_LIMIT = 32 * 1024 * 1024

BF16 = jnp.bfloat16
F32 = jnp.float32
I32 = jnp.int32


def matmul(left, right, left_dim, right_dim):
    return lax.dot_general(
        left, right, (((left_dim,), (right_dim,)), ((), ())), preferred_element_type=F32
    )


def params():
    return pltpu.CompilerParams(vmem_limit_bytes=VMEM_LIMIT)


def in_hbm(array):
    return pltpu.with_memory_space_constraint(array, pltpu.HBM)


def spans(extent, size):
    return [(start, min(size, extent - start)) for start in range(0, extent, size)]


def dispatch_kernel(experts, hosts, slots, block, pieces, *refs):
    plan_hbm, caps_hbm, ids_hbm, gates_hbm, tok_hbm, grad_hbm = refs[:6]
    send_refs, pick_ref = refs[6 : 6 + pieces], refs[6 + pieces]
    plan_ref, caps_ref, ids_ref, gates_ref, tok_ref, grad_ref, sems = refs[7 + pieces :]
    copies = [
        pltpu.make_async_copy(source, target, sems.at[i])
        for i, (source, target) in enumerate(
            (
                (ids_hbm, ids_ref),
                (plan_hbm, plan_ref),
                (caps_hbm, caps_ref),
                (gates_hbm, gates_ref),
                (tok_hbm, tok_ref),
                (grad_hbm, grad_ref),
            )
        )
    ]
    for copy in copies:
        copy.start()
    me = lax.axis_index("expert")
    choose, count = ids_ref.shape
    row = lax.broadcasted_iota(I32, (block, count), 0)
    col = lax.broadcasted_iota(I32, (block, count), 1)
    is_cot = row >= slots
    slot = jnp.where(is_cot, row - slots, row)
    valid = row < 2 * slots
    is_spare = slot >= OWN
    spare_slot = jnp.maximum(slot - OWN, 0)
    replica = jnp.where(is_spare, 1 + lax.div(spare_slot, SPARE), 0)
    position = jnp.where(is_spare, lax.rem(spare_slot, SPARE), slot)
    token_slot = lax.rem(col, hosts)
    earlier = (
        lax.broadcasted_iota(I32, (count, count), 0) < lax.broadcasted_iota(I32, (count, count), 1)
    )
    earlier = earlier.astype(F32).astype(BF16)
    cots = jnp.concatenate([is_cot.astype(F32)] * experts, axis=0)
    for copy in copies[:4]:
        copy.wait()
    members, weights, limits = [], [], []
    for index in range(experts):
        expert = index if pieces == 1 else me ^ index
        hot = (plan_ref[0, 0] == expert) | (plan_ref[1, 0] == expert)
        wanted = token_slot * hot.astype(I32)
        here = jnp.zeros((1, count), F32)
        weight = jnp.zeros((1, count), F32)
        for k in range(choose):
            chosen = ids_ref[k : k + 1, :] == expert
            here = jnp.where(chosen, 1.0, here)
            weight = jnp.where(chosen, gates_ref[k : k + 1, :], weight)
        fits = valid & (replica == wanted)
        members.append(jnp.where(fits, jnp.broadcast_to(here, fits.shape), 0.0))
        weights.append(jnp.broadcast_to(weight, fits.shape))
        room = jnp.where(is_spare, SPARE, caps_ref[expert] * BLK)
        limits.append(jnp.where(position < room, position, -1))
    member = jnp.concatenate(members, axis=0)
    weight = jnp.concatenate(weights, axis=0)
    limit = jnp.concatenate(limits, axis=0).astype(F32)
    before = matmul(member.astype(BF16), earlier, 1, 0)
    taken = jnp.where(before == limit, member, 0.0)
    pick_cot = taken * cots
    pick_tok = taken - pick_cot
    gate = jnp.sum(taken * weight, axis=1, keepdims=True)
    scaled = pick_tok * weight
    high = scaled.astype(BF16)
    pick_cot = pick_cot.astype(BF16)
    pick_ref[0] = high
    pick_ref[1] = (scaled - high.astype(F32)).astype(BF16)
    pick_ref[2] = pick_cot
    for copy in copies[4:]:
        copy.wait()
    rows = matmul(pick_tok.astype(BF16), tok_ref[...], 1, 0)
    cotangents = gate * matmul(pick_cot, grad_ref[...], 1, 0)
    send = (rows + cotangents).astype(BF16)
    size = send.shape[0] // pieces
    for i, send_ref in enumerate(send_refs):
        send_ref[...] = send[i * size : (i + 1) * size]


def dispatch(plan, caps, ids, gates, tokens, grads, experts, slots, block, pieces):
    count, feature = tokens.shape
    vmem = pl.BlockSpec(memory_space=pltpu.VMEM)
    size = experts * block // pieces
    outs = pl.pallas_call(
        functools.partial(dispatch_kernel, experts, plan.shape[1], slots, block, pieces),
        out_shape=(jax.ShapeDtypeStruct((size, feature), BF16),) * pieces
        + (jax.ShapeDtypeStruct((3, experts * block, count), BF16),),
        in_specs=[pl.BlockSpec(memory_space=pltpu.HBM)] * 6,
        out_specs=(vmem,) * (pieces + 1),
        scratch_shapes=[
            pltpu.SMEM(plan.shape, I32),
            pltpu.SMEM(caps.shape, I32),
            pltpu.VMEM(ids.shape, I32),
            pltpu.VMEM(gates.shape, F32),
            pltpu.VMEM(tokens.shape, BF16),
            pltpu.VMEM(grads.shape, BF16),
            pltpu.SemaphoreType.DMA((6,)),
        ],
        compiler_params=params(),
        name="dispatch",
    )(*(in_hbm(array) for array in (plan, caps, ids, gates, tokens, grads)))
    return outs[:pieces], outs[pieces]


def load_kernel(gate_hbm, up_hbm, down_hbm, pick_ref, gate_ref, up_ref, down_ref, sems):
    copies = []
    for source, target in ((gate_hbm, gate_ref), (up_hbm, up_ref), (down_hbm, down_ref)):
        for start, size in spans(source.shape[0], source.shape[0] // LOADS):
            rows = pl.ds(start, size)
            copies.append(
                pltpu.make_async_copy(source.at[rows], target.at[rows], sems.at[len(copies)])
            )
    for copy in copies:
        copy.start()
    for copy in copies:
        copy.wait()


def load_weights(gate, up, down, pick):
    hbm = pl.BlockSpec(memory_space=pltpu.HBM)
    vmem = pl.BlockSpec(memory_space=pltpu.VMEM)
    assert all(w.shape[0] % (16 * LOADS) == 0 for w in (gate, up, down))
    return pl.pallas_call(
        load_kernel,
        out_shape=tuple(pltpu.VMEM(w.shape, BF16) for w in (gate, up, down)),
        in_specs=[hbm, hbm, hbm, pl.BlockSpec(memory_space=pl.ANY)],
        out_specs=(vmem, vmem, vmem),
        scratch_shapes=[pltpu.SemaphoreType.DMA((3 * LOADS,))],
        compiler_params=params(),
        cost_estimate=pl.CostEstimate(
            flops=0, bytes_accessed=2 * 3 * gate.size * 2, transcendentals=0
        ),
        name="load_weights",
    )(in_hbm(gate), in_hbm(up), in_hbm(down), pick)


def half_columns(which, width):
    half = width // 2
    side = lax.rem(lax.axis_index("dp") + which, 2)
    return pl.ds(pl.multiple_of(side * half, half), half)


def half_partials(which, rows, cots, gate_ref, up_ref, down_ref, part_ref):
    width = gate_ref.shape[1]
    half = width // 2
    units = half_columns(which, width)
    part_ref[:, :half] = matmul(rows, gate_ref[:, units], 1, 0).astype(BF16)
    part_ref[:, half : 2 * half] = matmul(rows, up_ref[:, units], 1, 0).astype(BF16)
    part_ref[:, 2 * half :] = matmul(cots, down_ref[units, :], 1, 1).astype(BF16)


def give_kernel(group, slots, block, pieces, *refs):
    recv_refs = refs[:pieces]
    gate_ref, up_ref, down_ref, rows_ref, cots_ref, give_ref, wide, flat = refs[pieces:]
    size = group * block // pieces
    for i, recv_ref in enumerate(recv_refs):
        wide[i * size : (i + 1) * size, :] = recv_ref[...].astype(F32)
    for s in range(group):
        flat[0, s * slots : (s + 1) * slots, :] = wide[s * block : s * block + slots, :]
        flat[1, s * slots : (s + 1) * slots, :] = wide[s * block + slots : s * block + 2 * slots, :]
    rows = flat[0].astype(BF16)
    cots = flat[1].astype(BF16)
    rows_ref[...] = rows
    cots_ref[...] = cots
    half_partials(1, rows, cots, gate_ref, up_ref, down_ref, give_ref)


def keep_kernel(rows_ref, cots_ref, gate_ref, up_ref, down_ref, keep_ref):
    half_partials(0, rows_ref[...], cots_ref[...], gate_ref, up_ref, down_ref, keep_ref)


def add_kernel(left_ref, right_ref, sum_ref):
    sum_ref[...] = (left_ref[...].astype(F32) + right_ref[...].astype(F32)).astype(BF16)


def activate_kernel(near_ref, far_ref, mine_ref):
    half = mine_ref.shape[1] // 3
    total = near_ref[...].astype(F32) + far_ref[...].astype(F32)
    gate_pre, up_pre, hidden_grad = (total[:, i * half : (i + 1) * half] for i in range(3))
    sigma = jax.nn.sigmoid(gate_pre)
    active = gate_pre * sigma
    slope = sigma * (1.0 + gate_pre * (1.0 - sigma))
    mine_ref[:, :half] = (active * up_pre).astype(BF16)
    mine_ref[:, half : 2 * half] = (hidden_grad * up_pre * slope).astype(BF16)
    mine_ref[:, 2 * half :] = (hidden_grad * active).astype(BF16)


def half_outputs(which, acts_ref, gate_ref, up_ref, down_ref):
    width = gate_ref.shape[1]
    half = width // 2
    units = half_columns(which, width)
    outs = matmul(acts_ref[:, :half], down_ref[units, :], 1, 0)
    ins = matmul(acts_ref[:, half : 2 * half], gate_ref[:, units], 1, 1)
    return outs, ins + matmul(acts_ref[:, 2 * half :], up_ref[:, units], 1, 1)


def own_kernel(mine_ref, gate_ref, up_ref, down_ref, outs_ref, ins_ref):
    outs_ref[...], ins_ref[...] = half_outputs(0, mine_ref, gate_ref, up_ref, down_ref)


def back_kernel(group, slots, block, pieces, *refs):
    theirs_ref, outs_ref, ins_ref, gate_ref, up_ref, down_ref = refs[:6]
    back_refs = refs[6 : 6 + pieces]
    flat, wide = refs[6 + pieces :]
    outs, ins = half_outputs(1, theirs_ref, gate_ref, up_ref, down_ref)
    flat[0] = outs_ref[...] + outs
    flat[1] = ins_ref[...] + ins
    wide[...] = jnp.zeros_like(wide)
    for s in range(group):
        wide[s * block : s * block + slots, :] = flat[0, s * slots : (s + 1) * slots, :]
        wide[s * block + slots : s * block + 2 * slots, :] = flat[1, s * slots : (s + 1) * slots, :]
    size = group * block // pieces
    for i, back_ref in enumerate(back_refs):
        back_ref[...] = wide[i * size : (i + 1) * size, :].astype(BF16)


def by_rows(kernel, name, steps, arrays, weights, outs, scratch=(), flops=0):
    def tiled(shape):
        return pl.BlockSpec((shape[0] // steps, shape[1]), lambda i: (i, 0))

    def whole(shape):
        return pl.BlockSpec(shape, lambda i: (0, 0))

    moved = sum(array.size * array.dtype.itemsize for array in (*arrays, *weights))
    results = pl.pallas_call(
        kernel,
        grid=(steps,),
        out_shape=tuple(jax.ShapeDtypeStruct(shape, dtype) for shape, dtype in outs),
        in_specs=[tiled(array.shape) for array in arrays] + [whole(w.shape) for w in weights],
        out_specs=tuple(tiled(shape) for shape, _ in outs),
        scratch_shapes=list(scratch),
        compiler_params=params(),
        cost_estimate=pl.CostEstimate(flops=flops, bytes_accessed=moved, transcendentals=0),
        name=name,
    )(*arrays, *weights)
    return results if len(outs) > 1 else results[0]


def grads_kernel(
    rows_ref, cots_ref, mine_ref, theirs_ref, gate_hbm, up_hbm, down_hbm, gate_ref, up_ref, down_ref, sems
):
    width = gate_ref.shape[1]
    half = width // 2
    copies = []

    def send(source, target, rows):
        copies.append(
            pltpu.make_async_copy(source.at[rows], target.at[rows], sems.at[len(copies)])
        )
        copies[-1].start()

    sides = [(mine_ref, half_columns(0, width)), (theirs_ref, half_columns(1, width))]
    for acts_ref, units in sides:
        for start, size in spans(half, CHUNK):
            rows = pl.ds(pl.multiple_of(units.start + start, 16), size)
            hidden = acts_ref[:, start : start + size]
            down_ref[rows, :] = matmul(hidden, cots_ref[...], 0, 0).astype(BF16)
            send(down_ref, down_hbm, rows)
    for place, out_ref, out_hbm in ((1, gate_ref, gate_hbm), (2, up_ref, up_hbm)):
        for start, size in spans(out_ref.shape[0], CHUNK):
            rows = pl.ds(start, size)
            for acts_ref, units in sides:
                grad = acts_ref[:, place * half : (place + 1) * half]
                out_ref[rows, units] = matmul(rows_ref[:, rows], grad, 0, 0).astype(BF16)
            send(out_ref, out_hbm, rows)
    for copy in copies:
        copy.wait()


def weight_grads(rows, cots, mine, theirs):
    total, feature = rows.shape
    width = 2 * mine.shape[1] // 3
    vmem = pl.BlockSpec(memory_space=pltpu.VMEM)
    hbm = pl.BlockSpec(memory_space=pltpu.HBM)
    shapes = ((feature, width), (feature, width), (width, feature))
    pieces = 2 * len(spans(feature, CHUNK)) + 2 * len(spans(width // 2, CHUNK))
    return pl.pallas_call(
        grads_kernel,
        out_shape=tuple(jax.ShapeDtypeStruct(shape, BF16) for shape in shapes),
        in_specs=[vmem] * 4,
        out_specs=(hbm,) * 3,
        scratch_shapes=[pltpu.VMEM(shape, BF16) for shape in shapes]
        + [pltpu.SemaphoreType.DMA((pieces,))],
        compiler_params=params(),
        cost_estimate=pl.CostEstimate(
            flops=6 * total * feature * width,
            bytes_accessed=6 * feature * width,
            transcendentals=0,
        ),
        name="weight_grads",
    )(rows, cots, mine, theirs)


def combine_kernel(pieces, *refs):
    back_refs = refs[:pieces]
    pick_ref, mixed_hbm, token_hbm, mixed_ref, token_ref, sems = refs[pieces:]
    back = jnp.concatenate([back_ref[...] for back_ref in back_refs], axis=0)
    token_ref[...] = matmul(pick_ref[2], back, 0, 0).astype(BF16)
    token_copy = pltpu.make_async_copy(token_ref, token_hbm, sems.at[0])
    token_copy.start()
    mixed = matmul(pick_ref[0], back, 0, 0) + matmul(pick_ref[1], back, 0, 0)
    mixed_ref[...] = mixed.astype(BF16)
    mixed_copy = pltpu.make_async_copy(mixed_ref, mixed_hbm, sems.at[1])
    mixed_copy.start()
    token_copy.wait()
    mixed_copy.wait()


def combine(backs, pick):
    feature, count = backs[0].shape[1], pick.shape[2]
    vmem = pl.BlockSpec(memory_space=pltpu.VMEM)
    hbm = pl.BlockSpec(memory_space=pltpu.HBM)
    shape = (count, feature)
    return pl.pallas_call(
        functools.partial(combine_kernel, len(backs)),
        out_shape=(jax.ShapeDtypeStruct(shape, BF16),) * 2,
        in_specs=[vmem] * (len(backs) + 1),
        out_specs=(hbm, hbm),
        scratch_shapes=[
            pltpu.VMEM(shape, BF16),
            pltpu.VMEM(shape, BF16),
            pltpu.SemaphoreType.DMA((2,)),
        ],
        compiler_params=params(),
        name="combine",
    )(*backs, pick)


def swapped(array, axis, distance):
    return lax.ppermute(array, axis, [(i, i ^ distance) for i in range(lax.axis_size(axis))])


def over_experts(arrays, experts):
    if len(arrays) == 1:
        array = arrays[0]
        blocks = array.reshape(experts, -1, array.shape[1])
        moved = lax.all_to_all(blocks, "expert", split_axis=0, concat_axis=0, tiled=True)
        return [moved.reshape(array.shape)]
    moved = {d: swapped(arrays[d], "expert", d) for d in reversed(range(1, experts))}
    return [arrays[0]] + [moved[d] for d in range(1, experts)]


def shards(
    tokens,
    out_grad,
    gate_weights,
    expert_ids,
    replica_plan,
    cap_blocks,
    gate_weight,
    up_weight,
    down_weight,
):
    experts = lax.axis_size("expert")
    hosts = replica_plan.shape[1]
    assert tokens.shape[0] % hosts == 0 and experts % GROUP == 0
    assert all(n >= 4 and n & (n - 1) == 0 for n in (experts, lax.axis_size("dp")))
    slots = OWN + SPARE * (hosts - 1)
    block = -(-2 * slots // 8) * 8
    pieces = experts if experts <= GROUP else 1
    gate, up, down = gate_weight[0], up_weight[0], down_weight[0]
    sends, pick = dispatch(
        replica_plan,
        cap_blocks,
        expert_ids.T,
        gate_weights.T,
        tokens,
        out_grad,
        experts,
        slots,
        block,
        pieces,
    )
    recvs = over_experts(sends, experts)
    weights = load_weights(gate, up, down, pick)
    feature, width = gate.shape
    tile, big = GROUP * slots, GROUP * block
    steps, total, half = experts // GROUP, experts * slots, 3 * width // 2
    layout = (GROUP, slots, block, pieces)
    flops = 3 * total * feature * width
    scratch = [pltpu.VMEM((big, feature), F32), pltpu.VMEM((2, tile, feature), F32)]
    rows, cots, give = by_rows(
        functools.partial(give_kernel, *layout),
        "give",
        steps,
        recvs,
        weights,
        [((total, feature), BF16), ((total, feature), BF16), ((total, half), BF16)],
        scratch,
        flops,
    )
    got = swapped(give, "dp", 1)
    keep = by_rows(
        keep_kernel, "keep", steps, [rows, cots], weights, [((total, half), BF16)], (), flops
    )
    near = by_rows(add_kernel, "add", steps, [keep, got], [], [((total, half), BF16)])
    distance, last = 2, lax.axis_size("dp") // 2
    while distance < last:
        far = swapped(near, "dp", distance)
        near = by_rows(add_kernel, "add", steps, [near, far], [], [((total, half), BF16)])
        distance *= 2
    far = swapped(near, "dp", last)
    mine = by_rows(activate_kernel, "activate", steps, [near, far], [], [((total, half), BF16)])
    theirs = swapped(mine, "dp", 1)
    outs, ins = by_rows(
        own_kernel, "own", steps, [mine], weights, [((total, feature), F32)] * 2, (), flops
    )
    backs = by_rows(
        functools.partial(back_kernel, *layout),
        "back",
        steps,
        [theirs, outs, ins],
        weights,
        [((experts * block // pieces, feature), BF16)] * pieces,
        scratch[::-1],
        flops,
    )
    returned = over_experts(backs if pieces > 1 else [backs], experts)
    gate_grad, up_grad, down_grad = weight_grads(rows, cots, mine, theirs)
    mixed, token_grad = combine(returned, pick)
    return mixed, token_grad, gate_grad[None], up_grad[None], down_grad[None]


def solution(mesh):
    return jax.shard_map(
        shards,
        mesh=mesh,
        in_specs=(
            P(("groups", "expert"), "dp"),
            P(("groups", "expert"), "dp"),
            P(("groups", "expert"), None),
            P(("groups", "expert"), None),
            P("groups", None),
            P("groups"),
            P("expert", "dp", None),
            P("expert", "dp", None),
            P("expert", None, "dp"),
        ),
        out_specs=(
            P(("groups", "expert"), "dp"),
            P(("groups", "expert"), "dp"),
            P(("groups", "expert"), "dp", None),
            P(("groups", "expert"), "dp", None),
            P(("groups", "expert"), None, "dp"),
        ),
        check_vma=False,
    )
```

```python
import functools

import jax
import jax.numpy as jnp
from jax import lax
from jax.experimental import pallas as pl
from jax.experimental.pallas import tpu as pltpu
from jax.sharding import PartitionSpec as P

BLK = 4
MAXB = 2
SPARE = 2
OWN = BLK * MAXB
GROUP = 4
CHUNK = 128
LOADS = 4
VMEM_LIMIT = 32 * 1024 * 1024

BF16 = jnp.bfloat16
F32 = jnp.float32
I32 = jnp.int32


def matmul(left, right, left_dim, right_dim):
    return lax.dot_general(
        left, right, (((left_dim,), (right_dim,)), ((), ())), preferred_element_type=F32
    )


def params():
    return pltpu.CompilerParams(vmem_limit_bytes=VMEM_LIMIT)


def in_hbm(array):
    return pltpu.with_memory_space_constraint(array, pltpu.HBM)


def spans(extent, size):
    return [(start, min(size, extent - start)) for start in range(0, extent, size)]


def distance(index, experts):
    return (experts - index) % experts


def dispatch_kernel(experts, hosts, slots, block, pieces, *refs):
    plan_hbm, caps_hbm, ids_hbm, gates_hbm, tok_hbm, grad_hbm = refs[:6]
    send_refs, pick_ref = refs[6 : 6 + pieces], refs[6 + pieces]
    plan_ref, caps_ref, ids_ref, gates_ref, tok_ref, grad_ref, sems = refs[7 + pieces :]
    copies = [
        pltpu.make_async_copy(source, target, sems.at[i])
        for i, (source, target) in enumerate(
            (
                (ids_hbm, ids_ref),
                (plan_hbm, plan_ref),
                (caps_hbm, caps_ref),
                (gates_hbm, gates_ref),
                (tok_hbm, tok_ref),
                (grad_hbm, grad_ref),
            )
        )
    ]
    for copy in copies:
        copy.start()
    me = lax.axis_index("expert")
    choose, count = ids_ref.shape
    row = lax.broadcasted_iota(I32, (block, count), 0)
    col = lax.broadcasted_iota(I32, (block, count), 1)
    is_cot = row >= slots
    slot = jnp.where(is_cot, row - slots, row)
    valid = row < 2 * slots
    is_spare = slot >= OWN
    spare_slot = jnp.maximum(slot - OWN, 0)
    replica = jnp.where(is_spare, 1 + lax.div(spare_slot, SPARE), 0)
    position = jnp.where(is_spare, lax.rem(spare_slot, SPARE), slot)
    token_slot = lax.rem(col, hosts)
    earlier = (
        lax.broadcasted_iota(I32, (count, count), 0) < lax.broadcasted_iota(I32, (count, count), 1)
    )
    earlier = earlier.astype(F32).astype(BF16)
    cots = jnp.concatenate([is_cot.astype(F32)] * experts, axis=0)
    for copy in copies[:4]:
        copy.wait()
    members, weights, limits = [], [], []
    for index in range(experts):
        expert = index if pieces == 1 else me ^ distance(index, experts)
        hot = (plan_ref[0, 0] == expert) | (plan_ref[1, 0] == expert)
        wanted = token_slot * hot.astype(I32)
        here = jnp.zeros((1, count), F32)
        weight = jnp.zeros((1, count), F32)
        for k in range(choose):
            chosen = ids_ref[k : k + 1, :] == expert
            here = jnp.where(chosen, 1.0, here)
            weight = jnp.where(chosen, gates_ref[k : k + 1, :], weight)
        fits = valid & (replica == wanted)
        members.append(jnp.where(fits, jnp.broadcast_to(here, fits.shape), 0.0))
        weights.append(jnp.broadcast_to(weight, fits.shape))
        room = jnp.where(is_spare, SPARE, caps_ref[expert] * BLK)
        limits.append(jnp.where(position < room, position, -1))
    member = jnp.concatenate(members, axis=0)
    weight = jnp.concatenate(weights, axis=0)
    limit = jnp.concatenate(limits, axis=0).astype(F32)
    before = matmul(member.astype(BF16), earlier, 1, 0)
    taken = jnp.where(before == limit, member, 0.0)
    pick_cot = taken * cots
    pick_tok = taken - pick_cot
    gate = jnp.sum(taken * weight, axis=1, keepdims=True)
    scaled = pick_tok * weight
    high = scaled.astype(BF16)
    pick_cot = pick_cot.astype(BF16)
    pick_ref[0] = high
    pick_ref[1] = (scaled - high.astype(F32)).astype(BF16)
    pick_ref[2] = pick_cot
    for copy in copies[4:]:
        copy.wait()
    rows = matmul(pick_tok.astype(BF16), tok_ref[...], 1, 0)
    cotangents = gate * matmul(pick_cot, grad_ref[...], 1, 0)
    send = (rows + cotangents).astype(BF16)
    size = send.shape[0] // pieces
    for i, send_ref in enumerate(send_refs):
        send_ref[...] = send[i * size : (i + 1) * size]


def dispatch(plan, caps, ids, gates, tokens, grads, experts, slots, block, pieces):
    count, feature = tokens.shape
    vmem = pl.BlockSpec(memory_space=pltpu.VMEM)
    size = experts * block // pieces
    outs = pl.pallas_call(
        functools.partial(dispatch_kernel, experts, plan.shape[1], slots, block, pieces),
        out_shape=(jax.ShapeDtypeStruct((size, feature), BF16),) * pieces
        + (jax.ShapeDtypeStruct((3, experts * block, count), BF16),),
        in_specs=[pl.BlockSpec(memory_space=pltpu.HBM)] * 6,
        out_specs=(vmem,) * (pieces + 1),
        scratch_shapes=[
            pltpu.SMEM(plan.shape, I32),
            pltpu.SMEM(caps.shape, I32),
            pltpu.VMEM(ids.shape, I32),
            pltpu.VMEM(gates.shape, F32),
            pltpu.VMEM(tokens.shape, BF16),
            pltpu.VMEM(grads.shape, BF16),
            pltpu.SemaphoreType.DMA((6,)),
        ],
        compiler_params=params(),
        name="dispatch",
    )(*(in_hbm(array) for array in (plan, caps, ids, gates, tokens, grads)))
    return outs[:pieces], outs[pieces]


def load_kernel(gate_hbm, up_hbm, down_hbm, pick_ref, gate_ref, up_ref, down_ref, sems):
    copies = []
    for source, target in ((gate_hbm, gate_ref), (up_hbm, up_ref), (down_hbm, down_ref)):
        for start, size in spans(source.shape[0], source.shape[0] // LOADS):
            rows = pl.ds(start, size)
            copies.append(
                pltpu.make_async_copy(source.at[rows], target.at[rows], sems.at[len(copies)])
            )
    for copy in copies:
        copy.start()
    for copy in copies:
        copy.wait()


def load_weights(gate, up, down, pick):
    hbm = pl.BlockSpec(memory_space=pltpu.HBM)
    vmem = pl.BlockSpec(memory_space=pltpu.VMEM)
    assert all(w.shape[0] % (16 * LOADS) == 0 for w in (gate, up, down))
    return pl.pallas_call(
        load_kernel,
        out_shape=tuple(pltpu.VMEM(w.shape, BF16) for w in (gate, up, down)),
        in_specs=[hbm, hbm, hbm, pl.BlockSpec(memory_space=pl.ANY)],
        out_specs=(vmem, vmem, vmem),
        scratch_shapes=[pltpu.SemaphoreType.DMA((3 * LOADS,))],
        compiler_params=params(),
        cost_estimate=pl.CostEstimate(
            flops=0, bytes_accessed=2 * 3 * gate.size * 2, transcendentals=0
        ),
        name="load_weights",
    )(in_hbm(gate), in_hbm(up), in_hbm(down), pick)


def half_columns(which, width):
    half = width // 2
    side = lax.rem(lax.axis_index("dp") + which, 2)
    return pl.ds(pl.multiple_of(side * half, half), half)


def half_partials(which, rows, cots, gate_ref, up_ref, down_ref, part_ref):
    width = gate_ref.shape[1]
    half = width // 2
    units = half_columns(which, width)
    part_ref[:, :half] = matmul(rows, gate_ref[:, units], 1, 0).astype(BF16)
    part_ref[:, half : 2 * half] = matmul(rows, up_ref[:, units], 1, 0).astype(BF16)
    part_ref[:, 2 * half :] = matmul(cots, down_ref[units, :], 1, 1).astype(BF16)


def give_kernel(group, slots, block, pieces, *refs):
    recv_refs = refs[:pieces]
    gate_ref, up_ref, down_ref, rows_ref, cots_ref, give_ref, wide, flat = refs[pieces:]
    size = group * block // pieces
    for i, recv_ref in enumerate(recv_refs):
        wide[i * size : (i + 1) * size, :] = recv_ref[...].astype(F32)
    for s in range(group):
        flat[0, s * slots : (s + 1) * slots, :] = wide[s * block : s * block + slots, :]
        flat[1, s * slots : (s + 1) * slots, :] = wide[s * block + slots : s * block + 2 * slots, :]
    rows = flat[0].astype(BF16)
    cots = flat[1].astype(BF16)
    rows_ref[...] = rows
    cots_ref[...] = cots
    half_partials(1, rows, cots, gate_ref, up_ref, down_ref, give_ref)


def keep_kernel(rows_ref, cots_ref, gate_ref, up_ref, down_ref, keep_ref):
    half_partials(0, rows_ref[...], cots_ref[...], gate_ref, up_ref, down_ref, keep_ref)


def add_kernel(left_ref, right_ref, sum_ref):
    sum_ref[...] = (left_ref[...].astype(F32) + right_ref[...].astype(F32)).astype(BF16)


def activate_kernel(near_ref, far_ref, mine_ref):
    half = mine_ref.shape[1] // 3
    total = near_ref[...].astype(F32) + far_ref[...].astype(F32)
    gate_pre, up_pre, hidden_grad = (total[:, i * half : (i + 1) * half] for i in range(3))
    sigma = jax.nn.sigmoid(gate_pre)
    active = gate_pre * sigma
    slope = sigma * (1.0 + gate_pre * (1.0 - sigma))
    mine_ref[:, :half] = (active * up_pre).astype(BF16)
    mine_ref[:, half : 2 * half] = (hidden_grad * up_pre * slope).astype(BF16)
    mine_ref[:, 2 * half :] = (hidden_grad * active).astype(BF16)


def half_outputs(which, acts_ref, gate_ref, up_ref, down_ref):
    width = gate_ref.shape[1]
    half = width // 2
    units = half_columns(which, width)
    outs = matmul(acts_ref[:, :half], down_ref[units, :], 1, 0)
    ins = matmul(acts_ref[:, half : 2 * half], gate_ref[:, units], 1, 1)
    return outs, ins + matmul(acts_ref[:, 2 * half :], up_ref[:, units], 1, 1)


def own_kernel(mine_ref, gate_ref, up_ref, down_ref, outs_ref, ins_ref):
    outs_ref[...], ins_ref[...] = half_outputs(0, mine_ref, gate_ref, up_ref, down_ref)


def back_kernel(group, slots, block, pieces, *refs):
    theirs_ref, outs_ref, ins_ref, gate_ref, up_ref, down_ref = refs[:6]
    back_refs = refs[6 : 6 + pieces]
    flat, wide = refs[6 + pieces :]
    outs, ins = half_outputs(1, theirs_ref, gate_ref, up_ref, down_ref)
    flat[0] = outs_ref[...] + outs
    flat[1] = ins_ref[...] + ins
    wide[...] = jnp.zeros_like(wide)
    for s in range(group):
        wide[s * block : s * block + slots, :] = flat[0, s * slots : (s + 1) * slots, :]
        wide[s * block + slots : s * block + 2 * slots, :] = flat[1, s * slots : (s + 1) * slots, :]
    size = group * block // pieces
    for i, back_ref in enumerate(back_refs):
        back_ref[...] = wide[i * size : (i + 1) * size, :].astype(BF16)


def by_rows(kernel, name, steps, arrays, weights, outs, scratch=(), flops=0):
    def tiled(shape):
        return pl.BlockSpec((shape[0] // steps, shape[1]), lambda i: (i, 0))

    def whole(shape):
        return pl.BlockSpec(shape, lambda i: (0, 0))

    moved = sum(array.size * array.dtype.itemsize for array in (*arrays, *weights))
    results = pl.pallas_call(
        kernel,
        grid=(steps,),
        out_shape=tuple(jax.ShapeDtypeStruct(shape, dtype) for shape, dtype in outs),
        in_specs=[tiled(array.shape) for array in arrays] + [whole(w.shape) for w in weights],
        out_specs=tuple(tiled(shape) for shape, _ in outs),
        scratch_shapes=list(scratch),
        compiler_params=params(),
        cost_estimate=pl.CostEstimate(flops=flops, bytes_accessed=moved, transcendentals=0),
        name=name,
    )(*arrays, *weights)
    return results if len(outs) > 1 else results[0]


def grads_kernel(
    rows_ref, cots_ref, mine_ref, theirs_ref, gate_hbm, up_hbm, down_hbm, gate_ref, up_ref, down_ref, sems
):
    width = gate_ref.shape[1]
    half = width // 2
    copies = []

    def send(source, target, rows):
        copies.append(
            pltpu.make_async_copy(source.at[rows], target.at[rows], sems.at[len(copies)])
        )
        copies[-1].start()

    sides = [(mine_ref, half_columns(0, width)), (theirs_ref, half_columns(1, width))]
    for acts_ref, units in sides:
        for start, size in spans(half, CHUNK):
            rows = pl.ds(pl.multiple_of(units.start + start, 16), size)
            hidden = acts_ref[:, start : start + size]
            down_ref[rows, :] = matmul(hidden, cots_ref[...], 0, 0).astype(BF16)
            send(down_ref, down_hbm, rows)
    for place, out_ref, out_hbm in ((1, gate_ref, gate_hbm), (2, up_ref, up_hbm)):
        for start, size in spans(out_ref.shape[0], CHUNK):
            rows = pl.ds(start, size)
            for acts_ref, units in sides:
                grad = acts_ref[:, place * half : (place + 1) * half]
                out_ref[rows, units] = matmul(rows_ref[:, rows], grad, 0, 0).astype(BF16)
            send(out_ref, out_hbm, rows)
    for copy in copies:
        copy.wait()


def weight_grads(rows, cots, mine, theirs):
    total, feature = rows.shape
    width = 2 * mine.shape[1] // 3
    vmem = pl.BlockSpec(memory_space=pltpu.VMEM)
    hbm = pl.BlockSpec(memory_space=pltpu.HBM)
    shapes = ((feature, width), (feature, width), (width, feature))
    pieces = 2 * len(spans(feature, CHUNK)) + 2 * len(spans(width // 2, CHUNK))
    return pl.pallas_call(
        grads_kernel,
        out_shape=tuple(jax.ShapeDtypeStruct(shape, BF16) for shape in shapes),
        in_specs=[vmem] * 4,
        out_specs=(hbm,) * 3,
        scratch_shapes=[pltpu.VMEM(shape, BF16) for shape in shapes]
        + [pltpu.SemaphoreType.DMA((pieces,))],
        compiler_params=params(),
        cost_estimate=pl.CostEstimate(
            flops=6 * total * feature * width,
            bytes_accessed=6 * feature * width,
            transcendentals=0,
        ),
        name="weight_grads",
    )(rows, cots, mine, theirs)


def combine_kernel(pieces, *refs):
    back_refs = refs[:pieces]
    pick_ref, mixed_hbm, token_hbm, mixed_ref, token_ref, sems = refs[pieces:]
    back = jnp.concatenate([back_ref[...] for back_ref in back_refs], axis=0)
    token_ref[...] = matmul(pick_ref[2], back, 0, 0).astype(BF16)
    token_copy = pltpu.make_async_copy(token_ref, token_hbm, sems.at[0])
    token_copy.start()
    mixed = matmul(pick_ref[0], back, 0, 0) + matmul(pick_ref[1], back, 0, 0)
    mixed_ref[...] = mixed.astype(BF16)
    mixed_copy = pltpu.make_async_copy(mixed_ref, mixed_hbm, sems.at[1])
    mixed_copy.start()
    token_copy.wait()
    mixed_copy.wait()


def combine(backs, pick):
    feature, count = backs[0].shape[1], pick.shape[2]
    vmem = pl.BlockSpec(memory_space=pltpu.VMEM)
    hbm = pl.BlockSpec(memory_space=pltpu.HBM)
    shape = (count, feature)
    return pl.pallas_call(
        functools.partial(combine_kernel, len(backs)),
        out_shape=(jax.ShapeDtypeStruct(shape, BF16),) * 2,
        in_specs=[vmem] * (len(backs) + 1),
        out_specs=(hbm, hbm),
        scratch_shapes=[
            pltpu.VMEM(shape, BF16),
            pltpu.VMEM(shape, BF16),
            pltpu.SemaphoreType.DMA((2,)),
        ],
        compiler_params=params(),
        name="combine",
    )(*backs, pick)


def swapped(array, axis, distance):
    return lax.ppermute(array, axis, [(i, i ^ distance) for i in range(lax.axis_size(axis))])


def over_experts(arrays, experts):
    if len(arrays) == 1:
        array = arrays[0]
        blocks = array.reshape(experts, -1, array.shape[1])
        moved = lax.all_to_all(blocks, "expert", split_axis=0, concat_axis=0, tiled=True)
        return [moved.reshape(array.shape)]
    moved = [swapped(arrays[i], "expert", distance(i, experts)) for i in range(1, experts)]
    return [arrays[0]] + moved


def shards(
    tokens,
    out_grad,
    gate_weights,
    expert_ids,
    replica_plan,
    cap_blocks,
    gate_weight,
    up_weight,
    down_weight,
):
    experts = lax.axis_size("expert")
    hosts = replica_plan.shape[1]
    assert tokens.shape[0] % hosts == 0 and experts % GROUP == 0
    assert all(n >= 4 and n & (n - 1) == 0 for n in (experts, lax.axis_size("dp")))
    slots = OWN + SPARE * (hosts - 1)
    block = -(-2 * slots // 8) * 8
    pieces = experts if experts <= GROUP else 1
    gate, up, down = gate_weight[0], up_weight[0], down_weight[0]
    sends, pick = dispatch(
        replica_plan,
        cap_blocks,
        expert_ids.T,
        gate_weights.T,
        tokens,
        out_grad,
        experts,
        slots,
        block,
        pieces,
    )
    recvs = over_experts(sends, experts)
    weights = load_weights(gate, up, down, pick)
    feature, width = gate.shape
    tile, big = GROUP * slots, GROUP * block
    steps, total, half = experts // GROUP, experts * slots, 3 * width // 2
    layout = (GROUP, slots, block, pieces)
    flops = 3 * total * feature * width
    scratch = [pltpu.VMEM((big, feature), F32), pltpu.VMEM((2, tile, feature), F32)]
    rows, cots, give = by_rows(
        functools.partial(give_kernel, *layout),
        "give",
        steps,
        recvs,
        weights,
        [((total, feature), BF16), ((total, feature), BF16), ((total, half), BF16)],
        scratch,
        flops,
    )
    got = swapped(give, "dp", 1)
    keep = by_rows(
        keep_kernel, "keep", steps, [rows, cots], weights, [((total, half), BF16)], (), flops
    )
    near = by_rows(add_kernel, "add", steps, [keep, got], [], [((total, half), BF16)])
    step, last = 2, lax.axis_size("dp") // 2
    while step < last:
        far = swapped(near, "dp", step)
        near = by_rows(add_kernel, "add", steps, [near, far], [], [((total, half), BF16)])
        step *= 2
    far = swapped(near, "dp", last)
    mine = by_rows(activate_kernel, "activate", steps, [near, far], [], [((total, half), BF16)])
    theirs = swapped(mine, "dp", 1)
    outs, ins = by_rows(
        own_kernel, "own", steps, [mine], weights, [((total, feature), F32)] * 2, (), flops
    )
    backs = by_rows(
        functools.partial(back_kernel, *layout),
        "back",
        steps,
        [theirs, outs, ins],
        weights,
        [((experts * block // pieces, feature), BF16)] * pieces,
        scratch[::-1],
        flops,
    )
    returned = over_experts(backs if pieces > 1 else [backs], experts)
    gate_grad, up_grad, down_grad = weight_grads(rows, cots, mine, theirs)
    mixed, token_grad = combine(returned, pick)
    return mixed, token_grad, gate_grad[None], up_grad[None], down_grad[None]


def solution(mesh):
    return jax.shard_map(
        shards,
        mesh=mesh,
        in_specs=(
            P(("groups", "expert"), "dp"),
            P(("groups", "expert"), "dp"),
            P(("groups", "expert"), None),
            P(("groups", "expert"), None),
            P("groups", None),
            P("groups"),
            P("expert", "dp", None),
            P("expert", "dp", None),
            P("expert", None, "dp"),
        ),
        out_specs=(
            P(("groups", "expert"), "dp"),
            P(("groups", "expert"), "dp"),
            P(("groups", "expert"), "dp", None),
            P(("groups", "expert"), "dp", None),
            P(("groups", "expert"), None, "dp"),
        ),
        check_vma=False,
    )
```

```python
import functools

import jax
import jax.numpy as jnp
from jax import lax
from jax.experimental import pallas as pl
from jax.experimental.pallas import tpu as pltpu
from jax.sharding import PartitionSpec as P

BLK = 4
MAXB = 2
SPARE = 2
OWN = BLK * MAXB
GROUP = 4
CHUNK = 128
LOADS = 4
VMEM_LIMIT = 32 * 1024 * 1024

BF16 = jnp.bfloat16
F32 = jnp.float32
I32 = jnp.int32


def matmul(left, right, left_dim, right_dim):
    return lax.dot_general(
        left, right, (((left_dim,), (right_dim,)), ((), ())), preferred_element_type=F32
    )


def params():
    return pltpu.CompilerParams(vmem_limit_bytes=VMEM_LIMIT)


def in_hbm(array):
    return pltpu.with_memory_space_constraint(array, pltpu.HBM)


def spans(extent, size):
    return [(start, min(size, extent - start)) for start in range(0, extent, size)]


def distance(index, experts):
    return (experts - index) % experts


def dispatch_kernel(experts, hosts, slots, block, pieces, *refs):
    plan_hbm, caps_hbm, ids_hbm, gates_hbm, tok_hbm, grad_hbm = refs[:6]
    send_refs = refs[6 : 6 + pieces]
    scaled_ref, pick_ref, plan_ref, caps_ref, ids_ref, gates_ref, both_ref, sems = refs[6 + pieces :]
    choose, count = ids_ref.shape
    copies = [
        pltpu.make_async_copy(source, target, sems.at[i])
        for i, (source, target) in enumerate(
            (
                (ids_hbm, ids_ref),
                (plan_hbm, plan_ref),
                (caps_hbm, caps_ref),
                (gates_hbm, gates_ref),
                (tok_hbm, both_ref.at[pl.ds(0, count)]),
                (grad_hbm, both_ref.at[pl.ds(count, count)]),
            )
        )
    ]
    for copy in copies:
        copy.start()
    me = lax.axis_index("expert")
    row = lax.broadcasted_iota(I32, (block, count), 0)
    col = lax.broadcasted_iota(I32, (block, count), 1)
    is_cot = row >= slots
    slot = jnp.where(is_cot, row - slots, row)
    valid = row < 2 * slots
    is_spare = slot >= OWN
    spare_slot = jnp.maximum(slot - OWN, 0)
    replica = jnp.where(is_spare, 1 + lax.div(spare_slot, SPARE), 0)
    position = jnp.where(is_spare, lax.rem(spare_slot, SPARE), slot)
    token_slot = lax.rem(col, hosts)
    earlier = (
        lax.broadcasted_iota(I32, (count, count), 0) < lax.broadcasted_iota(I32, (count, count), 1)
    )
    earlier = earlier.astype(F32).astype(BF16)
    cots = jnp.concatenate([is_cot.astype(F32)] * experts, axis=0)
    for copy in copies[:4]:
        copy.wait()
    members, weights, limits = [], [], []
    for index in range(experts):
        expert = index if pieces == 1 else me ^ distance(index, experts)
        hot = (plan_ref[0, 0] == expert) | (plan_ref[1, 0] == expert)
        wanted = token_slot * hot.astype(I32)
        here = jnp.zeros((1, count), F32)
        weight = jnp.zeros((1, count), F32)
        for k in range(choose):
            chosen = ids_ref[k : k + 1, :] == expert
            here = jnp.where(chosen, 1.0, here)
            weight = jnp.where(chosen, gates_ref[k : k + 1, :], weight)
        fits = valid & (replica == wanted)
        members.append(jnp.where(fits, jnp.broadcast_to(here, fits.shape), 0.0))
        weights.append(jnp.broadcast_to(weight, fits.shape))
        room = jnp.where(is_spare, SPARE, caps_ref[expert] * BLK)
        limits.append(jnp.where(position < room, position, -1))
    member = jnp.concatenate(members, axis=0)
    weight = jnp.concatenate(weights, axis=0)
    limit = jnp.concatenate(limits, axis=0).astype(F32)
    before = matmul(member.astype(BF16), earlier, 1, 0)
    taken = jnp.where(before == limit, member, 0.0)
    pick_cot = taken * cots
    pick_tok = taken - pick_cot
    picks = jnp.concatenate([pick_tok.astype(BF16), pick_cot.astype(BF16)], axis=1)
    gate = jnp.sum(pick_cot * weight, axis=1, keepdims=True)
    scale = jnp.where(cots[:, :1] > 0.0, gate, 1.0)
    scaled_ref[...] = pick_tok * weight
    pick_ref[...] = pick_cot
    for copy in copies[4:]:
        copy.wait()
    send = (scale * matmul(picks, both_ref[...], 1, 0)).astype(BF16)
    size = send.shape[0] // pieces
    for i, send_ref in enumerate(send_refs):
        send_ref[...] = send[i * size : (i + 1) * size]


def dispatch(plan, caps, ids, gates, tokens, grads, experts, slots, block, pieces):
    count, feature = tokens.shape
    vmem = pl.BlockSpec(memory_space=pltpu.VMEM)
    size = experts * block // pieces
    outs = pl.pallas_call(
        functools.partial(dispatch_kernel, experts, plan.shape[1], slots, block, pieces),
        out_shape=(jax.ShapeDtypeStruct((size, feature), BF16),) * pieces
        + (jax.ShapeDtypeStruct((experts * block, count), F32),) * 2,
        in_specs=[pl.BlockSpec(memory_space=pltpu.HBM)] * 6,
        out_specs=(vmem,) * (pieces + 2),
        scratch_shapes=[
            pltpu.SMEM(plan.shape, I32),
            pltpu.SMEM(caps.shape, I32),
            pltpu.VMEM(ids.shape, I32),
            pltpu.VMEM(gates.shape, F32),
            pltpu.VMEM((2 * count, feature), BF16),
            pltpu.SemaphoreType.DMA((6,)),
        ],
        compiler_params=params(),
        name="dispatch",
    )(*(in_hbm(array) for array in (plan, caps, ids, gates, tokens, grads)))
    return outs[:pieces], outs[pieces:]


def load_kernel(
    gate_hbm, up_hbm, down_hbm, scaled_ref, pick_ref, gate_ref, up_ref, down_ref, merge_ref, sems
):
    copies = []
    for source, target in ((gate_hbm, gate_ref), (up_hbm, up_ref), (down_hbm, down_ref)):
        for start, size in spans(source.shape[0], source.shape[0] // LOADS):
            rows = pl.ds(start, size)
            copies.append(
                pltpu.make_async_copy(source.at[rows], target.at[rows], sems.at[len(copies)])
            )
    for copy in copies:
        copy.start()
    scaled = scaled_ref[...].T
    count = scaled.shape[0]
    high = scaled.astype(BF16)
    merge_ref[:count, :] = high
    merge_ref[count : 2 * count, :] = (scaled - high.astype(F32)).astype(BF16)
    merge_ref[2 * count :, :] = pick_ref[...].T.astype(BF16)
    for copy in copies:
        copy.wait()


def load_weights(gate, up, down, scaled, pick):
    hbm = pl.BlockSpec(memory_space=pltpu.HBM)
    vmem = pl.BlockSpec(memory_space=pltpu.VMEM)
    assert all(w.shape[0] % (16 * LOADS) == 0 for w in (gate, up, down))
    merge = jax.ShapeDtypeStruct((3 * pick.shape[1], pick.shape[0]), BF16)
    return pl.pallas_call(
        load_kernel,
        out_shape=tuple(pltpu.VMEM(w.shape, BF16) for w in (gate, up, down)) + (merge,),
        in_specs=[hbm, hbm, hbm, vmem, vmem],
        out_specs=(vmem,) * 4,
        scratch_shapes=[pltpu.SemaphoreType.DMA((3 * LOADS,))],
        compiler_params=params(),
        cost_estimate=pl.CostEstimate(
            flops=0, bytes_accessed=2 * 3 * gate.size * 2, transcendentals=0
        ),
        name="load_weights",
    )(in_hbm(gate), in_hbm(up), in_hbm(down), scaled, pick)


def half_columns(which, width):
    half = width // 2
    side = lax.rem(lax.axis_index("dp") + which, 2)
    return pl.ds(pl.multiple_of(side * half, half), half)


def half_partials(which, rows, cots, gate_ref, up_ref, down_ref, part_ref):
    width = gate_ref.shape[1]
    half = width // 2
    units = half_columns(which, width)
    part_ref[:, :half] = matmul(rows, gate_ref[:, units], 1, 0).astype(BF16)
    part_ref[:, half : 2 * half] = matmul(rows, up_ref[:, units], 1, 0).astype(BF16)
    part_ref[:, 2 * half :] = matmul(cots, down_ref[units, :], 1, 1).astype(BF16)


def give_kernel(group, slots, block, pieces, *refs):
    recv_refs = refs[:pieces]
    gate_ref, up_ref, down_ref, rows_ref, cots_ref, give_ref, wide, flat = refs[pieces:]
    size = group * block // pieces
    for i, recv_ref in enumerate(recv_refs):
        wide[i * size : (i + 1) * size, :] = recv_ref[...].astype(F32)
    for s in range(group):
        flat[0, s * slots : (s + 1) * slots, :] = wide[s * block : s * block + slots, :]
        flat[1, s * slots : (s + 1) * slots, :] = wide[s * block + slots : s * block + 2 * slots, :]
    rows = flat[0].astype(BF16)
    cots = flat[1].astype(BF16)
    rows_ref[...] = rows
    cots_ref[...] = cots
    half_partials(1, rows, cots, gate_ref, up_ref, down_ref, give_ref)


def keep_kernel(rows_ref, cots_ref, gate_ref, up_ref, down_ref, keep_ref):
    half_partials(0, rows_ref[...], cots_ref[...], gate_ref, up_ref, down_ref, keep_ref)


def add_kernel(left_ref, right_ref, sum_ref):
    sum_ref[...] = (left_ref[...].astype(F32) + right_ref[...].astype(F32)).astype(BF16)


def activate_kernel(near_ref, far_ref, mine_ref):
    half = mine_ref.shape[1] // 3
    total = near_ref[...].astype(F32) + far_ref[...].astype(F32)
    gate_pre, up_pre, hidden_grad = (total[:, i * half : (i + 1) * half] for i in range(3))
    sigma = jax.nn.sigmoid(gate_pre)
    active = gate_pre * sigma
    slope = sigma * (1.0 + gate_pre * (1.0 - sigma))
    mine_ref[:, :half] = (active * up_pre).astype(BF16)
    mine_ref[:, half : 2 * half] = (hidden_grad * up_pre * slope).astype(BF16)
    mine_ref[:, 2 * half :] = (hidden_grad * active).astype(BF16)


def half_outputs(which, acts_ref, gate_ref, up_ref, down_ref):
    width = gate_ref.shape[1]
    half = width // 2
    units = half_columns(which, width)
    outs = matmul(acts_ref[:, :half], down_ref[units, :], 1, 0)
    ins = matmul(acts_ref[:, half : 2 * half], gate_ref[:, units], 1, 1)
    return outs, ins + matmul(acts_ref[:, 2 * half :], up_ref[:, units], 1, 1)


def own_kernel(mine_ref, gate_ref, up_ref, down_ref, outs_ref, ins_ref):
    outs_ref[...], ins_ref[...] = half_outputs(0, mine_ref, gate_ref, up_ref, down_ref)


def back_kernel(group, slots, block, pieces, *refs):
    theirs_ref, outs_ref, ins_ref, gate_ref, up_ref, down_ref = refs[:6]
    back_refs = refs[6 : 6 + pieces]
    flat, wide = refs[6 + pieces :]
    outs, ins = half_outputs(1, theirs_ref, gate_ref, up_ref, down_ref)
    flat[0] = outs_ref[...] + outs
    flat[1] = ins_ref[...] + ins
    wide[...] = jnp.zeros_like(wide)
    for s in range(group):
        wide[s * block : s * block + slots, :] = flat[0, s * slots : (s + 1) * slots, :]
        wide[s * block + slots : s * block + 2 * slots, :] = flat[1, s * slots : (s + 1) * slots, :]
    size = group * block // pieces
    for i, back_ref in enumerate(back_refs):
        back_ref[...] = wide[i * size : (i + 1) * size, :].astype(BF16)


def by_rows(kernel, name, steps, arrays, weights, outs, scratch=(), flops=0):
    def tiled(shape):
        return pl.BlockSpec((shape[0] // steps, shape[1]), lambda i: (i, 0))

    def whole(shape):
        return pl.BlockSpec(shape, lambda i: (0, 0))

    moved = sum(array.size * array.dtype.itemsize for array in (*arrays, *weights))
    results = pl.pallas_call(
        kernel,
        grid=(steps,),
        out_shape=tuple(jax.ShapeDtypeStruct(shape, dtype) for shape, dtype in outs),
        in_specs=[tiled(array.shape) for array in arrays] + [whole(w.shape) for w in weights],
        out_specs=tuple(tiled(shape) for shape, _ in outs),
        scratch_shapes=list(scratch),
        compiler_params=params(),
        cost_estimate=pl.CostEstimate(flops=flops, bytes_accessed=moved, transcendentals=0),
        name=name,
    )(*arrays, *weights)
    return results if len(outs) > 1 else results[0]


def grads_kernel(
    rows_ref, cots_ref, mine_ref, theirs_ref, gate_hbm, up_hbm, down_hbm, gate_ref, up_ref, down_ref, sems
):
    width = gate_ref.shape[1]
    half = width // 2
    copies = []

    def send(source, target, rows):
        copies.append(
            pltpu.make_async_copy(source.at[rows], target.at[rows], sems.at[len(copies)])
        )
        copies[-1].start()

    sides = [(mine_ref, half_columns(0, width)), (theirs_ref, half_columns(1, width))]
    for acts_ref, units in sides:
        for start, size in spans(half, CHUNK):
            rows = pl.ds(pl.multiple_of(units.start + start, 16), size)
            hidden = acts_ref[:, start : start + size]
            down_ref[rows, :] = matmul(hidden, cots_ref[...], 0, 0).astype(BF16)
            send(down_ref, down_hbm, rows)
    for place, out_ref, out_hbm in ((1, gate_ref, gate_hbm), (2, up_ref, up_hbm)):
        for start, size in spans(out_ref.shape[0], CHUNK):
            rows = pl.ds(start, size)
            for acts_ref, units in sides:
                grad = acts_ref[:, place * half : (place + 1) * half]
                out_ref[rows, units] = matmul(rows_ref[:, rows], grad, 0, 0).astype(BF16)
            send(out_ref, out_hbm, rows)
    for copy in copies:
        copy.wait()


def weight_grads(rows, cots, mine, theirs):
    total, feature = rows.shape
    width = 2 * mine.shape[1] // 3
    vmem = pl.BlockSpec(memory_space=pltpu.VMEM)
    hbm = pl.BlockSpec(memory_space=pltpu.HBM)
    shapes = ((feature, width), (feature, width), (width, feature))
    pieces = 2 * len(spans(feature, CHUNK)) + 2 * len(spans(width // 2, CHUNK))
    return pl.pallas_call(
        grads_kernel,
        out_shape=tuple(jax.ShapeDtypeStruct(shape, BF16) for shape in shapes),
        in_specs=[vmem] * 4,
        out_specs=(hbm,) * 3,
        scratch_shapes=[pltpu.VMEM(shape, BF16) for shape in shapes]
        + [pltpu.SemaphoreType.DMA((pieces,))],
        compiler_params=params(),
        cost_estimate=pl.CostEstimate(
            flops=6 * total * feature * width,
            bytes_accessed=6 * feature * width,
            transcendentals=0,
        ),
        name="weight_grads",
    )(rows, cots, mine, theirs)


def combine_kernel(columns, pieces, *refs):
    back_refs = refs[:pieces]
    merge_ref, mixed_hbm, token_hbm, mixed_ref, token_ref, sems = refs[pieces:]
    count = mixed_ref.shape[0]
    copies = []
    for start, size in columns:
        part = pl.ds(start, size)
        back = jnp.concatenate([back_ref[:, part] for back_ref in back_refs], axis=0)
        sums = matmul(merge_ref[...], back, 1, 0)
        mixed_ref[:, part] = (sums[:count] + sums[count : 2 * count]).astype(BF16)
        token_ref[:, part] = sums[2 * count :].astype(BF16)
        for source, target in ((mixed_ref, mixed_hbm), (token_ref, token_hbm)):
            copies.append(
                pltpu.make_async_copy(
                    source.at[:, part], target.at[:, part], sems.at[len(copies)]
                )
            )
            copies[-1].start()
    for copy in copies:
        copy.wait()


def combine(backs, merge):
    feature, count = backs[0].shape[1], merge.shape[0] // 3
    columns = spans(feature, 2 * CHUNK if feature % CHUNK == 0 else feature)
    vmem = pl.BlockSpec(memory_space=pltpu.VMEM)
    hbm = pl.BlockSpec(memory_space=pltpu.HBM)
    shape = (count, feature)
    return pl.pallas_call(
        functools.partial(combine_kernel, columns, len(backs)),
        out_shape=(jax.ShapeDtypeStruct(shape, BF16),) * 2,
        in_specs=[vmem] * (len(backs) + 1),
        out_specs=(hbm, hbm),
        scratch_shapes=[
            pltpu.VMEM(shape, BF16),
            pltpu.VMEM(shape, BF16),
            pltpu.SemaphoreType.DMA((2 * len(columns),)),
        ],
        compiler_params=params(),
        name="combine",
    )(*backs, merge)


def swapped(array, axis, distance):
    return lax.ppermute(array, axis, [(i, i ^ distance) for i in range(lax.axis_size(axis))])


def over_experts(arrays, experts):
    if len(arrays) == 1:
        array = arrays[0]
        blocks = array.reshape(experts, -1, array.shape[1])
        moved = lax.all_to_all(blocks, "expert", split_axis=0, concat_axis=0, tiled=True)
        return [moved.reshape(array.shape)]
    moved = [swapped(arrays[i], "expert", distance(i, experts)) for i in range(1, experts)]
    return [arrays[0]] + moved


def shards(
    tokens,
    out_grad,
    gate_weights,
    expert_ids,
    replica_plan,
    cap_blocks,
    gate_weight,
    up_weight,
    down_weight,
):
    experts = lax.axis_size("expert")
    hosts = replica_plan.shape[1]
    assert tokens.shape[0] % hosts == 0 and experts % GROUP == 0
    assert all(n >= 4 and n & (n - 1) == 0 for n in (experts, lax.axis_size("dp")))
    slots = OWN + SPARE * (hosts - 1)
    block = -(-2 * slots // 8) * 8
    pieces = experts if experts <= GROUP else 1
    gate, up, down = gate_weight[0], up_weight[0], down_weight[0]
    sends, (scaled, pick) = dispatch(
        replica_plan,
        cap_blocks,
        expert_ids.T,
        gate_weights.T,
        tokens,
        out_grad,
        experts,
        slots,
        block,
        pieces,
    )
    recvs = over_experts(sends, experts)
    *weights, merge = load_weights(gate, up, down, scaled, pick)
    feature, width = gate.shape
    tile, big = GROUP * slots, GROUP * block
    steps, total, half = experts // GROUP, experts * slots, 3 * width // 2
    layout = (GROUP, slots, block, pieces)
    flops = 3 * total * feature * width
    scratch = [pltpu.VMEM((big, feature), F32), pltpu.VMEM((2, tile, feature), F32)]
    rows, cots, give = by_rows(
        functools.partial(give_kernel, *layout),
        "give",
        steps,
        recvs,
        weights,
        [((total, feature), BF16), ((total, feature), BF16), ((total, half), BF16)],
        scratch,
        flops,
    )
    got = swapped(give, "dp", 1)
    keep = by_rows(
        keep_kernel, "keep", steps, [rows, cots], weights, [((total, half), BF16)], (), flops
    )
    near = by_rows(add_kernel, "add", steps, [keep, got], [], [((total, half), BF16)])
    step, last = 2, lax.axis_size("dp") // 2
    while step < last:
        far = swapped(near, "dp", step)
        near = by_rows(add_kernel, "add", steps, [near, far], [], [((total, half), BF16)])
        step *= 2
    far = swapped(near, "dp", last)
    mine = by_rows(activate_kernel, "activate", steps, [near, far], [], [((total, half), BF16)])
    theirs = swapped(mine, "dp", 1)
    outs, ins = by_rows(
        own_kernel, "own", steps, [mine], weights, [((total, feature), F32)] * 2, (), flops
    )
    backs = by_rows(
        functools.partial(back_kernel, *layout),
        "back",
        steps,
        [theirs, outs, ins],
        weights,
        [((experts * block // pieces, feature), BF16)] * pieces,
        scratch[::-1],
        flops,
    )
    returned = over_experts(backs if pieces > 1 else [backs], experts)
    gate_grad, up_grad, down_grad = weight_grads(rows, cots, mine, theirs)
    mixed, token_grad = combine(returned, merge)
    return mixed, token_grad, gate_grad[None], up_grad[None], down_grad[None]


def solution(mesh):
    return jax.shard_map(
        shards,
        mesh=mesh,
        in_specs=(
            P(("groups", "expert"), "dp"),
            P(("groups", "expert"), "dp"),
            P(("groups", "expert"), None),
            P(("groups", "expert"), None),
            P("groups", None),
            P("groups"),
            P("expert", "dp", None),
            P("expert", "dp", None),
            P("expert", None, "dp"),
        ),
        out_specs=(
            P(("groups", "expert"), "dp"),
            P(("groups", "expert"), "dp"),
            P(("groups", "expert"), "dp", None),
            P(("groups", "expert"), "dp", None),
            P(("groups", "expert"), None, "dp"),
        ),
        check_vma=False,
    )
```

```python
import functools

import jax
import jax.numpy as jnp
from jax import lax
from jax.experimental import pallas as pl
from jax.experimental.pallas import tpu as pltpu
from jax.sharding import PartitionSpec as P

BLK = 4
MAXB = 2
SPARE = 2
OWN = BLK * MAXB
GROUP = 4
CHUNK = 128
LOADS = 4
VMEM_LIMIT = 32 * 1024 * 1024

BF16 = jnp.bfloat16
F32 = jnp.float32
I32 = jnp.int32


def matmul(left, right, left_dim, right_dim):
    return lax.dot_general(
        left, right, (((left_dim,), (right_dim,)), ((), ())), preferred_element_type=F32
    )


def params():
    return pltpu.CompilerParams(vmem_limit_bytes=VMEM_LIMIT)


def in_hbm(array):
    return pltpu.with_memory_space_constraint(array, pltpu.HBM)


def spans(extent, size):
    return [(start, min(size, extent - start)) for start in range(0, extent, size)]


def padded(rows):
    return -(-rows // 8) * 8


def distance(index, experts):
    return (experts - index) % experts


def dispatch_kernel(experts, hosts, slots, chunks, pieces, *refs):
    plan_hbm, caps_hbm, ids_hbm, gates_hbm, tok_hbm, grad_hbm = refs[:6]
    send_refs = refs[6 : 6 + pieces]
    scaled_ref, pick_ref, plan_ref, caps_ref, ids_ref, gates_ref, both_ref, wide, sems = refs[6 + pieces :]
    choose, count = ids_ref.shape
    block = padded(2 * slots)
    pairs = [(ids_hbm, ids_ref), (plan_hbm, plan_ref), (caps_hbm, caps_ref), (gates_hbm, gates_ref)]
    for place, source in enumerate((tok_hbm, grad_hbm)):
        for start, size in spans(count, count // LOADS):
            target = both_ref.at[pl.ds(place * count + start, size)]
            pairs.append((source.at[pl.ds(start, size)], target))
    copies = [
        pltpu.make_async_copy(source, target, sems.at[i])
        for i, (source, target) in enumerate(pairs)
    ]
    for copy in copies:
        copy.start()
    me = lax.axis_index("expert")
    row = lax.broadcasted_iota(I32, (block, count), 0)
    col = lax.broadcasted_iota(I32, (block, count), 1)
    is_cot = row >= slots
    slot = jnp.where(is_cot, row - slots, row)
    valid = row < 2 * slots
    is_spare = slot >= OWN
    spare_slot = jnp.maximum(slot - OWN, 0)
    replica = jnp.where(is_spare, 1 + lax.div(spare_slot, SPARE), 0)
    position = jnp.where(is_spare, lax.rem(spare_slot, SPARE), slot)
    token_slot = lax.rem(col, hosts)
    earlier = (
        lax.broadcasted_iota(I32, (count, count), 0) < lax.broadcasted_iota(I32, (count, count), 1)
    )
    earlier = earlier.astype(F32).astype(BF16)
    cots = jnp.concatenate([is_cot.astype(F32)] * experts, axis=0)
    for copy in copies[:4]:
        copy.wait()
    members, weights, limits = [], [], []
    for index in range(experts):
        expert = index if pieces == 1 else me ^ distance(index, experts)
        hot = (plan_ref[0, 0] == expert) | (plan_ref[1, 0] == expert)
        wanted = token_slot * hot.astype(I32)
        here = jnp.zeros((1, count), F32)
        weight = jnp.zeros((1, count), F32)
        for k in range(choose):
            chosen = ids_ref[k : k + 1, :] == expert
            here = jnp.where(chosen, 1.0, here)
            weight = jnp.where(chosen, gates_ref[k : k + 1, :], weight)
        fits = valid & (replica == wanted)
        members.append(jnp.where(fits, jnp.broadcast_to(here, fits.shape), 0.0))
        weights.append(jnp.broadcast_to(weight, fits.shape))
        room = jnp.where(is_spare, SPARE, caps_ref[expert] * BLK)
        limits.append(jnp.where(position < room, position, -1))
    member = jnp.concatenate(members, axis=0)
    weight = jnp.concatenate(weights, axis=0)
    limit = jnp.concatenate(limits, axis=0).astype(F32)
    before = matmul(member.astype(BF16), earlier, 1, 0)
    taken = jnp.where(before == limit, member, 0.0)
    pick_cot = taken * cots
    pick_tok = taken - pick_cot
    picks = jnp.concatenate([pick_tok.astype(BF16), pick_cot.astype(BF16)], axis=1)
    gate = jnp.sum(pick_cot * weight, axis=1, keepdims=True)
    scale = jnp.where(cots[:, :1] > 0.0, gate, 1.0)
    scaled_ref[...] = pick_tok * weight
    pick_ref[...] = pick_cot
    for copy in copies[4:]:
        copy.wait()
    send = scale * matmul(picks, both_ref[...], 1, 0)
    if pieces == 1:
        send_refs[0][...] = send.astype(BF16)
        return
    width = send.shape[1] // chunks
    for i, send_ref in enumerate(send_refs):
        for j in range(chunks):
            rows = send[i * block : i * block + 2 * slots, j * width : (j + 1) * width]
            wide[2 * slots * j : 2 * slots * (j + 1), :] = rows
        send_ref[...] = wide[...].astype(BF16)


def dispatch(plan, caps, ids, gates, tokens, grads, experts, slots, chunks, pieces):
    count, feature = tokens.shape
    vmem = pl.BlockSpec(memory_space=pltpu.VMEM)
    block = padded(2 * slots)
    sent = (experts * block, feature) if pieces == 1 else (2 * slots * chunks, feature // chunks)
    outs = pl.pallas_call(
        functools.partial(dispatch_kernel, experts, plan.shape[1], slots, chunks, pieces),
        out_shape=(jax.ShapeDtypeStruct(sent, BF16),) * pieces
        + (jax.ShapeDtypeStruct((experts * block, count), F32),) * 2,
        in_specs=[pl.BlockSpec(memory_space=pltpu.HBM)] * 6,
        out_specs=(vmem,) * (pieces + 2),
        scratch_shapes=[
            pltpu.SMEM(plan.shape, I32),
            pltpu.SMEM(caps.shape, I32),
            pltpu.VMEM(ids.shape, I32),
            pltpu.VMEM(gates.shape, F32),
            pltpu.VMEM((2 * count, feature), BF16),
            pltpu.VMEM((2 * slots * chunks, feature // chunks), F32),
            pltpu.SemaphoreType.DMA((4 + 2 * LOADS,)),
        ],
        compiler_params=params(),
        name="dispatch",
    )(*(in_hbm(array) for array in (plan, caps, ids, gates, tokens, grads)))
    return outs[:pieces], outs[pieces:]


def load_kernel(
    gate_hbm, up_hbm, down_hbm, scaled_ref, pick_ref, gate_ref, up_ref, down_ref, merge_ref, sems
):
    copies = []
    for source, target in ((gate_hbm, gate_ref), (up_hbm, up_ref), (down_hbm, down_ref)):
        for start, size in spans(source.shape[0], source.shape[0] // LOADS):
            rows = pl.ds(start, size)
            copies.append(
                pltpu.make_async_copy(source.at[rows], target.at[rows], sems.at[len(copies)])
            )
    for copy in copies:
        copy.start()
    scaled = scaled_ref[...].T
    count = scaled.shape[0]
    high = scaled.astype(BF16)
    merge_ref[:count, :] = high
    merge_ref[count : 2 * count, :] = (scaled - high.astype(F32)).astype(BF16)
    merge_ref[2 * count :, :] = pick_ref[...].T.astype(BF16)
    for copy in copies:
        copy.wait()


def load_weights(gate, up, down, scaled, pick):
    hbm = pl.BlockSpec(memory_space=pltpu.HBM)
    vmem = pl.BlockSpec(memory_space=pltpu.VMEM)
    assert all(w.shape[0] % (16 * LOADS) == 0 for w in (gate, up, down))
    merge = jax.ShapeDtypeStruct((3 * pick.shape[1], pick.shape[0]), BF16)
    return pl.pallas_call(
        load_kernel,
        out_shape=tuple(pltpu.VMEM(w.shape, BF16) for w in (gate, up, down)) + (merge,),
        in_specs=[hbm, hbm, hbm, vmem, vmem],
        out_specs=(vmem,) * 4,
        scratch_shapes=[pltpu.SemaphoreType.DMA((3 * LOADS,))],
        compiler_params=params(),
        cost_estimate=pl.CostEstimate(
            flops=0, bytes_accessed=2 * 3 * gate.size * 2, transcendentals=0
        ),
        name="load_weights",
    )(in_hbm(gate), in_hbm(up), in_hbm(down), scaled, pick)


def half_columns(which, width):
    half = width // 2
    side = lax.rem(lax.axis_index("dp") + which, 2)
    return pl.ds(pl.multiple_of(side * half, half), half)


def half_partials(which, rows, cots, gate_ref, up_ref, down_ref, part_ref):
    width = gate_ref.shape[1]
    half = width // 2
    units = half_columns(which, width)
    part_ref[:, :half] = matmul(rows, gate_ref[:, units], 1, 0).astype(BF16)
    part_ref[:, half : 2 * half] = matmul(rows, up_ref[:, units], 1, 0).astype(BF16)
    part_ref[:, 2 * half :] = matmul(cots, down_ref[units, :], 1, 1).astype(BF16)


def give_kernel(slots, chunks, pieces, *refs):
    recv_refs = refs[:pieces]
    gate_ref, up_ref, down_ref, rows_ref, cots_ref, give_ref, wide, flat = refs[pieces:]
    group, block, width = wide.shape
    for s in range(group):
        recv_ref, start = (recv_refs[0], s * block) if pieces == 1 else (recv_refs[s], 0)
        wide[s] = recv_ref[start : start + block, :].astype(F32)
        for j in range(chunks):
            columns = pl.ds(j * width, width)
            for kind in range(2):
                place = (2 * j + kind) * slots
                flat[kind, s * slots : (s + 1) * slots, columns] = wide[s, place : place + slots, :]
    rows = flat[0].astype(BF16)
    cots = flat[1].astype(BF16)
    rows_ref[...] = rows
    cots_ref[...] = cots
    half_partials(1, rows, cots, gate_ref, up_ref, down_ref, give_ref)


def keep_kernel(rows_ref, cots_ref, gate_ref, up_ref, down_ref, keep_ref):
    half_partials(0, rows_ref[...], cots_ref[...], gate_ref, up_ref, down_ref, keep_ref)


def add_kernel(left_ref, right_ref, sum_ref):
    sum_ref[...] = (left_ref[...].astype(F32) + right_ref[...].astype(F32)).astype(BF16)


def activate_kernel(near_ref, far_ref, mine_ref):
    half = mine_ref.shape[1] // 3
    total = near_ref[...].astype(F32) + far_ref[...].astype(F32)
    gate_pre, up_pre, hidden_grad = (total[:, i * half : (i + 1) * half] for i in range(3))
    sigma = jax.nn.sigmoid(gate_pre)
    active = gate_pre * sigma
    slope = sigma * (1.0 + gate_pre * (1.0 - sigma))
    mine_ref[:, :half] = (active * up_pre).astype(BF16)
    mine_ref[:, half : 2 * half] = (hidden_grad * up_pre * slope).astype(BF16)
    mine_ref[:, 2 * half :] = (hidden_grad * active).astype(BF16)


def half_outputs(which, acts_ref, gate_ref, up_ref, down_ref):
    width = gate_ref.shape[1]
    half = width // 2
    units = half_columns(which, width)
    outs = matmul(acts_ref[:, :half], down_ref[units, :], 1, 0)
    ins = matmul(acts_ref[:, half : 2 * half], gate_ref[:, units], 1, 1)
    return outs, ins + matmul(acts_ref[:, 2 * half :], up_ref[:, units], 1, 1)


def own_kernel(mine_ref, gate_ref, up_ref, down_ref, outs_ref, ins_ref):
    outs_ref[...], ins_ref[...] = half_outputs(0, mine_ref, gate_ref, up_ref, down_ref)


def back_kernel(slots, chunks, pieces, *refs):
    theirs_ref, outs_ref, ins_ref, gate_ref, up_ref, down_ref = refs[:6]
    back_refs = refs[6 : 6 + pieces]
    flat, wide = refs[6 + pieces :]
    group, block, width = wide.shape
    outs, ins = half_outputs(1, theirs_ref, gate_ref, up_ref, down_ref)
    flat[0] = outs_ref[...] + outs
    flat[1] = ins_ref[...] + ins
    if block > 2 * slots * chunks:
        wide[...] = jnp.zeros_like(wide)
    for s in range(group):
        for j in range(chunks):
            columns = pl.ds(j * width, width)
            for kind in range(2):
                place = (2 * j + kind) * slots
                wide[s, place : place + slots, :] = flat[kind, s * slots : (s + 1) * slots, columns]
        back_ref, start = (back_refs[0], s * block) if pieces == 1 else (back_refs[s], 0)
        back_ref[start : start + block, :] = wide[s].astype(BF16)


def by_rows(kernel, name, steps, arrays, weights, outs, scratch=(), flops=0):
    def tiled(shape):
        return pl.BlockSpec((shape[0] // steps, shape[1]), lambda i: (i, 0))

    def whole(shape):
        return pl.BlockSpec(shape, lambda i: (0, 0))

    moved = sum(array.size * array.dtype.itemsize for array in (*arrays, *weights))
    results = pl.pallas_call(
        kernel,
        grid=(steps,),
        out_shape=tuple(jax.ShapeDtypeStruct(shape, dtype) for shape, dtype in outs),
        in_specs=[tiled(array.shape) for array in arrays] + [whole(w.shape) for w in weights],
        out_specs=tuple(tiled(shape) for shape, _ in outs),
        scratch_shapes=list(scratch),
        compiler_params=params(),
        cost_estimate=pl.CostEstimate(flops=flops, bytes_accessed=moved, transcendentals=0),
        name=name,
    )(*arrays, *weights)
    return results if len(outs) > 1 else results[0]


def grads_kernel(
    rows_ref, cots_ref, mine_ref, theirs_ref, gate_hbm, up_hbm, down_hbm, gate_ref, up_ref, down_ref, sems
):
    width = gate_ref.shape[1]
    half = width // 2
    copies = []

    def send(source, target, rows):
        copies.append(
            pltpu.make_async_copy(source.at[rows], target.at[rows], sems.at[len(copies)])
        )
        copies[-1].start()

    sides = [(mine_ref, half_columns(0, width)), (theirs_ref, half_columns(1, width))]
    for acts_ref, units in sides:
        for start, size in spans(half, CHUNK):
            rows = pl.ds(pl.multiple_of(units.start + start, 16), size)
            hidden = acts_ref[:, start : start + size]
            down_ref[rows, :] = matmul(hidden, cots_ref[...], 0, 0).astype(BF16)
            send(down_ref, down_hbm, rows)
    for place, out_ref, out_hbm in ((1, gate_ref, gate_hbm), (2, up_ref, up_hbm)):
        for start, size in spans(out_ref.shape[0], CHUNK):
            rows = pl.ds(start, size)
            for acts_ref, units in sides:
                grad = acts_ref[:, place * half : (place + 1) * half]
                out_ref[rows, units] = matmul(rows_ref[:, rows], grad, 0, 0).astype(BF16)
            send(out_ref, out_hbm, rows)
    for copy in copies:
        copy.wait()


def weight_grads(rows, cots, mine, theirs):
    total, feature = rows.shape
    width = 2 * mine.shape[1] // 3
    vmem = pl.BlockSpec(memory_space=pltpu.VMEM)
    hbm = pl.BlockSpec(memory_space=pltpu.HBM)
    shapes = ((feature, width), (feature, width), (width, feature))
    pieces = 2 * len(spans(feature, CHUNK)) + 2 * len(spans(width // 2, CHUNK))
    return pl.pallas_call(
        grads_kernel,
        out_shape=tuple(jax.ShapeDtypeStruct(shape, BF16) for shape in shapes),
        in_specs=[vmem] * 4,
        out_specs=(hbm,) * 3,
        scratch_shapes=[pltpu.VMEM(shape, BF16) for shape in shapes]
        + [pltpu.SemaphoreType.DMA((pieces,))],
        compiler_params=params(),
        cost_estimate=pl.CostEstimate(
            flops=6 * total * feature * width,
            bytes_accessed=6 * feature * width,
            transcendentals=0,
        ),
        name="weight_grads",
    )(rows, cots, mine, theirs)


def combine_kernel(columns, slots, chunks, pieces, *refs):
    back_refs = refs[:pieces]
    merge_ref, mixed_hbm, token_hbm, mixed_ref, token_ref, wide, flat, sems = refs[pieces:]
    if pieces > 1:
        flat[...] = jnp.zeros_like(flat)
        rows, width, block = 2 * slots, back_refs[0].shape[1], padded(2 * slots)
        for i, back_ref in enumerate(back_refs):
            wide[i] = back_ref[...].astype(F32)
            for j in range(chunks):
                part = pl.ds(j * width, width)
                flat[i * block : i * block + rows, part] = wide[i, j * rows : (j + 1) * rows, :]
    count = mixed_ref.shape[0]
    copies = []
    for start, size in columns:
        part = pl.ds(start, size)
        back = back_refs[0][:, part] if pieces == 1 else flat[:, part].astype(BF16)
        sums = matmul(merge_ref[...], back, 1, 0)
        mixed_ref[:, part] = (sums[:count] + sums[count : 2 * count]).astype(BF16)
        token_ref[:, part] = sums[2 * count :].astype(BF16)
        for source, target in ((mixed_ref, mixed_hbm), (token_ref, token_hbm)):
            copies.append(
                pltpu.make_async_copy(
                    source.at[:, part], target.at[:, part], sems.at[len(copies)]
                )
            )
            copies[-1].start()
    for copy in copies:
        copy.wait()


def combine(backs, merge, slots, chunks):
    pieces, feature, count = len(backs), chunks * backs[0].shape[1], merge.shape[0] // 3
    columns = spans(feature, 2 * CHUNK if feature % CHUNK == 0 else feature)
    vmem = pl.BlockSpec(memory_space=pltpu.VMEM)
    hbm = pl.BlockSpec(memory_space=pltpu.HBM)
    shape = (count, feature)
    staged = [(pieces, *backs[0].shape), (merge.shape[1], feature)] if pieces > 1 else [(8, 128)] * 2
    return pl.pallas_call(
        functools.partial(combine_kernel, columns, slots, chunks, pieces),
        out_shape=(jax.ShapeDtypeStruct(shape, BF16),) * 2,
        in_specs=[vmem] * (pieces + 1),
        out_specs=(hbm, hbm),
        scratch_shapes=[
            pltpu.VMEM(shape, BF16),
            pltpu.VMEM(shape, BF16),
            *(pltpu.VMEM(extent, F32) for extent in staged),
            pltpu.SemaphoreType.DMA((2 * len(columns),)),
        ],
        compiler_params=params(),
        name="combine",
    )(*backs, merge)


def swapped(array, axis, distance):
    return lax.ppermute(array, axis, [(i, i ^ distance) for i in range(lax.axis_size(axis))])


def over_experts(arrays, experts):
    if len(arrays) == 1:
        array = arrays[0]
        blocks = array.reshape(experts, -1, array.shape[1])
        moved = lax.all_to_all(blocks, "expert", split_axis=0, concat_axis=0, tiled=True)
        return [moved.reshape(array.shape)]
    moved = [swapped(arrays[i], "expert", distance(i, experts)) for i in range(1, experts)]
    return [arrays[0]] + moved


def shards(
    tokens,
    out_grad,
    gate_weights,
    expert_ids,
    replica_plan,
    cap_blocks,
    gate_weight,
    up_weight,
    down_weight,
):
    experts = lax.axis_size("expert")
    hosts = replica_plan.shape[1]
    assert tokens.shape[0] % hosts == 0 and experts % GROUP == 0
    assert all(n >= 4 and n & (n - 1) == 0 for n in (experts, lax.axis_size("dp")))
    slots = OWN + SPARE * (hosts - 1)
    gate, up, down = gate_weight[0], up_weight[0], down_weight[0]
    feature, width = gate.shape
    pieces = experts if experts <= GROUP and feature % CHUNK == 0 else 1
    chunks = feature // CHUNK if pieces > 1 else 1
    block = 2 * slots * chunks if pieces > 1 else padded(2 * slots)
    sends, (scaled, pick) = dispatch(
        replica_plan,
        cap_blocks,
        expert_ids.T,
        gate_weights.T,
        tokens,
        out_grad,
        experts,
        slots,
        chunks,
        pieces,
    )
    recvs = over_experts(sends, experts)
    *weights, merge = load_weights(gate, up, down, scaled, pick)
    steps, total, half = experts // GROUP, experts * slots, 3 * width // 2
    layout = (slots, chunks, pieces)
    flops = 3 * total * feature * width
    scratch = [
        pltpu.VMEM((GROUP, block, feature // chunks), F32),
        pltpu.VMEM((2, GROUP * slots, feature), F32),
    ]
    rows, cots, give = by_rows(
        functools.partial(give_kernel, *layout),
        "give",
        steps,
        recvs,
        weights,
        [((total, feature), BF16), ((total, feature), BF16), ((total, half), BF16)],
        scratch,
        flops,
    )
    got = swapped(give, "dp", 1)
    keep = by_rows(
        keep_kernel, "keep", steps, [rows, cots], weights, [((total, half), BF16)], (), flops
    )
    near = by_rows(add_kernel, "add", steps, [keep, got], [], [((total, half), BF16)])
    step, last = 2, lax.axis_size("dp") // 2
    while step < last:
        far = swapped(near, "dp", step)
        near = by_rows(add_kernel, "add", steps, [near, far], [], [((total, half), BF16)])
        step *= 2
    far = swapped(near, "dp", last)
    mine = by_rows(activate_kernel, "activate", steps, [near, far], [], [((total, half), BF16)])
    theirs = swapped(mine, "dp", 1)
    outs, ins = by_rows(
        own_kernel, "own", steps, [mine], weights, [((total, feature), F32)] * 2, (), flops
    )
    backs = by_rows(
        functools.partial(back_kernel, *layout),
        "back",
        steps,
        [theirs, outs, ins],
        weights,
        [((experts * block // pieces, feature // chunks), BF16)] * pieces,
        scratch[::-1],
        flops,
    )
    returned = over_experts(backs if pieces > 1 else [backs], experts)
    gate_grad, up_grad, down_grad = weight_grads(rows, cots, mine, theirs)
    mixed, token_grad = combine(returned, merge, slots, chunks)
    return mixed, token_grad, gate_grad[None], up_grad[None], down_grad[None]


def solution(mesh):
    return jax.shard_map(
        shards,
        mesh=mesh,
        in_specs=(
            P(("groups", "expert"), "dp"),
            P(("groups", "expert"), "dp"),
            P(("groups", "expert"), None),
            P(("groups", "expert"), None),
            P("groups", None),
            P("groups"),
            P("expert", "dp", None),
            P("expert", "dp", None),
            P("expert", None, "dp"),
        ),
        out_specs=(
            P(("groups", "expert"), "dp"),
            P(("groups", "expert"), "dp"),
            P(("groups", "expert"), "dp", None),
            P(("groups", "expert"), "dp", None),
            P(("groups", "expert"), None, "dp"),
        ),
        check_vma=False,
    )
```

```python
import functools

import jax
import jax.numpy as jnp
from jax import lax
from jax.experimental import pallas as pl
from jax.experimental.pallas import tpu as pltpu
from jax.sharding import PartitionSpec as P

BLK = 4
MAXB = 2
SPARE = 2
OWN = BLK * MAXB
GROUP = 4
CHUNK = 128
LOADS = 4
COST_F = 4_000_000_000
COST_B = 12_000_000
VMEM_LIMIT = 32 * 1024 * 1024

BF16 = jnp.bfloat16
F32 = jnp.float32
I32 = jnp.int32


def matmul(left, right, left_dim, right_dim):
    return lax.dot_general(
        left, right, (((left_dim,), (right_dim,)), ((), ())), preferred_element_type=F32
    )


def params():
    return pltpu.CompilerParams(vmem_limit_bytes=VMEM_LIMIT)


def in_hbm(array):
    return pltpu.with_memory_space_constraint(array, pltpu.HBM)


def spans(extent, size):
    return [(start, min(size, extent - start)) for start in range(0, extent, size)]


def padded(rows):
    return -(-rows // 8) * 8


def distance(index, experts):
    return (experts - index) % experts


def dispatch_kernel(experts, hosts, slots, chunks, pieces, *refs):
    plan_hbm, caps_hbm, ids_hbm, gates_hbm, tok_hbm, grad_hbm = refs[:6]
    send_refs = refs[6 : 6 + pieces]
    scaled_ref, pick_ref, plan_ref, caps_ref, ids_ref, gates_ref, both_ref, wide, sems = refs[6 + pieces :]
    choose, count = ids_ref.shape
    block = padded(2 * slots)
    pairs = [(ids_hbm, ids_ref), (plan_hbm, plan_ref), (caps_hbm, caps_ref), (gates_hbm, gates_ref)]
    for place, source in enumerate((tok_hbm, grad_hbm)):
        for start, size in spans(count, count // LOADS):
            target = both_ref.at[pl.ds(place * count + start, size)]
            pairs.append((source.at[pl.ds(start, size)], target))
    copies = [
        pltpu.make_async_copy(source, target, sems.at[i])
        for i, (source, target) in enumerate(pairs)
    ]
    for copy in copies:
        copy.start()
    me = lax.axis_index("expert")
    row = lax.broadcasted_iota(I32, (block, count), 0)
    col = lax.broadcasted_iota(I32, (block, count), 1)
    is_cot = row >= slots
    slot = jnp.where(is_cot, row - slots, row)
    valid = row < 2 * slots
    is_spare = slot >= OWN
    spare_slot = jnp.maximum(slot - OWN, 0)
    replica = jnp.where(is_spare, 1 + lax.div(spare_slot, SPARE), 0)
    position = jnp.where(is_spare, lax.rem(spare_slot, SPARE), slot)
    token_slot = lax.rem(col, hosts)
    earlier = (
        lax.broadcasted_iota(I32, (count, count), 0) < lax.broadcasted_iota(I32, (count, count), 1)
    )
    earlier = earlier.astype(F32).astype(BF16)
    cots = jnp.concatenate([is_cot.astype(F32)] * experts, axis=0)
    for copy in copies[:4]:
        copy.wait()
    members, weights, limits = [], [], []
    for index in range(experts):
        expert = index if pieces == 1 else me ^ distance(index, experts)
        hot = (plan_ref[0, 0] == expert) | (plan_ref[1, 0] == expert)
        wanted = token_slot * hot.astype(I32)
        here = jnp.zeros((1, count), F32)
        weight = jnp.zeros((1, count), F32)
        for k in range(choose):
            chosen = ids_ref[k : k + 1, :] == expert
            here = jnp.where(chosen, 1.0, here)
            weight = jnp.where(chosen, gates_ref[k : k + 1, :], weight)
        fits = valid & (replica == wanted)
        members.append(jnp.where(fits, jnp.broadcast_to(here, fits.shape), 0.0))
        weights.append(jnp.broadcast_to(weight, fits.shape))
        room = jnp.where(is_spare, SPARE, caps_ref[expert] * BLK)
        limits.append(jnp.where(position < room, position, -1))
    member = jnp.concatenate(members, axis=0)
    weight = jnp.concatenate(weights, axis=0)
    limit = jnp.concatenate(limits, axis=0).astype(F32)
    before = matmul(member.astype(BF16), earlier, 1, 0)
    taken = jnp.where(before == limit, member, 0.0)
    pick_cot = taken * cots
    pick_tok = taken - pick_cot
    picks = jnp.concatenate([pick_tok.astype(BF16), pick_cot.astype(BF16)], axis=1)
    gate = jnp.sum(pick_cot * weight, axis=1, keepdims=True)
    scale = jnp.where(cots[:, :1] > 0.0, gate, 1.0)
    scaled_ref[...] = pick_tok * weight
    pick_ref[...] = pick_cot
    for copy in copies[4:]:
        copy.wait()
    send = scale * matmul(picks, both_ref[...], 1, 0)
    if pieces == 1:
        send_refs[0][...] = send.astype(BF16)
        return
    width = send.shape[1] // chunks
    for i, send_ref in enumerate(send_refs):
        for j in range(chunks):
            rows = send[i * block : i * block + 2 * slots, j * width : (j + 1) * width]
            wide[2 * slots * j : 2 * slots * (j + 1), :] = rows
        send_ref[...] = wide[...].astype(BF16)


def dispatch(plan, caps, ids, gates, tokens, grads, experts, slots, chunks, pieces):
    count, feature = tokens.shape
    vmem = pl.BlockSpec(memory_space=pltpu.VMEM)
    block = padded(2 * slots)
    sent = (experts * block, feature) if pieces == 1 else (2 * slots * chunks, feature // chunks)
    outs = pl.pallas_call(
        functools.partial(dispatch_kernel, experts, plan.shape[1], slots, chunks, pieces),
        out_shape=(jax.ShapeDtypeStruct(sent, BF16),) * pieces
        + (jax.ShapeDtypeStruct((experts * block, count), F32),) * 2,
        in_specs=[pl.BlockSpec(memory_space=pltpu.HBM)] * 6,
        out_specs=(vmem,) * (pieces + 2),
        scratch_shapes=[
            pltpu.SMEM(plan.shape, I32),
            pltpu.SMEM(caps.shape, I32),
            pltpu.VMEM(ids.shape, I32),
            pltpu.VMEM(gates.shape, F32),
            pltpu.VMEM((2 * count, feature), BF16),
            pltpu.VMEM((2 * slots * chunks, feature // chunks), F32),
            pltpu.SemaphoreType.DMA((4 + 2 * LOADS,)),
        ],
        compiler_params=params(),
        cost_estimate=pl.CostEstimate(flops=COST_F, bytes_accessed=COST_B, transcendentals=0),
        name="dispatch",
    )(*(in_hbm(array) for array in (plan, caps, ids, gates, tokens, grads)))
    return outs[:pieces], outs[pieces:]


def merge_kernel(scaled_ref, pick_ref, merge_ref):
    scaled = scaled_ref[...].T
    count = scaled.shape[0]
    high = scaled.astype(BF16)
    merge_ref[:count, :] = high
    merge_ref[count : 2 * count, :] = (scaled - high.astype(F32)).astype(BF16)
    merge_ref[2 * count :, :] = pick_ref[...].T.astype(BF16)


def merged(scaled, pick):
    vmem = pl.BlockSpec(memory_space=pltpu.VMEM)
    return pl.pallas_call(
        merge_kernel,
        out_shape=jax.ShapeDtypeStruct((3 * pick.shape[1], pick.shape[0]), BF16),
        in_specs=[vmem, vmem],
        out_specs=vmem,
        compiler_params=params(),
        name="merge",
    )(scaled, pick)


def half_columns(which, width):
    half = width // 2
    side = lax.rem(lax.axis_index("dp") + which, 2)
    return pl.ds(pl.multiple_of(side * half, half), half)


def half_partials(which, rows, cots, gate_ref, up_ref, down_ref, part_ref):
    width = gate_ref.shape[1]
    half = width // 2
    units = half_columns(which, width)
    part_ref[:, :half] = matmul(rows, gate_ref[:, units], 1, 0).astype(BF16)
    part_ref[:, half : 2 * half] = matmul(rows, up_ref[:, units], 1, 0).astype(BF16)
    part_ref[:, 2 * half :] = matmul(cots, down_ref[units, :], 1, 1).astype(BF16)


def give_kernel(slots, chunks, pieces, *refs):
    recv_refs = refs[:pieces]
    gate_ref, up_ref, down_ref, rows_ref, cots_ref, give_ref, wide, flat = refs[pieces:]
    group, block, width = wide.shape
    for s in range(group):
        recv_ref, start = (recv_refs[0], s * block) if pieces == 1 else (recv_refs[s], 0)
        wide[s] = recv_ref[start : start + block, :].astype(F32)
        for j in range(chunks):
            columns = pl.ds(j * width, width)
            for kind in range(2):
                place = (2 * j + kind) * slots
                flat[kind, s * slots : (s + 1) * slots, columns] = wide[s, place : place + slots, :]
    rows = flat[0].astype(BF16)
    cots = flat[1].astype(BF16)
    rows_ref[...] = rows
    cots_ref[...] = cots
    half_partials(1, rows, cots, gate_ref, up_ref, down_ref, give_ref)


def keep_kernel(rows_ref, cots_ref, gate_ref, up_ref, down_ref, keep_ref):
    half_partials(0, rows_ref[...], cots_ref[...], gate_ref, up_ref, down_ref, keep_ref)


def add_kernel(left_ref, right_ref, sum_ref):
    sum_ref[...] = (left_ref[...].astype(F32) + right_ref[...].astype(F32)).astype(BF16)


def activate_kernel(near_ref, far_ref, mine_ref):
    half = mine_ref.shape[1] // 3
    total = near_ref[...].astype(F32) + far_ref[...].astype(F32)
    gate_pre, up_pre, hidden_grad = (total[:, i * half : (i + 1) * half] for i in range(3))
    sigma = jax.nn.sigmoid(gate_pre)
    active = gate_pre * sigma
    slope = sigma * (1.0 + gate_pre * (1.0 - sigma))
    mine_ref[:, :half] = (active * up_pre).astype(BF16)
    mine_ref[:, half : 2 * half] = (hidden_grad * up_pre * slope).astype(BF16)
    mine_ref[:, 2 * half :] = (hidden_grad * active).astype(BF16)


def half_outputs(which, acts_ref, gate_ref, up_ref, down_ref):
    width = gate_ref.shape[1]
    half = width // 2
    units = half_columns(which, width)
    outs = matmul(acts_ref[:, :half], down_ref[units, :], 1, 0)
    ins = matmul(acts_ref[:, half : 2 * half], gate_ref[:, units], 1, 1)
    return outs, ins + matmul(acts_ref[:, 2 * half :], up_ref[:, units], 1, 1)


def own_kernel(mine_ref, gate_ref, up_ref, down_ref, outs_ref, ins_ref):
    outs_ref[...], ins_ref[...] = half_outputs(0, mine_ref, gate_ref, up_ref, down_ref)


def back_kernel(slots, chunks, pieces, *refs):
    theirs_ref, outs_ref, ins_ref, gate_ref, up_ref, down_ref = refs[:6]
    back_refs = refs[6 : 6 + pieces]
    flat, wide = refs[6 + pieces :]
    group, block, width = wide.shape
    outs, ins = half_outputs(1, theirs_ref, gate_ref, up_ref, down_ref)
    flat[0] = outs_ref[...] + outs
    flat[1] = ins_ref[...] + ins
    if block > 2 * slots * chunks:
        wide[...] = jnp.zeros_like(wide)
    for s in range(group):
        for j in range(chunks):
            columns = pl.ds(j * width, width)
            for kind in range(2):
                place = (2 * j + kind) * slots
                wide[s, place : place + slots, :] = flat[kind, s * slots : (s + 1) * slots, columns]
        back_ref, start = (back_refs[0], s * block) if pieces == 1 else (back_refs[s], 0)
        back_ref[start : start + block, :] = wide[s].astype(BF16)


def by_rows(kernel, name, steps, arrays, weights, outs, scratch=(), flops=0):
    def tiled(shape):
        return pl.BlockSpec((shape[0] // steps, shape[1]), lambda i: (i, 0))

    def whole(shape):
        return pl.BlockSpec(shape, lambda i: (0, 0))

    moved = sum(array.size * array.dtype.itemsize for array in (*arrays, *weights))
    results = pl.pallas_call(
        kernel,
        grid=(steps,),
        out_shape=tuple(jax.ShapeDtypeStruct(shape, dtype) for shape, dtype in outs),
        in_specs=[tiled(array.shape) for array in arrays] + [whole(w.shape) for w in weights],
        out_specs=tuple(tiled(shape) for shape, _ in outs),
        scratch_shapes=list(scratch),
        compiler_params=params(),
        cost_estimate=pl.CostEstimate(flops=flops, bytes_accessed=moved, transcendentals=0),
        name=name,
    )(*arrays, *weights)
    return results if len(outs) > 1 else results[0]


def grads_kernel(
    rows_ref, cots_ref, mine_ref, theirs_ref, gate_hbm, up_hbm, down_hbm, gate_ref, up_ref, down_ref, sems
):
    width = gate_ref.shape[1]
    half = width // 2
    copies = []

    def send(source, target, rows):
        copies.append(
            pltpu.make_async_copy(source.at[rows], target.at[rows], sems.at[len(copies)])
        )
        copies[-1].start()

    sides = [(mine_ref, half_columns(0, width)), (theirs_ref, half_columns(1, width))]
    for acts_ref, units in sides:
        for start, size in spans(half, CHUNK):
            rows = pl.ds(pl.multiple_of(units.start + start, 16), size)
            hidden = acts_ref[:, start : start + size]
            down_ref[rows, :] = matmul(hidden, cots_ref[...], 0, 0).astype(BF16)
            send(down_ref, down_hbm, rows)
    for place, out_ref, out_hbm in ((1, gate_ref, gate_hbm), (2, up_ref, up_hbm)):
        for start, size in spans(out_ref.shape[0], CHUNK):
            rows = pl.ds(start, size)
            for acts_ref, units in sides:
                grad = acts_ref[:, place * half : (place + 1) * half]
                out_ref[rows, units] = matmul(rows_ref[:, rows], grad, 0, 0).astype(BF16)
            send(out_ref, out_hbm, rows)
    for copy in copies:
        copy.wait()


def weight_grads(rows, cots, mine, theirs):
    total, feature = rows.shape
    width = 2 * mine.shape[1] // 3
    vmem = pl.BlockSpec(memory_space=pltpu.VMEM)
    hbm = pl.BlockSpec(memory_space=pltpu.HBM)
    shapes = ((feature, width), (feature, width), (width, feature))
    pieces = 2 * len(spans(feature, CHUNK)) + 2 * len(spans(width // 2, CHUNK))
    return pl.pallas_call(
        grads_kernel,
        out_shape=tuple(jax.ShapeDtypeStruct(shape, BF16) for shape in shapes),
        in_specs=[vmem] * 4,
        out_specs=(hbm,) * 3,
        scratch_shapes=[pltpu.VMEM(shape, BF16) for shape in shapes]
        + [pltpu.SemaphoreType.DMA((pieces,))],
        compiler_params=params(),
        cost_estimate=pl.CostEstimate(
            flops=6 * total * feature * width,
            bytes_accessed=6 * feature * width,
            transcendentals=0,
        ),
        name="weight_grads",
    )(rows, cots, mine, theirs)


def combine_kernel(columns, slots, chunks, pieces, *refs):
    back_refs = refs[:pieces]
    merge_ref, mixed_hbm, token_hbm, mixed_ref, token_ref, wide, flat, sems = refs[pieces:]
    if pieces > 1:
        flat[...] = jnp.zeros_like(flat)
        rows, width, block = 2 * slots, back_refs[0].shape[1], padded(2 * slots)
        for i, back_ref in enumerate(back_refs):
            wide[i] = back_ref[...].astype(F32)
            for j in range(chunks):
                part = pl.ds(j * width, width)
                flat[i * block : i * block + rows, part] = wide[i, j * rows : (j + 1) * rows, :]
    count = mixed_ref.shape[0]
    copies = []
    for start, size in columns:
        part = pl.ds(start, size)
        back = back_refs[0][:, part] if pieces == 1 else flat[:, part].astype(BF16)
        sums = matmul(merge_ref[...], back, 1, 0)
        mixed_ref[:, part] = (sums[:count] + sums[count : 2 * count]).astype(BF16)
        token_ref[:, part] = sums[2 * count :].astype(BF16)
        for source, target in ((mixed_ref, mixed_hbm), (token_ref, token_hbm)):
            copies.append(
                pltpu.make_async_copy(
                    source.at[:, part], target.at[:, part], sems.at[len(copies)]
                )
            )
            copies[-1].start()
    for copy in copies:
        copy.wait()


def combine(backs, merge, slots, chunks):
    pieces, feature, count = len(backs), chunks * backs[0].shape[1], merge.shape[0] // 3
    columns = spans(feature, 2 * CHUNK if feature % CHUNK == 0 else feature)
    vmem = pl.BlockSpec(memory_space=pltpu.VMEM)
    hbm = pl.BlockSpec(memory_space=pltpu.HBM)
    shape = (count, feature)
    staged = [(pieces, *backs[0].shape), (merge.shape[1], feature)] if pieces > 1 else [(8, 128)] * 2
    return pl.pallas_call(
        functools.partial(combine_kernel, columns, slots, chunks, pieces),
        out_shape=(jax.ShapeDtypeStruct(shape, BF16),) * 2,
        in_specs=[vmem] * (pieces + 1),
        out_specs=(hbm, hbm),
        scratch_shapes=[
            pltpu.VMEM(shape, BF16),
            pltpu.VMEM(shape, BF16),
            *(pltpu.VMEM(extent, F32) for extent in staged),
            pltpu.SemaphoreType.DMA((2 * len(columns),)),
        ],
        compiler_params=params(),
        name="combine",
    )(*backs, merge)


def swapped(array, axis, distance):
    return lax.ppermute(array, axis, [(i, i ^ distance) for i in range(lax.axis_size(axis))])


def over_experts(arrays, experts):
    if len(arrays) == 1:
        array = arrays[0]
        blocks = array.reshape(experts, -1, array.shape[1])
        moved = lax.all_to_all(blocks, "expert", split_axis=0, concat_axis=0, tiled=True)
        return [moved.reshape(array.shape)]
    moved = [swapped(arrays[i], "expert", distance(i, experts)) for i in range(1, experts)]
    return [arrays[0]] + moved


def shards(
    tokens,
    out_grad,
    gate_weights,
    expert_ids,
    replica_plan,
    cap_blocks,
    gate_weight,
    up_weight,
    down_weight,
):
    experts = lax.axis_size("expert")
    hosts = replica_plan.shape[1]
    assert tokens.shape[0] % hosts == 0 and experts % GROUP == 0
    assert all(n >= 4 and n & (n - 1) == 0 for n in (experts, lax.axis_size("dp")))
    slots = OWN + SPARE * (hosts - 1)
    gate, up, down = gate_weight[0], up_weight[0], down_weight[0]
    feature, width = gate.shape
    pieces = experts if experts <= GROUP and feature % CHUNK == 0 else 1
    chunks = feature // CHUNK if pieces > 1 else 1
    block = 2 * slots * chunks if pieces > 1 else padded(2 * slots)
    sends, (scaled, pick) = dispatch(
        replica_plan,
        cap_blocks,
        expert_ids.T,
        gate_weights.T,
        tokens,
        out_grad,
        experts,
        slots,
        chunks,
        pieces,
    )
    recvs = over_experts(sends, experts)
    weights = (gate, up, down)
    merge = merged(scaled, pick)
    steps, total, half = experts // GROUP, experts * slots, 3 * width // 2
    layout = (slots, chunks, pieces)
    flops = 3 * total * feature * width
    scratch = [
        pltpu.VMEM((GROUP, block, feature // chunks), F32),
        pltpu.VMEM((2, GROUP * slots, feature), F32),
    ]
    rows, cots, give = by_rows(
        functools.partial(give_kernel, *layout),
        "give",
        steps,
        recvs,
        weights,
        [((total, feature), BF16), ((total, feature), BF16), ((total, half), BF16)],
        scratch,
        flops,
    )
    got = swapped(give, "dp", 1)
    keep = by_rows(
        keep_kernel, "keep", steps, [rows, cots], weights, [((total, half), BF16)], (), flops
    )
    near = by_rows(add_kernel, "add", steps, [keep, got], [], [((total, half), BF16)])
    step, last = 2, lax.axis_size("dp") // 2
    while step < last:
        far = swapped(near, "dp", step)
        near = by_rows(add_kernel, "add", steps, [near, far], [], [((total, half), BF16)])
        step *= 2
    far = swapped(near, "dp", last)
    mine = by_rows(activate_kernel, "activate", steps, [near, far], [], [((total, half), BF16)])
    theirs = swapped(mine, "dp", 1)
    outs, ins = by_rows(
        own_kernel, "own", steps, [mine], weights, [((total, feature), F32)] * 2, (), flops
    )
    backs = by_rows(
        functools.partial(back_kernel, *layout),
        "back",
        steps,
        [theirs, outs, ins],
        weights,
        [((experts * block // pieces, feature // chunks), BF16)] * pieces,
        scratch[::-1],
        flops,
    )
    returned = over_experts(backs if pieces > 1 else [backs], experts)
    gate_grad, up_grad, down_grad = weight_grads(rows, cots, mine, theirs)
    mixed, token_grad = combine(returned, merge, slots, chunks)
    return mixed, token_grad, gate_grad[None], up_grad[None], down_grad[None]


def solution(mesh):
    return jax.shard_map(
        shards,
        mesh=mesh,
        in_specs=(
            P(("groups", "expert"), "dp"),
            P(("groups", "expert"), "dp"),
            P(("groups", "expert"), None),
            P(("groups", "expert"), None),
            P("groups", None),
            P("groups"),
            P("expert", "dp", None),
            P("expert", "dp", None),
            P("expert", None, "dp"),
        ),
        out_specs=(
            P(("groups", "expert"), "dp"),
            P(("groups", "expert"), "dp"),
            P(("groups", "expert"), "dp", None),
            P(("groups", "expert"), "dp", None),
            P(("groups", "expert"), None, "dp"),
        ),
        check_vma=False,
    )
```

```python
import functools

import jax
import jax.numpy as jnp
from jax import lax
from jax.experimental import pallas as pl
from jax.experimental.pallas import tpu as pltpu
from jax.sharding import PartitionSpec as P

BLK = 4
MAXB = 2
SPARE = 2
OWN = BLK * MAXB
GROUP = 4
CHUNK = 128
LOADS = 4
COST_F = 4_000_000_000
COST_B = 12_000_000
VMEM_LIMIT = 32 * 1024 * 1024

BF16 = jnp.bfloat16
F32 = jnp.float32
I32 = jnp.int32


def matmul(left, right, left_dim, right_dim):
    return lax.dot_general(
        left, right, (((left_dim,), (right_dim,)), ((), ())), preferred_element_type=F32
    )


def params():
    return pltpu.CompilerParams(vmem_limit_bytes=VMEM_LIMIT)


def in_hbm(array):
    return pltpu.with_memory_space_constraint(array, pltpu.HBM)


def spans(extent, size):
    return [(start, min(size, extent - start)) for start in range(0, extent, size)]


def padded(rows):
    return -(-rows // 8) * 8


def distance(index, experts):
    return (experts - index) % experts


def dispatch_kernel(experts, hosts, slots, chunks, pieces, *refs):
    plan_hbm, caps_hbm, ids_hbm, gates_hbm, tok_hbm, grad_hbm = refs[:6]
    send_refs = refs[6 : 6 + pieces]
    scaled_ref, pick_ref, plan_ref, caps_ref, ids_ref, gates_ref, both_ref, wide, sems = refs[6 + pieces :]
    choose, count = ids_ref.shape
    block = padded(2 * slots)
    pairs = [(ids_hbm, ids_ref), (plan_hbm, plan_ref), (caps_hbm, caps_ref), (gates_hbm, gates_ref)]
    for place, source in enumerate((tok_hbm, grad_hbm)):
        for start, size in spans(count, count // LOADS):
            target = both_ref.at[pl.ds(place * count + start, size)]
            pairs.append((source.at[pl.ds(start, size)], target))
    copies = [
        pltpu.make_async_copy(source, target, sems.at[i])
        for i, (source, target) in enumerate(pairs)
    ]
    for copy in copies:
        copy.start()
    me = lax.axis_index("expert")
    row = lax.broadcasted_iota(I32, (block, count), 0)
    col = lax.broadcasted_iota(I32, (block, count), 1)
    is_cot = row >= slots
    slot = jnp.where(is_cot, row - slots, row)
    valid = row < 2 * slots
    is_spare = slot >= OWN
    spare_slot = jnp.maximum(slot - OWN, 0)
    replica = jnp.where(is_spare, 1 + lax.div(spare_slot, SPARE), 0)
    position = jnp.where(is_spare, lax.rem(spare_slot, SPARE), slot)
    token_slot = lax.rem(col, hosts)
    earlier = (
        lax.broadcasted_iota(I32, (count, count), 0) < lax.broadcasted_iota(I32, (count, count), 1)
    )
    earlier = earlier.astype(F32).astype(BF16)
    cots = jnp.concatenate([is_cot.astype(F32)] * experts, axis=0)
    for copy in copies[:4]:
        copy.wait()
    places = lax.broadcasted_iota(I32, (1, experts), 1)
    members, weights, limits = [], [], []
    for index in range(experts):
        expert = index if pieces == 1 else me ^ distance(index, experts)
        hot = (plan_ref[0:1, 0:1] == expert) | (plan_ref[1:2, 0:1] == expert)
        wanted = jnp.where(hot, token_slot[:1], 0)
        here = jnp.zeros((1, count), F32)
        weight = jnp.zeros((1, count), F32)
        for k in range(choose):
            chosen = ids_ref[k : k + 1, :] == expert
            here = jnp.where(chosen, 1.0, here)
            weight = jnp.where(chosen, gates_ref[k : k + 1, :], weight)
        fits = valid & (replica == wanted)
        members.append(jnp.where(fits, jnp.broadcast_to(here, fits.shape), 0.0))
        weights.append(jnp.broadcast_to(weight, fits.shape))
        own_room = jnp.sum(jnp.where(places == expert, caps_ref[...], 0), axis=1, keepdims=True)
        room = jnp.where(is_spare, SPARE, own_room * BLK)
        limits.append(jnp.where(position < room, position, -1))
    member = jnp.concatenate(members, axis=0)
    weight = jnp.concatenate(weights, axis=0)
    limit = jnp.concatenate(limits, axis=0).astype(F32)
    before = matmul(member.astype(BF16), earlier, 1, 0)
    taken = jnp.where(before == limit, member, 0.0)
    pick_cot = taken * cots
    pick_tok = taken - pick_cot
    picks = jnp.concatenate([pick_tok.astype(BF16), pick_cot.astype(BF16)], axis=1)
    gate = jnp.sum(pick_cot * weight, axis=1, keepdims=True)
    scale = jnp.where(cots[:, :1] > 0.0, gate, 1.0)
    scaled_ref[...] = pick_tok * weight
    pick_ref[...] = pick_cot
    for copy in copies[4:]:
        copy.wait()
    send = scale * matmul(picks, both_ref[...], 1, 0)
    if pieces == 1:
        send_refs[0][...] = send.astype(BF16)
        return
    width = send.shape[1] // chunks
    for i, send_ref in enumerate(send_refs):
        for j in range(chunks):
            rows = send[i * block : i * block + 2 * slots, j * width : (j + 1) * width]
            wide[2 * slots * j : 2 * slots * (j + 1), :] = rows
        send_ref[...] = wide[...].astype(BF16)


def dispatch(plan, caps, ids, gates, tokens, grads, experts, slots, chunks, pieces):
    count, feature = tokens.shape
    vmem = pl.BlockSpec(memory_space=pltpu.VMEM)
    block = padded(2 * slots)
    sent = (experts * block, feature) if pieces == 1 else (2 * slots * chunks, feature // chunks)
    outs = pl.pallas_call(
        functools.partial(dispatch_kernel, experts, plan.shape[1], slots, chunks, pieces),
        out_shape=(jax.ShapeDtypeStruct(sent, BF16),) * pieces
        + (jax.ShapeDtypeStruct((experts * block, count), F32),) * 2,
        in_specs=[pl.BlockSpec(memory_space=pltpu.HBM)] * 6,
        out_specs=(vmem,) * (pieces + 2),
        scratch_shapes=[
            pltpu.VMEM(plan.shape, I32),
            pltpu.VMEM(caps.shape, I32),
            pltpu.VMEM(ids.shape, I32),
            pltpu.VMEM(gates.shape, F32),
            pltpu.VMEM((2 * count, feature), BF16),
            pltpu.VMEM((2 * slots * chunks, feature // chunks), F32),
            pltpu.SemaphoreType.DMA((4 + 2 * LOADS,)),
        ],
        compiler_params=params(),
        cost_estimate=pl.CostEstimate(flops=COST_F, bytes_accessed=COST_B, transcendentals=0),
        name="dispatch",
    )(*(in_hbm(array) for array in (plan, caps, ids, gates, tokens, grads)))
    return outs[:pieces], outs[pieces:]


def half_columns(which, width):
    half = width // 2
    side = lax.rem(lax.axis_index("dp") + which, 2)
    return pl.ds(pl.multiple_of(side * half, half), half)


def half_partials(which, rows, cots, gate_ref, up_ref, down_ref, part_ref):
    width = gate_ref.shape[1]
    half = width // 2
    units = half_columns(which, width)
    part_ref[:, :half] = matmul(rows, gate_ref[:, units], 1, 0).astype(BF16)
    part_ref[:, half : 2 * half] = matmul(rows, up_ref[:, units], 1, 0).astype(BF16)
    part_ref[:, 2 * half :] = matmul(cots, down_ref[units, :], 1, 1).astype(BF16)


def give_kernel(slots, chunks, pieces, *refs):
    recv_refs = refs[:pieces]
    gate_ref, up_ref, down_ref, rows_ref, cots_ref, give_ref, wide, flat = refs[pieces:]
    group, block, width = wide.shape
    for s in range(group):
        recv_ref, start = (recv_refs[0], s * block) if pieces == 1 else (recv_refs[s], 0)
        wide[s] = recv_ref[start : start + block, :].astype(F32)
        for j in range(chunks):
            columns = pl.ds(j * width, width)
            for kind in range(2):
                place = (2 * j + kind) * slots
                flat[kind, s * slots : (s + 1) * slots, columns] = wide[s, place : place + slots, :]
    rows = flat[0].astype(BF16)
    cots = flat[1].astype(BF16)
    rows_ref[...] = rows
    cots_ref[...] = cots
    half_partials(1, rows, cots, gate_ref, up_ref, down_ref, give_ref)


def keep_kernel(rows_ref, cots_ref, gate_ref, up_ref, down_ref, keep_ref):
    half_partials(0, rows_ref[...], cots_ref[...], gate_ref, up_ref, down_ref, keep_ref)


def add_kernel(left_ref, right_ref, sum_ref):
    sum_ref[...] = (left_ref[...].astype(F32) + right_ref[...].astype(F32)).astype(BF16)


def activate_kernel(near_ref, far_ref, mine_ref):
    half = mine_ref.shape[1] // 3
    total = near_ref[...].astype(F32) + far_ref[...].astype(F32)
    gate_pre, up_pre, hidden_grad = (total[:, i * half : (i + 1) * half] for i in range(3))
    sigma = jax.nn.sigmoid(gate_pre)
    active = gate_pre * sigma
    slope = sigma * (1.0 + gate_pre * (1.0 - sigma))
    mine_ref[:, :half] = (active * up_pre).astype(BF16)
    mine_ref[:, half : 2 * half] = (hidden_grad * up_pre * slope).astype(BF16)
    mine_ref[:, 2 * half :] = (hidden_grad * active).astype(BF16)


def half_outputs(which, acts_ref, gate_ref, up_ref, down_ref):
    width = gate_ref.shape[1]
    half = width // 2
    units = half_columns(which, width)
    outs = matmul(acts_ref[:, :half], down_ref[units, :], 1, 0)
    ins = matmul(acts_ref[:, half : 2 * half], gate_ref[:, units], 1, 1)
    return outs, ins + matmul(acts_ref[:, 2 * half :], up_ref[:, units], 1, 1)


def own_kernel(mine_ref, scaled_ref, pick_ref, gate_ref, up_ref, down_ref, outs_ref, ins_ref, merge_ref):
    outs_ref[...], ins_ref[...] = half_outputs(0, mine_ref, gate_ref, up_ref, down_ref)
    scaled = scaled_ref[...].T
    count = scaled.shape[0]
    high = scaled.astype(BF16)
    merge_ref[:count, :] = high
    merge_ref[count : 2 * count, :] = (scaled - high.astype(F32)).astype(BF16)
    merge_ref[2 * count :, :] = pick_ref[...].T.astype(BF16)


def back_kernel(slots, chunks, pieces, *refs):
    theirs_ref, outs_ref, ins_ref, gate_ref, up_ref, down_ref = refs[:6]
    back_refs = refs[6 : 6 + pieces]
    flat, wide = refs[6 + pieces :]
    group, block, width = wide.shape
    outs, ins = half_outputs(1, theirs_ref, gate_ref, up_ref, down_ref)
    flat[0] = outs_ref[...] + outs
    flat[1] = ins_ref[...] + ins
    if block > 2 * slots * chunks:
        wide[...] = jnp.zeros_like(wide)
    for s in range(group):
        for j in range(chunks):
            columns = pl.ds(j * width, width)
            for kind in range(2):
                place = (2 * j + kind) * slots
                wide[s, place : place + slots, :] = flat[kind, s * slots : (s + 1) * slots, columns]
        back_ref, start = (back_refs[0], s * block) if pieces == 1 else (back_refs[s], 0)
        back_ref[start : start + block, :] = wide[s].astype(BF16)


def by_rows(kernel, name, steps, arrays, weights, outs, scratch=(), flops=0):
    def tiled(shape):
        return pl.BlockSpec((shape[0] // steps, shape[1]), lambda i: (i, 0))

    def whole(shape):
        return pl.BlockSpec(shape, lambda i: (0, 0))

    moved = sum(array.size * array.dtype.itemsize for array in (*arrays, *weights))
    results = pl.pallas_call(
        kernel,
        grid=(steps,),
        out_shape=tuple(jax.ShapeDtypeStruct(shape, dtype) for shape, dtype in outs),
        in_specs=[tiled(array.shape) for array in arrays] + [whole(w.shape) for w in weights],
        out_specs=tuple(tiled(shape) for shape, _ in outs),
        scratch_shapes=list(scratch),
        compiler_params=params(),
        cost_estimate=pl.CostEstimate(flops=flops, bytes_accessed=moved, transcendentals=0),
        name=name,
    )(*arrays, *weights)
    return results if len(outs) > 1 else results[0]


def grads_kernel(
    rows_ref, cots_ref, mine_ref, theirs_ref, gate_hbm, up_hbm, down_hbm, gate_ref, up_ref, down_ref, sems
):
    width = gate_ref.shape[1]
    half = width // 2
    copies = []

    def send(source, target, rows):
        copies.append(
            pltpu.make_async_copy(source.at[rows], target.at[rows], sems.at[len(copies)])
        )
        copies[-1].start()

    sides = [(mine_ref, half_columns(0, width)), (theirs_ref, half_columns(1, width))]
    for acts_ref, units in sides:
        for start, size in spans(half, CHUNK):
            rows = pl.ds(pl.multiple_of(units.start + start, 16), size)
            hidden = acts_ref[:, start : start + size]
            down_ref[rows, :] = matmul(hidden, cots_ref[...], 0, 0).astype(BF16)
            send(down_ref, down_hbm, rows)
    for place, out_ref, out_hbm in ((1, gate_ref, gate_hbm), (2, up_ref, up_hbm)):
        for start, size in spans(out_ref.shape[0], CHUNK):
            rows = pl.ds(start, size)
            for acts_ref, units in sides:
                grad = acts_ref[:, place * half : (place + 1) * half]
                out_ref[rows, units] = matmul(rows_ref[:, rows], grad, 0, 0).astype(BF16)
            send(out_ref, out_hbm, rows)
    for copy in copies:
        copy.wait()


def weight_grads(rows, cots, mine, theirs):
    total, feature = rows.shape
    width = 2 * mine.shape[1] // 3
    vmem = pl.BlockSpec(memory_space=pltpu.VMEM)
    hbm = pl.BlockSpec(memory_space=pltpu.HBM)
    shapes = ((feature, width), (feature, width), (width, feature))
    pieces = 2 * len(spans(feature, CHUNK)) + 2 * len(spans(width // 2, CHUNK))
    return pl.pallas_call(
        grads_kernel,
        out_shape=tuple(jax.ShapeDtypeStruct(shape, BF16) for shape in shapes),
        in_specs=[vmem] * 4,
        out_specs=(hbm,) * 3,
        scratch_shapes=[pltpu.VMEM(shape, BF16) for shape in shapes]
        + [pltpu.SemaphoreType.DMA((pieces,))],
        compiler_params=params(),
        cost_estimate=pl.CostEstimate(
            flops=6 * total * feature * width,
            bytes_accessed=6 * feature * width,
            transcendentals=0,
        ),
        name="weight_grads",
    )(rows, cots, mine, theirs)


def combine_kernel(columns, slots, chunks, pieces, *refs):
    back_refs = refs[:pieces]
    merge_ref, mixed_hbm, token_hbm, mixed_ref, token_ref, wide, flat, sems = refs[pieces:]
    if pieces > 1:
        flat[...] = jnp.zeros_like(flat)
        rows, width, block = 2 * slots, back_refs[0].shape[1], padded(2 * slots)
        for i, back_ref in enumerate(back_refs):
            wide[i] = back_ref[...].astype(F32)
            for j in range(chunks):
                part = pl.ds(j * width, width)
                flat[i * block : i * block + rows, part] = wide[i, j * rows : (j + 1) * rows, :]
    count = mixed_ref.shape[0]
    copies = []
    for start, size in columns:
        part = pl.ds(start, size)
        back = back_refs[0][:, part] if pieces == 1 else flat[:, part].astype(BF16)
        depth = merge_ref.shape[1]
        sums = sum(
            matmul(merge_ref[3 * count * i : 3 * count * (i + 1), :], back[i * depth : (i + 1) * depth], 1, 0)
            for i in range(back.shape[0] // depth)
        )
        mixed_ref[:, part] = (sums[:count] + sums[count : 2 * count]).astype(BF16)
        token_ref[:, part] = sums[2 * count :].astype(BF16)
        for source, target in ((mixed_ref, mixed_hbm), (token_ref, token_hbm)):
            copies.append(
                pltpu.make_async_copy(
                    source.at[:, part], target.at[:, part], sems.at[len(copies)]
                )
            )
            copies[-1].start()
    for copy in copies:
        copy.wait()


def combine(backs, merge, count, slots, chunks):
    pieces, feature = len(backs), chunks * backs[0].shape[1]
    columns = spans(feature, 2 * CHUNK if feature % CHUNK == 0 else feature)
    vmem = pl.BlockSpec(memory_space=pltpu.VMEM)
    hbm = pl.BlockSpec(memory_space=pltpu.HBM)
    shape = (count, feature)
    staged = [(pieces, *backs[0].shape), (merge.shape[1], feature)] if pieces > 1 else [(8, 128)] * 2
    return pl.pallas_call(
        functools.partial(combine_kernel, columns, slots, chunks, pieces),
        out_shape=(jax.ShapeDtypeStruct(shape, BF16),) * 2,
        in_specs=[vmem] * (pieces + 1),
        out_specs=(hbm, hbm),
        scratch_shapes=[
            pltpu.VMEM(shape, BF16),
            pltpu.VMEM(shape, BF16),
            *(pltpu.VMEM(extent, F32) for extent in staged),
            pltpu.SemaphoreType.DMA((2 * len(columns),)),
        ],
        compiler_params=params(),
        name="combine",
    )(*backs, merge)


def swapped(array, axis, distance):
    return lax.ppermute(array, axis, [(i, i ^ distance) for i in range(lax.axis_size(axis))])


def over_experts(arrays, experts):
    if len(arrays) == 1:
        array = arrays[0]
        blocks = array.reshape(experts, -1, array.shape[1])
        moved = lax.all_to_all(blocks, "expert", split_axis=0, concat_axis=0, tiled=True)
        return [moved.reshape(array.shape)]
    moved = [swapped(arrays[i], "expert", distance(i, experts)) for i in range(1, experts)]
    return [arrays[0]] + moved


def shards(
    tokens,
    out_grad,
    gate_weights,
    expert_ids,
    replica_plan,
    cap_blocks,
    gate_weight,
    up_weight,
    down_weight,
):
    experts = lax.axis_size("expert")
    hosts = replica_plan.shape[1]
    assert tokens.shape[0] % hosts == 0 and experts % GROUP == 0
    assert all(n >= 4 and n & (n - 1) == 0 for n in (experts, lax.axis_size("dp")))
    slots = OWN + SPARE * (hosts - 1)
    gate, up, down = gate_weight[0], up_weight[0], down_weight[0]
    feature, width = gate.shape
    pieces = experts if experts <= GROUP and feature % CHUNK == 0 else 1
    chunks = feature // CHUNK if pieces > 1 else 1
    block = 2 * slots * chunks if pieces > 1 else padded(2 * slots)
    sends, (scaled, pick) = dispatch(
        replica_plan,
        cap_blocks[None],
        expert_ids.T,
        gate_weights.T,
        tokens,
        out_grad,
        experts,
        slots,
        chunks,
        pieces,
    )
    recvs = over_experts(sends, experts)
    weights = (gate, up, down)
    steps, total, half = experts // GROUP, experts * slots, 3 * width // 2
    layout = (slots, chunks, pieces)
    flops = 3 * total * feature * width
    scratch = [
        pltpu.VMEM((GROUP, block, feature // chunks), F32),
        pltpu.VMEM((2, GROUP * slots, feature), F32),
    ]
    rows, cots, give = by_rows(
        functools.partial(give_kernel, *layout),
        "give",
        steps,
        recvs,
        weights,
        [((total, feature), BF16), ((total, feature), BF16), ((total, half), BF16)],
        scratch,
        flops,
    )
    got = swapped(give, "dp", 1)
    keep = by_rows(
        keep_kernel, "keep", steps, [rows, cots], weights, [((total, half), BF16)], (), flops
    )
    near = by_rows(add_kernel, "add", steps, [keep, got], [], [((total, half), BF16)])
    step, last = 2, lax.axis_size("dp") // 2
    while step < last:
        far = swapped(near, "dp", step)
        near = by_rows(add_kernel, "add", steps, [near, far], [], [((total, half), BF16)])
        step *= 2
    far = swapped(near, "dp", last)
    mine = by_rows(activate_kernel, "activate", steps, [near, far], [], [((total, half), BF16)])
    theirs = swapped(mine, "dp", 1)
    merge_shape = (steps * 3 * pick.shape[1], pick.shape[0] // steps)
    outs, ins, merge = by_rows(
        own_kernel,
        "own",
        steps,
        [mine, scaled, pick],
        weights,
        [((total, feature), F32), ((total, feature), F32), (merge_shape, BF16)],
        (),
        flops,
    )
    backs = by_rows(
        functools.partial(back_kernel, *layout),
        "back",
        steps,
        [theirs, outs, ins],
        weights,
        [((experts * block // pieces, feature // chunks), BF16)] * pieces,
        scratch[::-1],
        flops,
    )
    returned = over_experts(backs if pieces > 1 else [backs], experts)
    gate_grad, up_grad, down_grad = weight_grads(rows, cots, mine, theirs)
    mixed, token_grad = combine(returned, merge, tokens.shape[0], slots, chunks)
    return mixed, token_grad, gate_grad[None], up_grad[None], down_grad[None]


def solution(mesh):
    return jax.shard_map(
        shards,
        mesh=mesh,
        in_specs=(
            P(("groups", "expert"), "dp"),
            P(("groups", "expert"), "dp"),
            P(("groups", "expert"), None),
            P(("groups", "expert"), None),
            P("groups", None),
            P("groups"),
            P("expert", "dp", None),
            P("expert", "dp", None),
            P("expert", None, "dp"),
        ),
        out_specs=(
            P(("groups", "expert"), "dp"),
            P(("groups", "expert"), "dp"),
            P(("groups", "expert"), "dp", None),
            P(("groups", "expert"), "dp", None),
            P(("groups", "expert"), None, "dp"),
        ),
        check_vma=False,
    )
```

```python
import functools

import jax
import jax.numpy as jnp
from jax import lax
from jax.experimental import pallas as pl
from jax.experimental.pallas import tpu as pltpu
from jax.sharding import PartitionSpec as P

BLK = 4
MAXB = 2
SPARE = 2
OWN = BLK * MAXB
GROUP = 4
CHUNK = 128
LOADS = 4
VMEM_LIMIT = 32 * 1024 * 1024

BF16 = jnp.bfloat16
F32 = jnp.float32
I32 = jnp.int32


def matmul(left, right, left_dim, right_dim):
    return lax.dot_general(
        left, right, (((left_dim,), (right_dim,)), ((), ())), preferred_element_type=F32
    )


def params():
    return pltpu.CompilerParams(vmem_limit_bytes=VMEM_LIMIT)


def in_hbm(array):
    return pltpu.with_memory_space_constraint(array, pltpu.HBM)


def spans(extent, size):
    return [(start, min(size, extent - start)) for start in range(0, extent, size)]


def padded(rows):
    return -(-rows // 8) * 8


def distance(index, experts):
    return (experts - index) % experts


def dispatch_kernel(experts, hosts, slots, chunks, pieces, *refs):
    plan_hbm, caps_hbm, ids_hbm, gates_hbm, tok_hbm, grad_hbm = refs[:6]
    send_refs = refs[6 : 6 + pieces]
    scaled_ref, pick_ref, plan_ref, caps_ref, ids_ref, gates_ref, both_ref, wide, sems = refs[6 + pieces :]
    choose, count = ids_ref.shape
    block = padded(2 * slots)
    pairs = [(ids_hbm, ids_ref), (plan_hbm, plan_ref), (caps_hbm, caps_ref), (gates_hbm, gates_ref)]
    for place, source in enumerate((tok_hbm, grad_hbm)):
        for start, size in spans(count, count // LOADS):
            target = both_ref.at[pl.ds(place * count + start, size)]
            pairs.append((source.at[pl.ds(start, size)], target))
    copies = [
        pltpu.make_async_copy(source, target, sems.at[i])
        for i, (source, target) in enumerate(pairs)
    ]
    for copy in copies:
        copy.start()
    me = lax.axis_index("expert")
    row = lax.broadcasted_iota(I32, (block, count), 0)
    col = lax.broadcasted_iota(I32, (block, count), 1)
    is_cot = row >= slots
    slot = jnp.where(is_cot, row - slots, row)
    valid = row < 2 * slots
    is_spare = slot >= OWN
    spare_slot = jnp.maximum(slot - OWN, 0)
    replica = jnp.where(is_spare, 1 + lax.div(spare_slot, SPARE), 0)
    position = jnp.where(is_spare, lax.rem(spare_slot, SPARE), slot)
    token_slot = lax.rem(col, hosts)
    earlier = (
        lax.broadcasted_iota(I32, (count, count), 0) < lax.broadcasted_iota(I32, (count, count), 1)
    )
    earlier = earlier.astype(F32).astype(BF16)
    cots = jnp.concatenate([is_cot.astype(F32)] * experts, axis=0)
    for copy in copies[:4]:
        copy.wait()
    members, weights, limits = [], [], []
    for index in range(experts):
        expert = index if pieces == 1 else me ^ distance(index, experts)
        hot = (plan_ref[0, 0] == expert) | (plan_ref[1, 0] == expert)
        wanted = token_slot * hot.astype(I32)
        here = jnp.zeros((1, count), F32)
        weight = jnp.zeros((1, count), F32)
        for k in range(choose):
            chosen = ids_ref[k : k + 1, :] == expert
            here = jnp.where(chosen, 1.0, here)
            weight = jnp.where(chosen, gates_ref[k : k + 1, :], weight)
        fits = valid & (replica == wanted)
        members.append(jnp.where(fits, jnp.broadcast_to(here, fits.shape), 0.0))
        weights.append(jnp.broadcast_to(weight, fits.shape))
        room = jnp.where(is_spare, SPARE, caps_ref[expert] * BLK)
        limits.append(jnp.where(position < room, position, -1))
    member = jnp.concatenate(members, axis=0)
    weight = jnp.concatenate(weights, axis=0)
    limit = jnp.concatenate(limits, axis=0).astype(F32)
    before = matmul(member.astype(BF16), earlier, 1, 0)
    taken = jnp.where(before == limit, member, 0.0)
    pick_cot = taken * cots
    pick_tok = taken - pick_cot
    picks = jnp.concatenate([pick_tok.astype(BF16), pick_cot.astype(BF16)], axis=1)
    gate = jnp.sum(pick_cot * weight, axis=1, keepdims=True)
    scale = jnp.where(cots[:, :1] > 0.0, gate, 1.0)
    scaled_ref[...] = pick_tok * weight
    pick_ref[...] = pick_cot
    for copy in copies[4:]:
        copy.wait()
    send = scale * matmul(picks, both_ref[...], 1, 0)
    if pieces == 1:
        send_refs[0][...] = send.astype(BF16)
        return
    width = send.shape[1] // chunks
    for i, send_ref in enumerate(send_refs):
        for j in range(chunks):
            rows = send[i * block : i * block + 2 * slots, j * width : (j + 1) * width]
            wide[2 * slots * j : 2 * slots * (j + 1), :] = rows
        send_ref[...] = wide[...].astype(BF16)


def dispatch(plan, caps, ids, gates, tokens, grads, experts, slots, chunks, pieces):
    count, feature = tokens.shape
    vmem = pl.BlockSpec(memory_space=pltpu.VMEM)
    block = padded(2 * slots)
    sent = (experts * block, feature) if pieces == 1 else (2 * slots * chunks, feature // chunks)
    outs = pl.pallas_call(
        functools.partial(dispatch_kernel, experts, plan.shape[1], slots, chunks, pieces),
        out_shape=(jax.ShapeDtypeStruct(sent, BF16),) * pieces
        + (jax.ShapeDtypeStruct((experts * block, count), F32),) * 2,
        in_specs=[pl.BlockSpec(memory_space=pltpu.HBM)] * 6,
        out_specs=(vmem,) * (pieces + 2),
        scratch_shapes=[
            pltpu.SMEM(plan.shape, I32),
            pltpu.SMEM(caps.shape, I32),
            pltpu.VMEM(ids.shape, I32),
            pltpu.VMEM(gates.shape, F32),
            pltpu.VMEM((2 * count, feature), BF16),
            pltpu.VMEM((2 * slots * chunks, feature // chunks), F32),
            pltpu.SemaphoreType.DMA((4 + 2 * LOADS,)),
        ],
        compiler_params=params(),
        name="dispatch",
    )(*(in_hbm(array) for array in (plan, caps, ids, gates, tokens, grads)))
    return outs[:pieces], outs[pieces:]


def load_kernel(
    gate_hbm, up_hbm, down_hbm, scaled_ref, pick_ref, gate_ref, up_ref, down_ref, merge_ref, sems
):
    copies = []
    for source, target in ((gate_hbm, gate_ref), (up_hbm, up_ref), (down_hbm, down_ref)):
        for start, size in spans(source.shape[0], source.shape[0] // LOADS):
            rows = pl.ds(start, size)
            copies.append(
                pltpu.make_async_copy(source.at[rows], target.at[rows], sems.at[len(copies)])
            )
    for copy in copies:
        copy.start()
    scaled = scaled_ref[...].T
    count = scaled.shape[0]
    high = scaled.astype(BF16)
    merge_ref[:count, :] = high
    merge_ref[count : 2 * count, :] = (scaled - high.astype(F32)).astype(BF16)
    merge_ref[2 * count :, :] = pick_ref[...].T.astype(BF16)
    for copy in copies:
        copy.wait()


def load_weights(gate, up, down, scaled, pick):
    hbm = pl.BlockSpec(memory_space=pltpu.HBM)
    vmem = pl.BlockSpec(memory_space=pltpu.VMEM)
    assert all(w.shape[0] % (16 * LOADS) == 0 for w in (gate, up, down))
    merge = jax.ShapeDtypeStruct((3 * pick.shape[1], pick.shape[0]), BF16)
    return pl.pallas_call(
        load_kernel,
        out_shape=tuple(pltpu.VMEM(w.shape, BF16) for w in (gate, up, down)) + (merge,),
        in_specs=[hbm, hbm, hbm, vmem, vmem],
        out_specs=(vmem,) * 4,
        scratch_shapes=[pltpu.SemaphoreType.DMA((3 * LOADS,))],
        compiler_params=params(),
        cost_estimate=pl.CostEstimate(
            flops=0, bytes_accessed=2 * 3 * gate.size * 2, transcendentals=0
        ),
        name="load_weights",
    )(in_hbm(gate), in_hbm(up), in_hbm(down), scaled, pick)


def half_columns(which, width):
    half = width // 2
    side = lax.rem(lax.axis_index("dp") + which, 2)
    return pl.ds(pl.multiple_of(side * half, half), half)


def half_partials(which, rows, cots, gate_ref, up_ref, down_ref, part_ref):
    width = gate_ref.shape[1]
    half = width // 2
    units = half_columns(which, width)
    both = jnp.concatenate([gate_ref[:, units], up_ref[:, units]], axis=1)
    part_ref[:, : 2 * half] = matmul(rows, both, 1, 0).astype(BF16)
    part_ref[:, 2 * half :] = matmul(cots, down_ref[units, :], 1, 1).astype(BF16)


def give_kernel(slots, chunks, pieces, *refs):
    recv_refs = refs[:pieces]
    gate_ref, up_ref, down_ref, rows_ref, cots_ref, give_ref, wide, flat = refs[pieces:]
    group, block, width = wide.shape
    for s in range(group):
        recv_ref, start = (recv_refs[0], s * block) if pieces == 1 else (recv_refs[s], 0)
        wide[s] = recv_ref[start : start + block, :].astype(F32)
        for j in range(chunks):
            columns = pl.ds(j * width, width)
            for kind in range(2):
                place = (2 * j + kind) * slots
                flat[kind, s * slots : (s + 1) * slots, columns] = wide[s, place : place + slots, :]
    rows = flat[0].astype(BF16)
    cots = flat[1].astype(BF16)
    rows_ref[...] = rows
    cots_ref[...] = cots
    half_partials(1, rows, cots, gate_ref, up_ref, down_ref, give_ref)


def keep_kernel(rows_ref, cots_ref, gate_ref, up_ref, down_ref, keep_ref):
    half_partials(0, rows_ref[...], cots_ref[...], gate_ref, up_ref, down_ref, keep_ref)


def add_kernel(left_ref, right_ref, sum_ref):
    sum_ref[...] = (left_ref[...].astype(F32) + right_ref[...].astype(F32)).astype(BF16)


def activate_kernel(near_ref, far_ref, mine_ref):
    half = mine_ref.shape[1] // 3
    total = near_ref[...].astype(F32) + far_ref[...].astype(F32)
    gate_pre, up_pre, hidden_grad = (total[:, i * half : (i + 1) * half] for i in range(3))
    sigma = jax.nn.sigmoid(gate_pre)
    active = gate_pre * sigma
    slope = sigma * (1.0 + gate_pre * (1.0 - sigma))
    mine_ref[:, :half] = (active * up_pre).astype(BF16)
    mine_ref[:, half : 2 * half] = (hidden_grad * up_pre * slope).astype(BF16)
    mine_ref[:, 2 * half :] = (hidden_grad * active).astype(BF16)


def half_outputs(which, acts_ref, gate_ref, up_ref, down_ref):
    width = gate_ref.shape[1]
    half = width // 2
    units = half_columns(which, width)
    outs = matmul(acts_ref[:, :half], down_ref[units, :], 1, 0)
    both = jnp.concatenate([gate_ref[:, units], up_ref[:, units]], axis=1)
    return outs, matmul(acts_ref[:, half:], both, 1, 1)


def own_kernel(mine_ref, gate_ref, up_ref, down_ref, outs_ref, ins_ref):
    outs_ref[...], ins_ref[...] = half_outputs(0, mine_ref, gate_ref, up_ref, down_ref)


def back_kernel(slots, chunks, pieces, *refs):
    theirs_ref, outs_ref, ins_ref, gate_ref, up_ref, down_ref = refs[:6]
    back_refs = refs[6 : 6 + pieces]
    flat, wide = refs[6 + pieces :]
    group, block, width = wide.shape
    outs, ins = half_outputs(1, theirs_ref, gate_ref, up_ref, down_ref)
    flat[0] = outs_ref[...] + outs
    flat[1] = ins_ref[...] + ins
    if block > 2 * slots * chunks:
        wide[...] = jnp.zeros_like(wide)
    for s in range(group):
        for j in range(chunks):
            columns = pl.ds(j * width, width)
            for kind in range(2):
                place = (2 * j + kind) * slots
                wide[s, place : place + slots, :] = flat[kind, s * slots : (s + 1) * slots, columns]
        back_ref, start = (back_refs[0], s * block) if pieces == 1 else (back_refs[s], 0)
        back_ref[start : start + block, :] = wide[s].astype(BF16)


def by_rows(kernel, name, steps, arrays, weights, outs, scratch=(), flops=0):
    def tiled(shape):
        return pl.BlockSpec((shape[0] // steps, shape[1]), lambda i: (i, 0))

    def whole(shape):
        return pl.BlockSpec(shape, lambda i: (0, 0))

    moved = sum(array.size * array.dtype.itemsize for array in (*arrays, *weights))
    results = pl.pallas_call(
        kernel,
        grid=(steps,),
        out_shape=tuple(jax.ShapeDtypeStruct(shape, dtype) for shape, dtype in outs),
        in_specs=[tiled(array.shape) for array in arrays] + [whole(w.shape) for w in weights],
        out_specs=tuple(tiled(shape) for shape, _ in outs),
        scratch_shapes=list(scratch),
        compiler_params=params(),
        cost_estimate=pl.CostEstimate(flops=flops, bytes_accessed=moved, transcendentals=0),
        name=name,
    )(*arrays, *weights)
    return results if len(outs) > 1 else results[0]


def grads_kernel(
    rows_ref, cots_ref, mine_ref, theirs_ref, gate_hbm, up_hbm, down_hbm, gate_ref, up_ref, down_ref, sems
):
    width = gate_ref.shape[1]
    half = width // 2
    copies = []

    def send(source, target, rows):
        copies.append(
            pltpu.make_async_copy(source.at[rows], target.at[rows], sems.at[len(copies)])
        )
        copies[-1].start()

    sides = [(mine_ref, half_columns(0, width)), (theirs_ref, half_columns(1, width))]
    for acts_ref, units in sides:
        for start, size in spans(half, CHUNK):
            rows = pl.ds(pl.multiple_of(units.start + start, 16), size)
            hidden = acts_ref[:, start : start + size]
            down_ref[rows, :] = matmul(hidden, cots_ref[...], 0, 0).astype(BF16)
            send(down_ref, down_hbm, rows)
    for place, out_ref, out_hbm in ((1, gate_ref, gate_hbm), (2, up_ref, up_hbm)):
        for start, size in spans(out_ref.shape[0], CHUNK):
            rows = pl.ds(start, size)
            for acts_ref, units in sides:
                grad = acts_ref[:, place * half : (place + 1) * half]
                out_ref[rows, units] = matmul(rows_ref[:, rows], grad, 0, 0).astype(BF16)
            send(out_ref, out_hbm, rows)
    for copy in copies:
        copy.wait()


def weight_grads(rows, cots, mine, theirs):
    total, feature = rows.shape
    width = 2 * mine.shape[1] // 3
    vmem = pl.BlockSpec(memory_space=pltpu.VMEM)
    hbm = pl.BlockSpec(memory_space=pltpu.HBM)
    shapes = ((feature, width), (feature, width), (width, feature))
    pieces = 2 * len(spans(feature, CHUNK)) + 2 * len(spans(width // 2, CHUNK))
    return pl.pallas_call(
        grads_kernel,
        out_shape=tuple(jax.ShapeDtypeStruct(shape, BF16) for shape in shapes),
        in_specs=[vmem] * 4,
        out_specs=(hbm,) * 3,
        scratch_shapes=[pltpu.VMEM(shape, BF16) for shape in shapes]
        + [pltpu.SemaphoreType.DMA((pieces,))],
        compiler_params=params(),
        cost_estimate=pl.CostEstimate(
            flops=6 * total * feature * width,
            bytes_accessed=6 * feature * width,
            transcendentals=0,
        ),
        name="weight_grads",
    )(rows, cots, mine, theirs)


def combine_kernel(columns, slots, chunks, pieces, *refs):
    back_refs = refs[:pieces]
    merge_ref, mixed_hbm, token_hbm, mixed_ref, token_ref, wide, flat, sems = refs[pieces:]
    if pieces > 1:
        flat[...] = jnp.zeros_like(flat)
        rows, width, block = 2 * slots, back_refs[0].shape[1], padded(2 * slots)
        for i, back_ref in enumerate(back_refs):
            wide[i] = back_ref[...].astype(F32)
            for j in range(chunks):
                part = pl.ds(j * width, width)
                flat[i * block : i * block + rows, part] = wide[i, j * rows : (j + 1) * rows, :]
    count = mixed_ref.shape[0]
    copies = []
    for start, size in columns:
        part = pl.ds(start, size)
        back = back_refs[0][:, part] if pieces == 1 else flat[:, part].astype(BF16)
        sums = matmul(merge_ref[...], back, 1, 0)
        mixed_ref[:, part] = (sums[:count] + sums[count : 2 * count]).astype(BF16)
        token_ref[:, part] = sums[2 * count :].astype(BF16)
        for source, target in ((mixed_ref, mixed_hbm), (token_ref, token_hbm)):
            copies.append(
                pltpu.make_async_copy(
                    source.at[:, part], target.at[:, part], sems.at[len(copies)]
                )
            )
            copies[-1].start()
    for copy in copies:
        copy.wait()


def combine(backs, merge, slots, chunks):
    pieces, feature, count = len(backs), chunks * backs[0].shape[1], merge.shape[0] // 3
    columns = spans(feature, 2 * CHUNK if feature % CHUNK == 0 else feature)
    vmem = pl.BlockSpec(memory_space=pltpu.VMEM)
    hbm = pl.BlockSpec(memory_space=pltpu.HBM)
    shape = (count, feature)
    staged = [(pieces, *backs[0].shape), (merge.shape[1], feature)] if pieces > 1 else [(8, 128)] * 2
    return pl.pallas_call(
        functools.partial(combine_kernel, columns, slots, chunks, pieces),
        out_shape=(jax.ShapeDtypeStruct(shape, BF16),) * 2,
        in_specs=[vmem] * (pieces + 1),
        out_specs=(hbm, hbm),
        scratch_shapes=[
            pltpu.VMEM(shape, BF16),
            pltpu.VMEM(shape, BF16),
            *(pltpu.VMEM(extent, F32) for extent in staged),
            pltpu.SemaphoreType.DMA((2 * len(columns),)),
        ],
        compiler_params=params(),
        name="combine",
    )(*backs, merge)


def swapped(array, axis, distance):
    return lax.ppermute(array, axis, [(i, i ^ distance) for i in range(lax.axis_size(axis))])


def over_experts(arrays, experts):
    if len(arrays) == 1:
        array = arrays[0]
        blocks = array.reshape(experts, -1, array.shape[1])
        moved = lax.all_to_all(blocks, "expert", split_axis=0, concat_axis=0, tiled=True)
        return [moved.reshape(array.shape)]
    moved = [swapped(arrays[i], "expert", distance(i, experts)) for i in range(1, experts)]
    return [arrays[0]] + moved


def shards(
    tokens,
    out_grad,
    gate_weights,
    expert_ids,
    replica_plan,
    cap_blocks,
    gate_weight,
    up_weight,
    down_weight,
):
    experts = lax.axis_size("expert")
    hosts = replica_plan.shape[1]
    assert tokens.shape[0] % hosts == 0 and experts % GROUP == 0
    assert all(n >= 4 and n & (n - 1) == 0 for n in (experts, lax.axis_size("dp")))
    slots = OWN + SPARE * (hosts - 1)
    gate, up, down = gate_weight[0], up_weight[0], down_weight[0]
    feature, width = gate.shape
    pieces = experts if experts <= GROUP and feature % CHUNK == 0 else 1
    chunks = feature // CHUNK if pieces > 1 else 1
    block = 2 * slots * chunks if pieces > 1 else padded(2 * slots)
    sends, (scaled, pick) = dispatch(
        replica_plan,
        cap_blocks,
        expert_ids.T,
        gate_weights.T,
        tokens,
        out_grad,
        experts,
        slots,
        chunks,
        pieces,
    )
    recvs = over_experts(sends, experts)
    *weights, merge = load_weights(gate, up, down, scaled, pick)
    steps, total, half = experts // GROUP, experts * slots, 3 * width // 2
    layout = (slots, chunks, pieces)
    flops = 3 * total * feature * width
    scratch = [
        pltpu.VMEM((GROUP, block, feature // chunks), F32),
        pltpu.VMEM((2, GROUP * slots, feature), F32),
    ]
    rows, cots, give = by_rows(
        functools.partial(give_kernel, *layout),
        "give",
        steps,
        recvs,
        weights,
        [((total, feature), BF16), ((total, feature), BF16), ((total, half), BF16)],
        scratch,
        flops,
    )
    got = swapped(give, "dp", 1)
    keep = by_rows(
        keep_kernel, "keep", steps, [rows, cots], weights, [((total, half), BF16)], (), flops
    )
    near = by_rows(add_kernel, "add", steps, [keep, got], [], [((total, half), BF16)])
    step, last = 2, lax.axis_size("dp") // 2
    while step < last:
        far = swapped(near, "dp", step)
        near = by_rows(add_kernel, "add", steps, [near, far], [], [((total, half), BF16)])
        step *= 2
    far = swapped(near, "dp", last)
    mine = by_rows(activate_kernel, "activate", steps, [near, far], [], [((total, half), BF16)])
    theirs = swapped(mine, "dp", 1)
    outs, ins = by_rows(
        own_kernel, "own", steps, [mine], weights, [((total, feature), F32)] * 2, (), flops
    )
    backs = by_rows(
        functools.partial(back_kernel, *layout),
        "back",
        steps,
        [theirs, outs, ins],
        weights,
        [((experts * block // pieces, feature // chunks), BF16)] * pieces,
        scratch[::-1],
        flops,
    )
    returned = over_experts(backs if pieces > 1 else [backs], experts)
    gate_grad, up_grad, down_grad = weight_grads(rows, cots, mine, theirs)
    mixed, token_grad = combine(returned, merge, slots, chunks)
    return mixed, token_grad, gate_grad[None], up_grad[None], down_grad[None]


def solution(mesh):
    return jax.shard_map(
        shards,
        mesh=mesh,
        in_specs=(
            P(("groups", "expert"), "dp"),
            P(("groups", "expert"), "dp"),
            P(("groups", "expert"), None),
            P(("groups", "expert"), None),
            P("groups", None),
            P("groups"),
            P("expert", "dp", None),
            P("expert", "dp", None),
            P("expert", None, "dp"),
        ),
        out_specs=(
            P(("groups", "expert"), "dp"),
            P(("groups", "expert"), "dp"),
            P(("groups", "expert"), "dp", None),
            P(("groups", "expert"), "dp", None),
            P(("groups", "expert"), None, "dp"),
        ),
        check_vma=False,
    )
```

```python
import functools

import jax
import jax.numpy as jnp
from jax import lax
from jax.experimental import pallas as pl
from jax.experimental.pallas import tpu as pltpu
from jax.sharding import PartitionSpec as P

BLK = 4
MAXB = 2
SPARE = 2
OWN = BLK * MAXB
GROUP = 4
ORDER = (0, 2, 3, 1)
CHUNK = 128
LOADS = 4
VMEM_LIMIT = 32 * 1024 * 1024

BF16 = jnp.bfloat16
F32 = jnp.float32
I32 = jnp.int32


def matmul(left, right, left_dim, right_dim):
    return lax.dot_general(
        left, right, (((left_dim,), (right_dim,)), ((), ())), preferred_element_type=F32
    )


def params():
    return pltpu.CompilerParams(vmem_limit_bytes=VMEM_LIMIT)


def in_hbm(array):
    return pltpu.with_memory_space_constraint(array, pltpu.HBM)


def spans(extent, size):
    return [(start, min(size, extent - start)) for start in range(0, extent, size)]


def padded(rows):
    return -(-rows // 8) * 8


def distance(index):
    return ORDER[index]


def dispatch_kernel(experts, hosts, slots, chunks, pieces, *refs):
    plan_hbm, caps_hbm, ids_hbm, gates_hbm, tok_hbm, grad_hbm = refs[:6]
    send_refs = refs[6 : 6 + pieces]
    scaled_ref, pick_ref, plan_ref, caps_ref, ids_ref, gates_ref, both_ref, wide, sems = refs[6 + pieces :]
    choose, count = ids_ref.shape
    block = padded(2 * slots)
    pairs = [(ids_hbm, ids_ref), (plan_hbm, plan_ref), (caps_hbm, caps_ref), (gates_hbm, gates_ref)]
    for place, source in enumerate((tok_hbm, grad_hbm)):
        for start, size in spans(count, count // LOADS):
            target = both_ref.at[pl.ds(place * count + start, size)]
            pairs.append((source.at[pl.ds(start, size)], target))
    copies = [
        pltpu.make_async_copy(source, target, sems.at[i])
        for i, (source, target) in enumerate(pairs)
    ]
    for copy in copies:
        copy.start()
    me = lax.axis_index("expert")
    row = lax.broadcasted_iota(I32, (block, count), 0)
    col = lax.broadcasted_iota(I32, (block, count), 1)
    is_cot = row >= slots
    slot = jnp.where(is_cot, row - slots, row)
    valid = row < 2 * slots
    is_spare = slot >= OWN
    spare_slot = jnp.maximum(slot - OWN, 0)
    replica = jnp.where(is_spare, 1 + lax.div(spare_slot, SPARE), 0)
    position = jnp.where(is_spare, lax.rem(spare_slot, SPARE), slot)
    token_slot = lax.rem(col, hosts)
    earlier = (
        lax.broadcasted_iota(I32, (count, count), 0) < lax.broadcasted_iota(I32, (count, count), 1)
    )
    earlier = earlier.astype(F32).astype(BF16)
    cots = jnp.concatenate([is_cot.astype(F32)] * experts, axis=0)
    for copy in copies[:4]:
        copy.wait()
    members, weights, limits = [], [], []
    for index in range(experts):
        expert = index if pieces == 1 else me ^ distance(index)
        hot = (plan_ref[0, 0] == expert) | (plan_ref[1, 0] == expert)
        wanted = token_slot * hot.astype(I32)
        here = jnp.zeros((1, count), F32)
        weight = jnp.zeros((1, count), F32)
        for k in range(choose):
            chosen = ids_ref[k : k + 1, :] == expert
            here = jnp.where(chosen, 1.0, here)
            weight = jnp.where(chosen, gates_ref[k : k + 1, :], weight)
        fits = valid & (replica == wanted)
        members.append(jnp.where(fits, jnp.broadcast_to(here, fits.shape), 0.0))
        weights.append(jnp.broadcast_to(weight, fits.shape))
        room = jnp.where(is_spare, SPARE, caps_ref[expert] * BLK)
        limits.append(jnp.where(position < room, position, -1))
    member = jnp.concatenate(members, axis=0)
    weight = jnp.concatenate(weights, axis=0)
    limit = jnp.concatenate(limits, axis=0).astype(F32)
    before = matmul(member.astype(BF16), earlier, 1, 0)
    taken = jnp.where(before == limit, member, 0.0)
    pick_cot = taken * cots
    pick_tok = taken - pick_cot
    picks = jnp.concatenate([pick_tok.astype(BF16), pick_cot.astype(BF16)], axis=1)
    gate = jnp.sum(pick_cot * weight, axis=1, keepdims=True)
    scale = jnp.where(cots[:, :1] > 0.0, gate, 1.0)
    scaled_ref[...] = pick_tok * weight
    pick_ref[...] = pick_cot
    for copy in copies[4:]:
        copy.wait()
    send = scale * matmul(picks, both_ref[...], 1, 0)
    if pieces == 1:
        send_refs[0][...] = send.astype(BF16)
        return
    width = send.shape[1] // chunks
    for i, send_ref in enumerate(send_refs):
        for j in range(chunks):
            rows = send[i * block : i * block + 2 * slots, j * width : (j + 1) * width]
            wide[2 * slots * j : 2 * slots * (j + 1), :] = rows
        send_ref[...] = wide[...].astype(BF16)


def dispatch(plan, caps, ids, gates, tokens, grads, experts, slots, chunks, pieces):
    count, feature = tokens.shape
    vmem = pl.BlockSpec(memory_space=pltpu.VMEM)
    block = padded(2 * slots)
    sent = (experts * block, feature) if pieces == 1 else (2 * slots * chunks, feature // chunks)
    outs = pl.pallas_call(
        functools.partial(dispatch_kernel, experts, plan.shape[1], slots, chunks, pieces),
        out_shape=(jax.ShapeDtypeStruct(sent, BF16),) * pieces
        + (jax.ShapeDtypeStruct((experts * block, count), F32),) * 2,
        in_specs=[pl.BlockSpec(memory_space=pltpu.HBM)] * 6,
        out_specs=(vmem,) * (pieces + 2),
        scratch_shapes=[
            pltpu.SMEM(plan.shape, I32),
            pltpu.SMEM(caps.shape, I32),
            pltpu.VMEM(ids.shape, I32),
            pltpu.VMEM(gates.shape, F32),
            pltpu.VMEM((2 * count, feature), BF16),
            pltpu.VMEM((2 * slots * chunks, feature // chunks), F32),
            pltpu.SemaphoreType.DMA((4 + 2 * LOADS,)),
        ],
        compiler_params=params(),
        name="dispatch",
    )(*(in_hbm(array) for array in (plan, caps, ids, gates, tokens, grads)))
    return outs[:pieces], outs[pieces:]


def load_kernel(
    gate_hbm, up_hbm, down_hbm, scaled_ref, pick_ref, gate_ref, up_ref, down_ref, merge_ref, sems
):
    copies = []
    for source, target in ((gate_hbm, gate_ref), (up_hbm, up_ref), (down_hbm, down_ref)):
        for start, size in spans(source.shape[0], source.shape[0] // LOADS):
            rows = pl.ds(start, size)
            copies.append(
                pltpu.make_async_copy(source.at[rows], target.at[rows], sems.at[len(copies)])
            )
    for copy in copies:
        copy.start()
    scaled = scaled_ref[...].T
    count = scaled.shape[0]
    high = scaled.astype(BF16)
    merge_ref[:count, :] = high
    merge_ref[count : 2 * count, :] = (scaled - high.astype(F32)).astype(BF16)
    merge_ref[2 * count :, :] = pick_ref[...].T.astype(BF16)
    for copy in copies:
        copy.wait()


def load_weights(gate, up, down, scaled, pick):
    hbm = pl.BlockSpec(memory_space=pltpu.HBM)
    vmem = pl.BlockSpec(memory_space=pltpu.VMEM)
    assert all(w.shape[0] % (16 * LOADS) == 0 for w in (gate, up, down))
    merge = jax.ShapeDtypeStruct((3 * pick.shape[1], pick.shape[0]), BF16)
    return pl.pallas_call(
        load_kernel,
        out_shape=tuple(pltpu.VMEM(w.shape, BF16) for w in (gate, up, down)) + (merge,),
        in_specs=[hbm, hbm, hbm, vmem, vmem],
        out_specs=(vmem,) * 4,
        scratch_shapes=[pltpu.SemaphoreType.DMA((3 * LOADS,))],
        compiler_params=params(),
        cost_estimate=pl.CostEstimate(
            flops=0, bytes_accessed=2 * 3 * gate.size * 2, transcendentals=0
        ),
        name="load_weights",
    )(in_hbm(gate), in_hbm(up), in_hbm(down), scaled, pick)


def half_columns(which, width):
    half = width // 2
    side = lax.rem(lax.axis_index("dp") + which, 2)
    return pl.ds(pl.multiple_of(side * half, half), half)


def half_partials(which, rows, cots, gate_ref, up_ref, down_ref, part_ref):
    width = gate_ref.shape[1]
    half = width // 2
    units = half_columns(which, width)
    both = jnp.concatenate([gate_ref[:, units], up_ref[:, units]], axis=1)
    part_ref[:, : 2 * half] = matmul(rows, both, 1, 0).astype(BF16)
    part_ref[:, 2 * half :] = matmul(cots, down_ref[units, :], 1, 1).astype(BF16)


def give_kernel(slots, chunks, pieces, *refs):
    recv_refs = refs[:pieces]
    gate_ref, up_ref, down_ref, rows_ref, cots_ref, give_ref, wide, flat = refs[pieces:]
    group, block, width = wide.shape
    for s in range(group):
        recv_ref, start = (recv_refs[0], s * block) if pieces == 1 else (recv_refs[s], 0)
        wide[s] = recv_ref[start : start + block, :].astype(F32)
        for j in range(chunks):
            columns = pl.ds(j * width, width)
            for kind in range(2):
                place = (2 * j + kind) * slots
                flat[kind, s * slots : (s + 1) * slots, columns] = wide[s, place : place + slots, :]
    rows = flat[0].astype(BF16)
    cots = flat[1].astype(BF16)
    rows_ref[...] = rows
    cots_ref[...] = cots
    half_partials(1, rows, cots, gate_ref, up_ref, down_ref, give_ref)


def keep_kernel(rows_ref, cots_ref, gate_ref, up_ref, down_ref, keep_ref):
    half_partials(0, rows_ref[...], cots_ref[...], gate_ref, up_ref, down_ref, keep_ref)


def add_kernel(left_ref, right_ref, sum_ref):
    sum_ref[...] = (left_ref[...].astype(F32) + right_ref[...].astype(F32)).astype(BF16)


def activate_kernel(near_ref, far_ref, mine_ref):
    half = mine_ref.shape[1] // 3
    total = near_ref[...].astype(F32) + far_ref[...].astype(F32)
    gate_pre, up_pre, hidden_grad = (total[:, i * half : (i + 1) * half] for i in range(3))
    sigma = jax.nn.sigmoid(gate_pre)
    active = gate_pre * sigma
    slope = sigma * (1.0 + gate_pre * (1.0 - sigma))
    mine_ref[:, :half] = (active * up_pre).astype(BF16)
    mine_ref[:, half : 2 * half] = (hidden_grad * up_pre * slope).astype(BF16)
    mine_ref[:, 2 * half :] = (hidden_grad * active).astype(BF16)


def half_outputs(which, acts_ref, gate_ref, up_ref, down_ref):
    width = gate_ref.shape[1]
    half = width // 2
    units = half_columns(which, width)
    outs = matmul(acts_ref[:, :half], down_ref[units, :], 1, 0)
    both = jnp.concatenate([gate_ref[:, units], up_ref[:, units]], axis=1)
    return outs, matmul(acts_ref[:, half:], both, 1, 1)


def own_kernel(mine_ref, gate_ref, up_ref, down_ref, outs_ref, ins_ref):
    outs_ref[...], ins_ref[...] = half_outputs(0, mine_ref, gate_ref, up_ref, down_ref)


def back_kernel(slots, chunks, pieces, *refs):
    theirs_ref, outs_ref, ins_ref, gate_ref, up_ref, down_ref = refs[:6]
    back_refs = refs[6 : 6 + pieces]
    flat, wide = refs[6 + pieces :]
    group, block, width = wide.shape
    outs, ins = half_outputs(1, theirs_ref, gate_ref, up_ref, down_ref)
    flat[0] = outs_ref[...] + outs
    flat[1] = ins_ref[...] + ins
    if block > 2 * slots * chunks:
        wide[...] = jnp.zeros_like(wide)
    for s in range(group):
        for j in range(chunks):
            columns = pl.ds(j * width, width)
            for kind in range(2):
                place = (2 * j + kind) * slots
                wide[s, place : place + slots, :] = flat[kind, s * slots : (s + 1) * slots, columns]
        back_ref, start = (back_refs[0], s * block) if pieces == 1 else (back_refs[s], 0)
        back_ref[start : start + block, :] = wide[s].astype(BF16)


def by_rows(kernel, name, steps, arrays, weights, outs, scratch=(), flops=0):
    def tiled(shape):
        return pl.BlockSpec((shape[0] // steps, shape[1]), lambda i: (i, 0))

    def whole(shape):
        return pl.BlockSpec(shape, lambda i: (0, 0))

    moved = sum(array.size * array.dtype.itemsize for array in (*arrays, *weights))
    results = pl.pallas_call(
        kernel,
        grid=(steps,),
        out_shape=tuple(jax.ShapeDtypeStruct(shape, dtype) for shape, dtype in outs),
        in_specs=[tiled(array.shape) for array in arrays] + [whole(w.shape) for w in weights],
        out_specs=tuple(tiled(shape) for shape, _ in outs),
        scratch_shapes=list(scratch),
        compiler_params=params(),
        cost_estimate=pl.CostEstimate(flops=flops, bytes_accessed=moved, transcendentals=0),
        name=name,
    )(*arrays, *weights)
    return results if len(outs) > 1 else results[0]


def grads_kernel(
    rows_ref, cots_ref, mine_ref, theirs_ref, gate_hbm, up_hbm, down_hbm, gate_ref, up_ref, down_ref, sems
):
    width = gate_ref.shape[1]
    half = width // 2
    copies = []

    def send(source, target, rows):
        copies.append(
            pltpu.make_async_copy(source.at[rows], target.at[rows], sems.at[len(copies)])
        )
        copies[-1].start()

    sides = [(mine_ref, half_columns(0, width)), (theirs_ref, half_columns(1, width))]
    for acts_ref, units in sides:
        for start, size in spans(half, CHUNK):
            rows = pl.ds(pl.multiple_of(units.start + start, 16), size)
            hidden = acts_ref[:, start : start + size]
            down_ref[rows, :] = matmul(hidden, cots_ref[...], 0, 0).astype(BF16)
            send(down_ref, down_hbm, rows)
    for place, out_ref, out_hbm in ((1, gate_ref, gate_hbm), (2, up_ref, up_hbm)):
        for start, size in spans(out_ref.shape[0], CHUNK):
            rows = pl.ds(start, size)
            for acts_ref, units in sides:
                grad = acts_ref[:, place * half : (place + 1) * half]
                out_ref[rows, units] = matmul(rows_ref[:, rows], grad, 0, 0).astype(BF16)
            send(out_ref, out_hbm, rows)
    for copy in copies:
        copy.wait()


def weight_grads(rows, cots, mine, theirs):
    total, feature = rows.shape
    width = 2 * mine.shape[1] // 3
    vmem = pl.BlockSpec(memory_space=pltpu.VMEM)
    hbm = pl.BlockSpec(memory_space=pltpu.HBM)
    shapes = ((feature, width), (feature, width), (width, feature))
    pieces = 2 * len(spans(feature, CHUNK)) + 2 * len(spans(width // 2, CHUNK))
    return pl.pallas_call(
        grads_kernel,
        out_shape=tuple(jax.ShapeDtypeStruct(shape, BF16) for shape in shapes),
        in_specs=[vmem] * 4,
        out_specs=(hbm,) * 3,
        scratch_shapes=[pltpu.VMEM(shape, BF16) for shape in shapes]
        + [pltpu.SemaphoreType.DMA((pieces,))],
        compiler_params=params(),
        cost_estimate=pl.CostEstimate(
            flops=6 * total * feature * width,
            bytes_accessed=6 * feature * width,
            transcendentals=0,
        ),
        name="weight_grads",
    )(rows, cots, mine, theirs)


def combine_kernel(columns, slots, chunks, pieces, *refs):
    back_refs = refs[:pieces]
    merge_ref, mixed_hbm, token_hbm, mixed_ref, token_ref, wide, flat, sems = refs[pieces:]
    if pieces > 1:
        flat[...] = jnp.zeros_like(flat)
        rows, width, block = 2 * slots, back_refs[0].shape[1], padded(2 * slots)
        for i, back_ref in enumerate(back_refs):
            wide[i] = back_ref[...].astype(F32)
            for j in range(chunks):
                part = pl.ds(j * width, width)
                flat[i * block : i * block + rows, part] = wide[i, j * rows : (j + 1) * rows, :]
    count = mixed_ref.shape[0]
    copies = []
    for start, size in columns:
        part = pl.ds(start, size)
        back = back_refs[0][:, part] if pieces == 1 else flat[:, part].astype(BF16)
        sums = matmul(merge_ref[...], back, 1, 0)
        mixed_ref[:, part] = (sums[:count] + sums[count : 2 * count]).astype(BF16)
        token_ref[:, part] = sums[2 * count :].astype(BF16)
        for source, target in ((mixed_ref, mixed_hbm), (token_ref, token_hbm)):
            copies.append(
                pltpu.make_async_copy(
                    source.at[:, part], target.at[:, part], sems.at[len(copies)]
                )
            )
            copies[-1].start()
    for copy in copies:
        copy.wait()


def combine(backs, merge, slots, chunks):
    pieces, feature, count = len(backs), chunks * backs[0].shape[1], merge.shape[0] // 3
    columns = spans(feature, 2 * CHUNK if feature % CHUNK == 0 else feature)
    vmem = pl.BlockSpec(memory_space=pltpu.VMEM)
    hbm = pl.BlockSpec(memory_space=pltpu.HBM)
    shape = (count, feature)
    staged = [(pieces, *backs[0].shape), (merge.shape[1], feature)] if pieces > 1 else [(8, 128)] * 2
    return pl.pallas_call(
        functools.partial(combine_kernel, columns, slots, chunks, pieces),
        out_shape=(jax.ShapeDtypeStruct(shape, BF16),) * 2,
        in_specs=[vmem] * (pieces + 1),
        out_specs=(hbm, hbm),
        scratch_shapes=[
            pltpu.VMEM(shape, BF16),
            pltpu.VMEM(shape, BF16),
            *(pltpu.VMEM(extent, F32) for extent in staged),
            pltpu.SemaphoreType.DMA((2 * len(columns),)),
        ],
        compiler_params=params(),
        name="combine",
    )(*backs, merge)


def swapped(array, axis, distance):
    return lax.ppermute(array, axis, [(i, i ^ distance) for i in range(lax.axis_size(axis))])


def over_experts(arrays, experts):
    if len(arrays) == 1:
        array = arrays[0]
        blocks = array.reshape(experts, -1, array.shape[1])
        moved = lax.all_to_all(blocks, "expert", split_axis=0, concat_axis=0, tiled=True)
        return [moved.reshape(array.shape)]
    moved = [swapped(arrays[i], "expert", distance(i)) for i in range(1, experts)]
    return [arrays[0]] + moved


def shards(
    tokens,
    out_grad,
    gate_weights,
    expert_ids,
    replica_plan,
    cap_blocks,
    gate_weight,
    up_weight,
    down_weight,
):
    experts = lax.axis_size("expert")
    hosts = replica_plan.shape[1]
    assert tokens.shape[0] % hosts == 0 and experts % GROUP == 0
    assert all(n >= 4 and n & (n - 1) == 0 for n in (experts, lax.axis_size("dp")))
    slots = OWN + SPARE * (hosts - 1)
    gate, up, down = gate_weight[0], up_weight[0], down_weight[0]
    feature, width = gate.shape
    pieces = experts if experts <= GROUP and feature % CHUNK == 0 else 1
    chunks = feature // CHUNK if pieces > 1 else 1
    block = 2 * slots * chunks if pieces > 1 else padded(2 * slots)
    sends, (scaled, pick) = dispatch(
        replica_plan,
        cap_blocks,
        expert_ids.T,
        gate_weights.T,
        tokens,
        out_grad,
        experts,
        slots,
        chunks,
        pieces,
    )
    recvs = over_experts(sends, experts)
    *weights, merge = load_weights(gate, up, down, scaled, pick)
    steps, total, half = experts // GROUP, experts * slots, 3 * width // 2
    layout = (slots, chunks, pieces)
    flops = 3 * total * feature * width
    scratch = [
        pltpu.VMEM((GROUP, block, feature // chunks), F32),
        pltpu.VMEM((2, GROUP * slots, feature), F32),
    ]
    rows, cots, give = by_rows(
        functools.partial(give_kernel, *layout),
        "give",
        steps,
        recvs,
        weights,
        [((total, feature), BF16), ((total, feature), BF16), ((total, half), BF16)],
        scratch,
        flops,
    )
    got = swapped(give, "dp", 1)
    keep = by_rows(
        keep_kernel, "keep", steps, [rows, cots], weights, [((total, half), BF16)], (), flops
    )
    near = by_rows(add_kernel, "add", steps, [keep, got], [], [((total, half), BF16)])
    step, last = 2, lax.axis_size("dp") // 2
    while step < last:
        far = swapped(near, "dp", step)
        near = by_rows(add_kernel, "add", steps, [near, far], [], [((total, half), BF16)])
        step *= 2
    far = swapped(near, "dp", last)
    mine = by_rows(activate_kernel, "activate", steps, [near, far], [], [((total, half), BF16)])
    theirs = swapped(mine, "dp", 1)
    outs, ins = by_rows(
        own_kernel, "own", steps, [mine], weights, [((total, feature), F32)] * 2, (), flops
    )
    backs = by_rows(
        functools.partial(back_kernel, *layout),
        "back",
        steps,
        [theirs, outs, ins],
        weights,
        [((experts * block // pieces, feature // chunks), BF16)] * pieces,
        scratch[::-1],
        flops,
    )
    returned = over_experts(backs if pieces > 1 else [backs], experts)
    gate_grad, up_grad, down_grad = weight_grads(rows, cots, mine, theirs)
    mixed, token_grad = combine(returned, merge, slots, chunks)
    return mixed, token_grad, gate_grad[None], up_grad[None], down_grad[None]


def solution(mesh):
    return jax.shard_map(
        shards,
        mesh=mesh,
        in_specs=(
            P(("groups", "expert"), "dp"),
            P(("groups", "expert"), "dp"),
            P(("groups", "expert"), None),
            P(("groups", "expert"), None),
            P("groups", None),
            P("groups"),
            P("expert", "dp", None),
            P("expert", "dp", None),
            P("expert", None, "dp"),
        ),
        out_specs=(
            P(("groups", "expert"), "dp"),
            P(("groups", "expert"), "dp"),
            P(("groups", "expert"), "dp", None),
            P(("groups", "expert"), "dp", None),
            P(("groups", "expert"), None, "dp"),
        ),
        check_vma=False,
    )
```

```python
import functools

import jax
import jax.numpy as jnp
from jax import lax
from jax.experimental import pallas as pl
from jax.experimental.pallas import tpu as pltpu
from jax.sharding import PartitionSpec as P

BLK = 4
MAXB = 2
SPARE = 2
OWN = BLK * MAXB
GROUP = 4
SEND_ORDER = (0, 2, 3, 1)
BACK_ORDER = (0, 3, 2, 1)
CHUNK = 128
LOADS = 4
VMEM_LIMIT = 32 * 1024 * 1024

BF16 = jnp.bfloat16
F32 = jnp.float32
I32 = jnp.int32


def matmul(left, right, left_dim, right_dim):
    return lax.dot_general(
        left, right, (((left_dim,), (right_dim,)), ((), ())), preferred_element_type=F32
    )


def params():
    return pltpu.CompilerParams(vmem_limit_bytes=VMEM_LIMIT)


def in_hbm(array):
    return pltpu.with_memory_space_constraint(array, pltpu.HBM)


def spans(extent, size):
    return [(start, min(size, extent - start)) for start in range(0, extent, size)]


def padded(rows):
    return -(-rows // 8) * 8


def dispatch_kernel(experts, hosts, slots, chunks, pieces, *refs):
    plan_hbm, caps_hbm, ids_hbm, gates_hbm, tok_hbm, grad_hbm = refs[:6]
    send_refs = refs[6 : 6 + pieces]
    scaled_ref, pick_ref, plan_ref, caps_ref, ids_ref, gates_ref, both_ref, wide, sems = refs[6 + pieces :]
    choose, count = ids_ref.shape
    block = padded(2 * slots)
    pairs = [(ids_hbm, ids_ref), (plan_hbm, plan_ref), (caps_hbm, caps_ref), (gates_hbm, gates_ref)]
    for place, source in enumerate((tok_hbm, grad_hbm)):
        for start, size in spans(count, count // LOADS):
            target = both_ref.at[pl.ds(place * count + start, size)]
            pairs.append((source.at[pl.ds(start, size)], target))
    copies = [
        pltpu.make_async_copy(source, target, sems.at[i])
        for i, (source, target) in enumerate(pairs)
    ]
    for copy in copies:
        copy.start()
    me = lax.axis_index("expert")
    row = lax.broadcasted_iota(I32, (block, count), 0)
    col = lax.broadcasted_iota(I32, (block, count), 1)
    is_cot = row >= slots
    slot = jnp.where(is_cot, row - slots, row)
    valid = row < 2 * slots
    is_spare = slot >= OWN
    spare_slot = jnp.maximum(slot - OWN, 0)
    replica = jnp.where(is_spare, 1 + lax.div(spare_slot, SPARE), 0)
    position = jnp.where(is_spare, lax.rem(spare_slot, SPARE), slot)
    token_slot = lax.rem(col, hosts)
    earlier = (
        lax.broadcasted_iota(I32, (count, count), 0) < lax.broadcasted_iota(I32, (count, count), 1)
    )
    earlier = earlier.astype(F32).astype(BF16)
    cots = jnp.concatenate([is_cot.astype(F32)] * experts, axis=0)
    for copy in copies[:4]:
        copy.wait()
    members, weights, limits = [], [], []
    for index in range(experts):
        expert = index if pieces == 1 else me ^ SEND_ORDER[index]
        hot = (plan_ref[0, 0] == expert) | (plan_ref[1, 0] == expert)
        wanted = token_slot * hot.astype(I32)
        here = jnp.zeros((1, count), F32)
        weight = jnp.zeros((1, count), F32)
        for k in range(choose):
            chosen = ids_ref[k : k + 1, :] == expert
            here = jnp.where(chosen, 1.0, here)
            weight = jnp.where(chosen, gates_ref[k : k + 1, :], weight)
        fits = valid & (replica == wanted)
        members.append(jnp.where(fits, jnp.broadcast_to(here, fits.shape), 0.0))
        weights.append(jnp.broadcast_to(weight, fits.shape))
        room = jnp.where(is_spare, SPARE, caps_ref[expert] * BLK)
        limits.append(jnp.where(position < room, position, -1))
    member = jnp.concatenate(members, axis=0)
    weight = jnp.concatenate(weights, axis=0)
    limit = jnp.concatenate(limits, axis=0).astype(F32)
    before = matmul(member.astype(BF16), earlier, 1, 0)
    taken = jnp.where(before == limit, member, 0.0)
    pick_cot = taken * cots
    pick_tok = taken - pick_cot
    picks = jnp.concatenate([pick_tok.astype(BF16), pick_cot.astype(BF16)], axis=1)
    gate = jnp.sum(pick_cot * weight, axis=1, keepdims=True)
    scale = jnp.where(cots[:, :1] > 0.0, gate, 1.0)
    scaled_ref[...] = pick_tok * weight
    pick_ref[...] = pick_cot
    for copy in copies[4:]:
        copy.wait()
    send = scale * matmul(picks, both_ref[...], 1, 0)
    if pieces == 1:
        send_refs[0][...] = send.astype(BF16)
        return
    width = send.shape[1] // chunks
    for i, send_ref in enumerate(send_refs):
        for j in range(chunks):
            rows = send[i * block : i * block + 2 * slots, j * width : (j + 1) * width]
            wide[2 * slots * j : 2 * slots * (j + 1), :] = rows
        send_ref[...] = wide[...].astype(BF16)


def dispatch(plan, caps, ids, gates, tokens, grads, experts, slots, chunks, pieces):
    count, feature = tokens.shape
    vmem = pl.BlockSpec(memory_space=pltpu.VMEM)
    block = padded(2 * slots)
    sent = (experts * block, feature) if pieces == 1 else (2 * slots * chunks, feature // chunks)
    outs = pl.pallas_call(
        functools.partial(dispatch_kernel, experts, plan.shape[1], slots, chunks, pieces),
        out_shape=(jax.ShapeDtypeStruct(sent, BF16),) * pieces
        + (jax.ShapeDtypeStruct((experts * block, count), F32),) * 2,
        in_specs=[pl.BlockSpec(memory_space=pltpu.HBM)] * 6,
        out_specs=(vmem,) * (pieces + 2),
        scratch_shapes=[
            pltpu.SMEM(plan.shape, I32),
            pltpu.SMEM(caps.shape, I32),
            pltpu.VMEM(ids.shape, I32),
            pltpu.VMEM(gates.shape, F32),
            pltpu.VMEM((2 * count, feature), BF16),
            pltpu.VMEM((2 * slots * chunks, feature // chunks), F32),
            pltpu.SemaphoreType.DMA((4 + 2 * LOADS,)),
        ],
        compiler_params=params(),
        name="dispatch",
    )(*(in_hbm(array) for array in (plan, caps, ids, gates, tokens, grads)))
    return outs[:pieces], outs[pieces:]


def load_kernel(
    gate_hbm, up_hbm, down_hbm, scaled_ref, pick_ref, gate_ref, up_ref, down_ref, merge_ref, sems
):
    copies = []
    for source, target in ((gate_hbm, gate_ref), (up_hbm, up_ref), (down_hbm, down_ref)):
        for start, size in spans(source.shape[0], source.shape[0] // LOADS):
            rows = pl.ds(start, size)
            copies.append(
                pltpu.make_async_copy(source.at[rows], target.at[rows], sems.at[len(copies)])
            )
    for copy in copies:
        copy.start()
    scaled = scaled_ref[...].T
    count = scaled.shape[0]
    high = scaled.astype(BF16)
    merge_ref[:count, :] = high
    merge_ref[count : 2 * count, :] = (scaled - high.astype(F32)).astype(BF16)
    merge_ref[2 * count :, :] = pick_ref[...].T.astype(BF16)
    for copy in copies:
        copy.wait()


def load_weights(gate, up, down, scaled, pick):
    hbm = pl.BlockSpec(memory_space=pltpu.HBM)
    vmem = pl.BlockSpec(memory_space=pltpu.VMEM)
    assert all(w.shape[0] % (16 * LOADS) == 0 for w in (gate, up, down))
    merge = jax.ShapeDtypeStruct((3 * pick.shape[1], pick.shape[0]), BF16)
    return pl.pallas_call(
        load_kernel,
        out_shape=tuple(pltpu.VMEM(w.shape, BF16) for w in (gate, up, down)) + (merge,),
        in_specs=[hbm, hbm, hbm, vmem, vmem],
        out_specs=(vmem,) * 4,
        scratch_shapes=[pltpu.SemaphoreType.DMA((3 * LOADS,))],
        compiler_params=params(),
        cost_estimate=pl.CostEstimate(
            flops=0, bytes_accessed=2 * 3 * gate.size * 2, transcendentals=0
        ),
        name="load_weights",
    )(in_hbm(gate), in_hbm(up), in_hbm(down), scaled, pick)


def half_columns(which, width):
    half = width // 2
    side = lax.rem(lax.axis_index("dp") + which, 2)
    return pl.ds(pl.multiple_of(side * half, half), half)


def half_partials(which, rows, cots, gate_ref, up_ref, down_ref, part_ref):
    width = gate_ref.shape[1]
    half = width // 2
    units = half_columns(which, width)
    both = jnp.concatenate([gate_ref[:, units], up_ref[:, units]], axis=1)
    part_ref[:, : 2 * half] = matmul(rows, both, 1, 0).astype(BF16)
    part_ref[:, 2 * half :] = matmul(cots, down_ref[units, :], 1, 1).astype(BF16)


def give_kernel(slots, chunks, pieces, *refs):
    recv_refs = refs[:pieces]
    gate_ref, up_ref, down_ref, rows_ref, cots_ref, give_ref, wide, flat = refs[pieces:]
    group, block, width = wide.shape
    for s in range(group):
        recv_ref, start = (recv_refs[0], s * block) if pieces == 1 else (recv_refs[s], 0)
        wide[s] = recv_ref[start : start + block, :].astype(F32)
        for j in range(chunks):
            columns = pl.ds(j * width, width)
            for kind in range(2):
                place = (2 * j + kind) * slots
                flat[kind, s * slots : (s + 1) * slots, columns] = wide[s, place : place + slots, :]
    rows = flat[0].astype(BF16)
    cots = flat[1].astype(BF16)
    rows_ref[...] = rows
    cots_ref[...] = cots
    half_partials(1, rows, cots, gate_ref, up_ref, down_ref, give_ref)


def keep_kernel(rows_ref, cots_ref, gate_ref, up_ref, down_ref, keep_ref):
    half_partials(0, rows_ref[...], cots_ref[...], gate_ref, up_ref, down_ref, keep_ref)


def add_kernel(left_ref, right_ref, sum_ref):
    sum_ref[...] = (left_ref[...].astype(F32) + right_ref[...].astype(F32)).astype(BF16)


def activate_kernel(near_ref, far_ref, mine_ref):
    half = mine_ref.shape[1] // 3
    total = near_ref[...].astype(F32) + far_ref[...].astype(F32)
    gate_pre, up_pre, hidden_grad = (total[:, i * half : (i + 1) * half] for i in range(3))
    sigma = jax.nn.sigmoid(gate_pre)
    active = gate_pre * sigma
    slope = sigma * (1.0 + gate_pre * (1.0 - sigma))
    mine_ref[:, :half] = (active * up_pre).astype(BF16)
    mine_ref[:, half : 2 * half] = (hidden_grad * up_pre * slope).astype(BF16)
    mine_ref[:, 2 * half :] = (hidden_grad * active).astype(BF16)


def half_outputs(which, acts_ref, gate_ref, up_ref, down_ref):
    width = gate_ref.shape[1]
    half = width // 2
    units = half_columns(which, width)
    outs = matmul(acts_ref[:, :half], down_ref[units, :], 1, 0)
    both = jnp.concatenate([gate_ref[:, units], up_ref[:, units]], axis=1)
    return outs, matmul(acts_ref[:, half:], both, 1, 1)


def own_kernel(mine_ref, gate_ref, up_ref, down_ref, outs_ref, ins_ref):
    outs_ref[...], ins_ref[...] = half_outputs(0, mine_ref, gate_ref, up_ref, down_ref)


def back_kernel(slots, chunks, pieces, *refs):
    theirs_ref, outs_ref, ins_ref, gate_ref, up_ref, down_ref = refs[:6]
    back_refs = refs[6 : 6 + pieces]
    flat, wide = refs[6 + pieces :]
    group, block, width = wide.shape
    outs, ins = half_outputs(1, theirs_ref, gate_ref, up_ref, down_ref)
    flat[0] = outs_ref[...] + outs
    flat[1] = ins_ref[...] + ins
    if block > 2 * slots * chunks:
        wide[...] = jnp.zeros_like(wide)
    for s in range(group):
        for j in range(chunks):
            columns = pl.ds(j * width, width)
            for kind in range(2):
                place = (2 * j + kind) * slots
                wide[s, place : place + slots, :] = flat[kind, s * slots : (s + 1) * slots, columns]
        if pieces == 1:
            back_ref, start = back_refs[0], s * block
        else:
            back_ref, start = back_refs[BACK_ORDER.index(SEND_ORDER[s])], 0
        back_ref[start : start + block, :] = wide[s].astype(BF16)


def by_rows(kernel, name, steps, arrays, weights, outs, scratch=(), flops=0):
    def tiled(shape):
        return pl.BlockSpec((shape[0] // steps, shape[1]), lambda i: (i, 0))

    def whole(shape):
        return pl.BlockSpec(shape, lambda i: (0, 0))

    moved = sum(array.size * array.dtype.itemsize for array in (*arrays, *weights))
    results = pl.pallas_call(
        kernel,
        grid=(steps,),
        out_shape=tuple(jax.ShapeDtypeStruct(shape, dtype) for shape, dtype in outs),
        in_specs=[tiled(array.shape) for array in arrays] + [whole(w.shape) for w in weights],
        out_specs=tuple(tiled(shape) for shape, _ in outs),
        scratch_shapes=list(scratch),
        compiler_params=params(),
        cost_estimate=pl.CostEstimate(flops=flops, bytes_accessed=moved, transcendentals=0),
        name=name,
    )(*arrays, *weights)
    return results if len(outs) > 1 else results[0]


def grads_kernel(
    rows_ref, cots_ref, mine_ref, theirs_ref, gate_hbm, up_hbm, down_hbm, gate_ref, up_ref, down_ref, sems
):
    width = gate_ref.shape[1]
    half = width // 2
    copies = []

    def send(source, target, rows):
        copies.append(
            pltpu.make_async_copy(source.at[rows], target.at[rows], sems.at[len(copies)])
        )
        copies[-1].start()

    sides = [(mine_ref, half_columns(0, width)), (theirs_ref, half_columns(1, width))]
    for acts_ref, units in sides:
        for start, size in spans(half, CHUNK):
            rows = pl.ds(pl.multiple_of(units.start + start, 16), size)
            hidden = acts_ref[:, start : start + size]
            down_ref[rows, :] = matmul(hidden, cots_ref[...], 0, 0).astype(BF16)
            send(down_ref, down_hbm, rows)
    for place, out_ref, out_hbm in ((1, gate_ref, gate_hbm), (2, up_ref, up_hbm)):
        for start, size in spans(out_ref.shape[0], CHUNK):
            rows = pl.ds(start, size)
            for acts_ref, units in sides:
                grad = acts_ref[:, place * half : (place + 1) * half]
                out_ref[rows, units] = matmul(rows_ref[:, rows], grad, 0, 0).astype(BF16)
            send(out_ref, out_hbm, rows)
    for copy in copies:
        copy.wait()


def weight_grads(rows, cots, mine, theirs):
    total, feature = rows.shape
    width = 2 * mine.shape[1] // 3
    vmem = pl.BlockSpec(memory_space=pltpu.VMEM)
    hbm = pl.BlockSpec(memory_space=pltpu.HBM)
    shapes = ((feature, width), (feature, width), (width, feature))
    pieces = 2 * len(spans(feature, CHUNK)) + 2 * len(spans(width // 2, CHUNK))
    return pl.pallas_call(
        grads_kernel,
        out_shape=tuple(jax.ShapeDtypeStruct(shape, BF16) for shape in shapes),
        in_specs=[vmem] * 4,
        out_specs=(hbm,) * 3,
        scratch_shapes=[pltpu.VMEM(shape, BF16) for shape in shapes]
        + [pltpu.SemaphoreType.DMA((pieces,))],
        compiler_params=params(),
        cost_estimate=pl.CostEstimate(
            flops=6 * total * feature * width,
            bytes_accessed=6 * feature * width,
            transcendentals=0,
        ),
        name="weight_grads",
    )(rows, cots, mine, theirs)


def combine_kernel(columns, slots, chunks, pieces, *refs):
    back_refs = refs[:pieces]
    merge_ref, mixed_hbm, token_hbm, mixed_ref, token_ref, wide, flat, sems = refs[pieces:]
    if pieces > 1:
        flat[...] = jnp.zeros_like(flat)
        rows, width, block = 2 * slots, back_refs[0].shape[1], padded(2 * slots)
        for i, back_ref in enumerate(back_refs):
            wide[i] = back_ref[...].astype(F32)
            first = SEND_ORDER.index(BACK_ORDER[i]) * block
            for j in range(chunks):
                part = pl.ds(j * width, width)
                flat[first : first + rows, part] = wide[i, j * rows : (j + 1) * rows, :]
    count = mixed_ref.shape[0]
    copies = []
    for start, size in columns:
        part = pl.ds(start, size)
        back = back_refs[0][:, part] if pieces == 1 else flat[:, part].astype(BF16)
        sums = matmul(merge_ref[...], back, 1, 0)
        mixed_ref[:, part] = (sums[:count] + sums[count : 2 * count]).astype(BF16)
        token_ref[:, part] = sums[2 * count :].astype(BF16)
        for source, target in ((mixed_ref, mixed_hbm), (token_ref, token_hbm)):
            copies.append(
                pltpu.make_async_copy(
                    source.at[:, part], target.at[:, part], sems.at[len(copies)]
                )
            )
            copies[-1].start()
    for copy in copies:
        copy.wait()


def combine(backs, merge, slots, chunks):
    pieces, feature, count = len(backs), chunks * backs[0].shape[1], merge.shape[0] // 3
    columns = spans(feature, 2 * CHUNK if feature % CHUNK == 0 else feature)
    vmem = pl.BlockSpec(memory_space=pltpu.VMEM)
    hbm = pl.BlockSpec(memory_space=pltpu.HBM)
    shape = (count, feature)
    staged = [(pieces, *backs[0].shape), (merge.shape[1], feature)] if pieces > 1 else [(8, 128)] * 2
    return pl.pallas_call(
        functools.partial(combine_kernel, columns, slots, chunks, pieces),
        out_shape=(jax.ShapeDtypeStruct(shape, BF16),) * 2,
        in_specs=[vmem] * (pieces + 1),
        out_specs=(hbm, hbm),
        scratch_shapes=[
            pltpu.VMEM(shape, BF16),
            pltpu.VMEM(shape, BF16),
            *(pltpu.VMEM(extent, F32) for extent in staged),
            pltpu.SemaphoreType.DMA((2 * len(columns),)),
        ],
        compiler_params=params(),
        name="combine",
    )(*backs, merge)


def swapped(array, axis, distance):
    return lax.ppermute(array, axis, [(i, i ^ distance) for i in range(lax.axis_size(axis))])


def over_experts(arrays, experts, order):
    if len(arrays) == 1:
        array = arrays[0]
        blocks = array.reshape(experts, -1, array.shape[1])
        moved = lax.all_to_all(blocks, "expert", split_axis=0, concat_axis=0, tiled=True)
        return [moved.reshape(array.shape)]
    moved = [swapped(arrays[i], "expert", order[i]) for i in range(1, experts)]
    return [arrays[0]] + moved


def shards(
    tokens,
    out_grad,
    gate_weights,
    expert_ids,
    replica_plan,
    cap_blocks,
    gate_weight,
    up_weight,
    down_weight,
):
    experts = lax.axis_size("expert")
    hosts = replica_plan.shape[1]
    assert tokens.shape[0] % hosts == 0 and experts % GROUP == 0
    assert all(n >= 4 and n & (n - 1) == 0 for n in (experts, lax.axis_size("dp")))
    slots = OWN + SPARE * (hosts - 1)
    gate, up, down = gate_weight[0], up_weight[0], down_weight[0]
    feature, width = gate.shape
    pieces = experts if experts <= GROUP and feature % CHUNK == 0 else 1
    chunks = feature // CHUNK if pieces > 1 else 1
    block = 2 * slots * chunks if pieces > 1 else padded(2 * slots)
    sends, (scaled, pick) = dispatch(
        replica_plan,
        cap_blocks,
        expert_ids.T,
        gate_weights.T,
        tokens,
        out_grad,
        experts,
        slots,
        chunks,
        pieces,
    )
    recvs = over_experts(sends, experts, SEND_ORDER)
    *weights, merge = load_weights(gate, up, down, scaled, pick)
    steps, total, half = experts // GROUP, experts * slots, 3 * width // 2
    layout = (slots, chunks, pieces)
    flops = 3 * total * feature * width
    scratch = [
        pltpu.VMEM((GROUP, block, feature // chunks), F32),
        pltpu.VMEM((2, GROUP * slots, feature), F32),
    ]
    rows, cots, give = by_rows(
        functools.partial(give_kernel, *layout),
        "give",
        steps,
        recvs,
        weights,
        [((total, feature), BF16), ((total, feature), BF16), ((total, half), BF16)],
        scratch,
        flops,
    )
    got = swapped(give, "dp", 1)
    keep = by_rows(
        keep_kernel, "keep", steps, [rows, cots], weights, [((total, half), BF16)], (), flops
    )
    near = by_rows(add_kernel, "add", steps, [keep, got], [], [((total, half), BF16)])
    step, last = 2, lax.axis_size("dp") // 2
    while step < last:
        far = swapped(near, "dp", step)
        near = by_rows(add_kernel, "add", steps, [near, far], [], [((total, half), BF16)])
        step *= 2
    far = swapped(near, "dp", last)
    mine = by_rows(activate_kernel, "activate", steps, [near, far], [], [((total, half), BF16)])
    theirs = swapped(mine, "dp", 1)
    outs, ins = by_rows(
        own_kernel, "own", steps, [mine], weights, [((total, feature), F32)] * 2, (), flops
    )
    backs = by_rows(
        functools.partial(back_kernel, *layout),
        "back",
        steps,
        [theirs, outs, ins],
        weights,
        [((experts * block // pieces, feature // chunks), BF16)] * pieces,
        scratch[::-1],
        flops,
    )
    returned = over_experts(backs if pieces > 1 else [backs], experts, BACK_ORDER)
    gate_grad, up_grad, down_grad = weight_grads(rows, cots, mine, theirs)
    mixed, token_grad = combine(returned, merge, slots, chunks)
    return mixed, token_grad, gate_grad[None], up_grad[None], down_grad[None]


def solution(mesh):
    return jax.shard_map(
        shards,
        mesh=mesh,
        in_specs=(
            P(("groups", "expert"), "dp"),
            P(("groups", "expert"), "dp"),
            P(("groups", "expert"), None),
            P(("groups", "expert"), None),
            P("groups", None),
            P("groups"),
            P("expert", "dp", None),
            P("expert", "dp", None),
            P("expert", None, "dp"),
        ),
        out_specs=(
            P(("groups", "expert"), "dp"),
            P(("groups", "expert"), "dp"),
            P(("groups", "expert"), "dp", None),
            P(("groups", "expert"), "dp", None),
            P(("groups", "expert"), None, "dp"),
        ),
        check_vma=False,
    )
```

```python
import functools

import jax
import jax.numpy as jnp
from jax import lax
from jax.experimental import pallas as pl
from jax.experimental.pallas import tpu as pltpu
from jax.sharding import PartitionSpec as P

BLK = 4
MAXB = 2
SPARE = 2
OWN = BLK * MAXB
GROUP = 4
CHUNK = 128
LOADS = 4
VMEM_LIMIT = 32 * 1024 * 1024

BF16 = jnp.bfloat16
F32 = jnp.float32
I32 = jnp.int32


def matmul(left, right, left_dim, right_dim):
    return lax.dot_general(
        left, right, (((left_dim,), (right_dim,)), ((), ())), preferred_element_type=F32
    )


def params():
    return pltpu.CompilerParams(vmem_limit_bytes=VMEM_LIMIT)


def in_hbm(array):
    return pltpu.with_memory_space_constraint(array, pltpu.HBM)


def spans(extent, size):
    return [(start, min(size, extent - start)) for start in range(0, extent, size)]


def padded(rows):
    return -(-rows // 8) * 8


def distance(index, experts):
    return (experts - index) % experts


def dispatch_kernel(experts, hosts, slots, chunks, pieces, *refs):
    plan_hbm, caps_hbm, ids_hbm, gates_hbm, tok_hbm, grad_hbm = refs[:6]
    send_refs = refs[6 : 6 + pieces]
    scaled_ref, pick_ref, plan_ref, caps_ref, ids_ref, gates_ref, both_ref, wide, sems = refs[6 + pieces :]
    choose, count = ids_ref.shape
    block = padded(2 * slots)
    pairs = [(ids_hbm, ids_ref), (plan_hbm, plan_ref), (caps_hbm, caps_ref), (gates_hbm, gates_ref)]
    for place, source in enumerate((tok_hbm, grad_hbm)):
        for start, size in spans(count, count // LOADS):
            target = both_ref.at[pl.ds(place * count + start, size)]
            pairs.append((source.at[pl.ds(start, size)], target))
    copies = [
        pltpu.make_async_copy(source, target, sems.at[i])
        for i, (source, target) in enumerate(pairs)
    ]
    for copy in copies:
        copy.start()
    me = lax.axis_index("expert")
    row = lax.broadcasted_iota(I32, (block, count), 0)
    col = lax.broadcasted_iota(I32, (block, count), 1)
    is_cot = row >= slots
    slot = jnp.where(is_cot, row - slots, row)
    valid = row < 2 * slots
    is_spare = slot >= OWN
    spare_slot = jnp.maximum(slot - OWN, 0)
    replica = jnp.where(is_spare, 1 + lax.div(spare_slot, SPARE), 0)
    position = jnp.where(is_spare, lax.rem(spare_slot, SPARE), slot)
    token_slot = lax.rem(col, hosts)
    earlier = (
        lax.broadcasted_iota(I32, (count, count), 0) < lax.broadcasted_iota(I32, (count, count), 1)
    )
    earlier = earlier.astype(F32).astype(BF16)
    cots = jnp.concatenate([is_cot.astype(F32)] * experts, axis=0)
    for copy in copies[:4]:
        copy.wait()
    members, weights, limits = [], [], []
    for index in range(experts):
        expert = index if pieces == 1 else me ^ distance(index, experts)
        hot = (plan_ref[0, 0] == expert) | (plan_ref[1, 0] == expert)
        wanted = token_slot * hot.astype(I32)
        here = jnp.zeros((1, count), F32)
        weight = jnp.zeros((1, count), F32)
        for k in range(choose):
            chosen = ids_ref[k : k + 1, :] == expert
            here = jnp.where(chosen, 1.0, here)
            weight = jnp.where(chosen, gates_ref[k : k + 1, :], weight)
        fits = valid & (replica == wanted)
        members.append(jnp.where(fits, jnp.broadcast_to(here, fits.shape), 0.0))
        weights.append(jnp.broadcast_to(weight, fits.shape))
        room = jnp.where(is_spare, SPARE, caps_ref[expert] * BLK)
        limits.append(jnp.where(position < room, position, -1))
    member = jnp.concatenate(members, axis=0)
    weight = jnp.concatenate(weights, axis=0)
    limit = jnp.concatenate(limits, axis=0).astype(F32)
    before = matmul(member.astype(BF16), earlier, 1, 0)
    taken = jnp.where(before == limit, member, 0.0)
    pick_cot = taken * cots
    pick_tok = taken - pick_cot
    picks = jnp.concatenate([pick_tok.astype(BF16), pick_cot.astype(BF16)], axis=1)
    gate = jnp.sum(pick_cot * weight, axis=1, keepdims=True)
    scale = jnp.where(cots[:, :1] > 0.0, gate, 1.0)
    scaled_ref[...] = pick_tok * weight
    pick_ref[...] = pick_cot
    for copy in copies[4:]:
        copy.wait()
    send = scale * matmul(picks, both_ref[...], 1, 0)
    if pieces == 1:
        send_refs[0][...] = send.astype(BF16)
        return
    width = send.shape[1] // chunks
    used = 2 * slots * chunks
    if wide.shape[0] > used:
        wide[used:, :] = jnp.zeros((wide.shape[0] - used, width), F32)
    for i, send_ref in enumerate(send_refs):
        for j in range(chunks):
            rows = send[i * block : i * block + 2 * slots, j * width : (j + 1) * width]
            wide[2 * slots * j : 2 * slots * (j + 1), :] = rows
        send_ref[...] = wide[...].astype(BF16)


def dispatch(plan, caps, ids, gates, tokens, grads, experts, slots, chunks, pieces):
    count, feature = tokens.shape
    vmem = pl.BlockSpec(memory_space=pltpu.VMEM)
    block = padded(2 * slots)
    packed = (padded(2 * slots * chunks), feature // chunks)
    sent = (experts * block, feature) if pieces == 1 else packed
    outs = pl.pallas_call(
        functools.partial(dispatch_kernel, experts, plan.shape[1], slots, chunks, pieces),
        out_shape=(jax.ShapeDtypeStruct(sent, BF16),) * pieces
        + (jax.ShapeDtypeStruct((experts * block, count), F32),) * 2,
        in_specs=[pl.BlockSpec(memory_space=pltpu.HBM)] * 6,
        out_specs=(vmem,) * (pieces + 2),
        scratch_shapes=[
            pltpu.SMEM(plan.shape, I32),
            pltpu.SMEM(caps.shape, I32),
            pltpu.VMEM(ids.shape, I32),
            pltpu.VMEM(gates.shape, F32),
            pltpu.VMEM((2 * count, feature), BF16),
            pltpu.VMEM(packed, F32),
            pltpu.SemaphoreType.DMA((4 + 2 * LOADS,)),
        ],
        compiler_params=params(),
        name="dispatch",
    )(*(in_hbm(array) for array in (plan, caps, ids, gates, tokens, grads)))
    return outs[:pieces], outs[pieces:]


def load_kernel(
    gate_hbm, up_hbm, down_hbm, scaled_ref, pick_ref, gate_ref, up_ref, down_ref, merge_ref, sems
):
    copies = []
    for source, target in ((gate_hbm, gate_ref), (up_hbm, up_ref), (down_hbm, down_ref)):
        for start, size in spans(source.shape[0], source.shape[0] // LOADS):
            rows = pl.ds(start, size)
            copies.append(
                pltpu.make_async_copy(source.at[rows], target.at[rows], sems.at[len(copies)])
            )
    for copy in copies:
        copy.start()
    scaled = scaled_ref[...].T
    count = scaled.shape[0]
    high = scaled.astype(BF16)
    merge_ref[:count, :] = high
    merge_ref[count : 2 * count, :] = (scaled - high.astype(F32)).astype(BF16)
    merge_ref[2 * count :, :] = pick_ref[...].T.astype(BF16)
    for copy in copies:
        copy.wait()


def load_weights(gate, up, down, scaled, pick):
    hbm = pl.BlockSpec(memory_space=pltpu.HBM)
    vmem = pl.BlockSpec(memory_space=pltpu.VMEM)
    assert all(w.shape[0] % (16 * LOADS) == 0 for w in (gate, up, down))
    merge = jax.ShapeDtypeStruct((3 * pick.shape[1], pick.shape[0]), BF16)
    return pl.pallas_call(
        load_kernel,
        out_shape=tuple(pltpu.VMEM(w.shape, BF16) for w in (gate, up, down)) + (merge,),
        in_specs=[hbm, hbm, hbm, vmem, vmem],
        out_specs=(vmem,) * 4,
        scratch_shapes=[pltpu.SemaphoreType.DMA((3 * LOADS,))],
        compiler_params=params(),
        cost_estimate=pl.CostEstimate(
            flops=0, bytes_accessed=2 * 3 * gate.size * 2, transcendentals=0
        ),
        name="load_weights",
    )(in_hbm(gate), in_hbm(up), in_hbm(down), scaled, pick)


def half_columns(which, width):
    half = width // 2
    side = lax.rem(lax.axis_index("dp") + which, 2)
    return pl.ds(pl.multiple_of(side * half, half), half)


def half_partials(which, rows, cots, gate_ref, up_ref, down_ref, part_ref):
    width = gate_ref.shape[1]
    half = width // 2
    units = half_columns(which, width)
    both = jnp.concatenate([gate_ref[:, units], up_ref[:, units]], axis=1)
    part_ref[:, : 2 * half] = matmul(rows, both, 1, 0).astype(BF16)
    part_ref[:, 2 * half :] = matmul(cots, down_ref[units, :], 1, 1).astype(BF16)


def give_kernel(slots, chunks, pieces, *refs):
    recv_refs = refs[:pieces]
    gate_ref, up_ref, down_ref, rows_ref, cots_ref, give_ref, wide, flat = refs[pieces:]
    group, block, width = wide.shape
    for s in range(group):
        recv_ref, start = (recv_refs[0], s * block) if pieces == 1 else (recv_refs[s], 0)
        wide[s] = recv_ref[start : start + block, :].astype(F32)
        for j in range(chunks):
            columns = pl.ds(j * width, width)
            for kind in range(2):
                place = (2 * j + kind) * slots
                flat[kind, s * slots : (s + 1) * slots, columns] = wide[s, place : place + slots, :]
    rows = flat[0].astype(BF16)
    cots = flat[1].astype(BF16)
    rows_ref[...] = rows
    cots_ref[...] = cots
    half_partials(1, rows, cots, gate_ref, up_ref, down_ref, give_ref)


def keep_kernel(rows_ref, cots_ref, gate_ref, up_ref, down_ref, keep_ref):
    half_partials(0, rows_ref[...], cots_ref[...], gate_ref, up_ref, down_ref, keep_ref)


def add_kernel(left_ref, right_ref, sum_ref):
    sum_ref[...] = (left_ref[...].astype(F32) + right_ref[...].astype(F32)).astype(BF16)


def activate_kernel(near_ref, far_ref, mine_ref):
    half = mine_ref.shape[1] // 3
    total = near_ref[...].astype(F32) + far_ref[...].astype(F32)
    gate_pre, up_pre, hidden_grad = (total[:, i * half : (i + 1) * half] for i in range(3))
    sigma = jax.nn.sigmoid(gate_pre)
    active = gate_pre * sigma
    slope = sigma * (1.0 + gate_pre * (1.0 - sigma))
    mine_ref[:, :half] = (active * up_pre).astype(BF16)
    mine_ref[:, half : 2 * half] = (hidden_grad * up_pre * slope).astype(BF16)
    mine_ref[:, 2 * half :] = (hidden_grad * active).astype(BF16)


def half_outputs(which, acts_ref, gate_ref, up_ref, down_ref):
    width = gate_ref.shape[1]
    half = width // 2
    units = half_columns(which, width)
    outs = matmul(acts_ref[:, :half], down_ref[units, :], 1, 0)
    both = jnp.concatenate([gate_ref[:, units], up_ref[:, units]], axis=1)
    return outs, matmul(acts_ref[:, half:], both, 1, 1)


def own_kernel(mine_ref, gate_ref, up_ref, down_ref, outs_ref, ins_ref):
    outs_ref[...], ins_ref[...] = half_outputs(0, mine_ref, gate_ref, up_ref, down_ref)


def back_kernel(slots, chunks, pieces, *refs):
    theirs_ref, outs_ref, ins_ref, gate_ref, up_ref, down_ref = refs[:6]
    back_refs = refs[6 : 6 + pieces]
    flat, wide = refs[6 + pieces :]
    group, block, width = wide.shape
    outs, ins = half_outputs(1, theirs_ref, gate_ref, up_ref, down_ref)
    flat[0] = outs_ref[...] + outs
    flat[1] = ins_ref[...] + ins
    used = 2 * slots * chunks
    if block > used:
        wide[:, used:, :] = jnp.zeros((group, block - used, width), F32)
    for s in range(group):
        for j in range(chunks):
            columns = pl.ds(j * width, width)
            for kind in range(2):
                place = (2 * j + kind) * slots
                wide[s, place : place + slots, :] = flat[kind, s * slots : (s + 1) * slots, columns]
        back_ref, start = (back_refs[0], s * block) if pieces == 1 else (back_refs[s], 0)
        back_ref[start : start + block, :] = wide[s].astype(BF16)


def by_rows(kernel, name, steps, arrays, weights, outs, scratch=(), flops=0):
    def tiled(shape):
        return pl.BlockSpec((shape[0] // steps, shape[1]), lambda i: (i, 0))

    def whole(shape):
        return pl.BlockSpec(shape, lambda i: (0, 0))

    moved = sum(array.size * array.dtype.itemsize for array in (*arrays, *weights))
    results = pl.pallas_call(
        kernel,
        grid=(steps,),
        out_shape=tuple(jax.ShapeDtypeStruct(shape, dtype) for shape, dtype in outs),
        in_specs=[tiled(array.shape) for array in arrays] + [whole(w.shape) for w in weights],
        out_specs=tuple(tiled(shape) for shape, _ in outs),
        scratch_shapes=list(scratch),
        compiler_params=params(),
        cost_estimate=pl.CostEstimate(flops=flops, bytes_accessed=moved, transcendentals=0),
        name=name,
    )(*arrays, *weights)
    return results if len(outs) > 1 else results[0]


def grads_kernel(
    rows_ref, cots_ref, mine_ref, theirs_ref, gate_hbm, up_hbm, down_hbm, gate_ref, up_ref, down_ref, sems
):
    width = gate_ref.shape[1]
    half = width // 2
    copies = []

    def send(source, target, rows):
        copies.append(
            pltpu.make_async_copy(source.at[rows], target.at[rows], sems.at[len(copies)])
        )
        copies[-1].start()

    sides = [(mine_ref, half_columns(0, width)), (theirs_ref, half_columns(1, width))]
    for acts_ref, units in sides:
        for start, size in spans(half, CHUNK):
            rows = pl.ds(pl.multiple_of(units.start + start, 16), size)
            hidden = acts_ref[:, start : start + size]
            down_ref[rows, :] = matmul(hidden, cots_ref[...], 0, 0).astype(BF16)
            send(down_ref, down_hbm, rows)
    for place, out_ref, out_hbm in ((1, gate_ref, gate_hbm), (2, up_ref, up_hbm)):
        for start, size in spans(out_ref.shape[0], CHUNK):
            rows = pl.ds(start, size)
            for acts_ref, units in sides:
                grad = acts_ref[:, place * half : (place + 1) * half]
                out_ref[rows, units] = matmul(rows_ref[:, rows], grad, 0, 0).astype(BF16)
            send(out_ref, out_hbm, rows)
    for copy in copies:
        copy.wait()


def weight_grads(rows, cots, mine, theirs):
    total, feature = rows.shape
    width = 2 * mine.shape[1] // 3
    vmem = pl.BlockSpec(memory_space=pltpu.VMEM)
    hbm = pl.BlockSpec(memory_space=pltpu.HBM)
    shapes = ((feature, width), (feature, width), (width, feature))
    pieces = 2 * len(spans(feature, CHUNK)) + 2 * len(spans(width // 2, CHUNK))
    return pl.pallas_call(
        grads_kernel,
        out_shape=tuple(jax.ShapeDtypeStruct(shape, BF16) for shape in shapes),
        in_specs=[vmem] * 4,
        out_specs=(hbm,) * 3,
        scratch_shapes=[pltpu.VMEM(shape, BF16) for shape in shapes]
        + [pltpu.SemaphoreType.DMA((pieces,))],
        compiler_params=params(),
        cost_estimate=pl.CostEstimate(
            flops=6 * total * feature * width,
            bytes_accessed=6 * feature * width,
            transcendentals=0,
        ),
        name="weight_grads",
    )(rows, cots, mine, theirs)


def combine_kernel(columns, slots, chunks, pieces, *refs):
    back_refs = refs[:pieces]
    merge_ref, mixed_hbm, token_hbm, mixed_ref, token_ref, wide, flat, sems = refs[pieces:]
    if pieces > 1:
        rows, width, block = 2 * slots, back_refs[0].shape[1], padded(2 * slots)
        for i, back_ref in enumerate(back_refs):
            wide[i] = back_ref[...].astype(F32)
            if block > rows:
                gap = pl.ds(i * block + rows, block - rows)
                flat[gap, :] = jnp.zeros((block - rows, flat.shape[1]), F32)
            for j in range(chunks):
                part = pl.ds(j * width, width)
                flat[i * block : i * block + rows, part] = wide[i, j * rows : (j + 1) * rows, :]
    count = mixed_ref.shape[0]
    copies = []
    for start, size in columns:
        part = pl.ds(start, size)
        back = back_refs[0][:, part] if pieces == 1 else flat[:, part].astype(BF16)
        sums = matmul(merge_ref[...], back, 1, 0)
        mixed_ref[:, part] = (sums[:count] + sums[count : 2 * count]).astype(BF16)
        token_ref[:, part] = sums[2 * count :].astype(BF16)
        for source, target in ((mixed_ref, mixed_hbm), (token_ref, token_hbm)):
            copies.append(
                pltpu.make_async_copy(
                    source.at[:, part], target.at[:, part], sems.at[len(copies)]
                )
            )
            copies[-1].start()
    for copy in copies:
        copy.wait()


def combine(backs, merge, slots, chunks):
    pieces, feature, count = len(backs), chunks * backs[0].shape[1], merge.shape[0] // 3
    columns = spans(feature, 2 * CHUNK if feature % CHUNK == 0 else feature)
    vmem = pl.BlockSpec(memory_space=pltpu.VMEM)
    hbm = pl.BlockSpec(memory_space=pltpu.HBM)
    shape = (count, feature)
    staged = [(pieces, *backs[0].shape), (merge.shape[1], feature)] if pieces > 1 else [(8, 128)] * 2
    return pl.pallas_call(
        functools.partial(combine_kernel, columns, slots, chunks, pieces),
        out_shape=(jax.ShapeDtypeStruct(shape, BF16),) * 2,
        in_specs=[vmem] * (pieces + 1),
        out_specs=(hbm, hbm),
        scratch_shapes=[
            pltpu.VMEM(shape, BF16),
            pltpu.VMEM(shape, BF16),
            *(pltpu.VMEM(extent, F32) for extent in staged),
            pltpu.SemaphoreType.DMA((2 * len(columns),)),
        ],
        compiler_params=params(),
        name="combine",
    )(*backs, merge)


def swapped(array, axis, distance):
    return lax.ppermute(array, axis, [(i, i ^ distance) for i in range(lax.axis_size(axis))])


def over_experts(arrays, experts):
    if len(arrays) == 1:
        array = arrays[0]
        blocks = array.reshape(experts, -1, array.shape[1])
        moved = lax.all_to_all(blocks, "expert", split_axis=0, concat_axis=0, tiled=True)
        return [moved.reshape(array.shape)]
    moved = [swapped(arrays[i], "expert", distance(i, experts)) for i in range(1, experts)]
    return [arrays[0]] + moved


def shards(
    tokens,
    out_grad,
    gate_weights,
    expert_ids,
    replica_plan,
    cap_blocks,
    gate_weight,
    up_weight,
    down_weight,
):
    experts = lax.axis_size("expert")
    hosts = replica_plan.shape[1]
    assert tokens.shape[0] % hosts == 0 and experts % GROUP == 0
    assert all(n >= 4 and n & (n - 1) == 0 for n in (experts, lax.axis_size("dp")))
    slots = OWN + SPARE * (hosts - 1)
    gate, up, down = gate_weight[0], up_weight[0], down_weight[0]
    feature, width = gate.shape
    pieces = experts if experts <= GROUP and feature % CHUNK == 0 else 1
    chunks = feature // CHUNK if pieces > 1 else 1
    block = padded(2 * slots * chunks)
    sends, (scaled, pick) = dispatch(
        replica_plan,
        cap_blocks,
        expert_ids.T,
        gate_weights.T,
        tokens,
        out_grad,
        experts,
        slots,
        chunks,
        pieces,
    )
    recvs = over_experts(sends, experts)
    *weights, merge = load_weights(gate, up, down, scaled, pick)
    steps, total, half = experts // GROUP, experts * slots, 3 * width // 2
    layout = (slots, chunks, pieces)
    flops = 3 * total * feature * width
    scratch = [
        pltpu.VMEM((GROUP, block, feature // chunks), F32),
        pltpu.VMEM((2, GROUP * slots, feature), F32),
    ]
    rows, cots, give = by_rows(
        functools.partial(give_kernel, *layout),
        "give",
        steps,
        recvs,
        weights,
        [((total, feature), BF16), ((total, feature), BF16), ((total, half), BF16)],
        scratch,
        flops,
    )
    got = swapped(give, "dp", 1)
    keep = by_rows(
        keep_kernel, "keep", steps, [rows, cots], weights, [((total, half), BF16)], (), flops
    )
    near = by_rows(add_kernel, "add", steps, [keep, got], [], [((total, half), BF16)])
    step, last = 2, lax.axis_size("dp") // 2
    while step < last:
        far = swapped(near, "dp", step)
        near = by_rows(add_kernel, "add", steps, [near, far], [], [((total, half), BF16)])
        step *= 2
    far = swapped(near, "dp", last)
    mine = by_rows(activate_kernel, "activate", steps, [near, far], [], [((total, half), BF16)])
    theirs = swapped(mine, "dp", 1)
    outs, ins = by_rows(
        own_kernel, "own", steps, [mine], weights, [((total, feature), F32)] * 2, (), flops
    )
    backs = by_rows(
        functools.partial(back_kernel, *layout),
        "back",
        steps,
        [theirs, outs, ins],
        weights,
        [((experts * block // pieces, feature // chunks), BF16)] * pieces,
        scratch[::-1],
        flops,
    )
    returned = over_experts(backs if pieces > 1 else [backs], experts)
    gate_grad, up_grad, down_grad = weight_grads(rows, cots, mine, theirs)
    mixed, token_grad = combine(returned, merge, slots, chunks)
    return mixed, token_grad, gate_grad[None], up_grad[None], down_grad[None]


def solution(mesh):
    return jax.shard_map(
        shards,
        mesh=mesh,
        in_specs=(
            P(("groups", "expert"), "dp"),
            P(("groups", "expert"), "dp"),
            P(("groups", "expert"), None),
            P(("groups", "expert"), None),
            P("groups", None),
            P("groups"),
            P("expert", "dp", None),
            P("expert", "dp", None),
            P("expert", None, "dp"),
        ),
        out_specs=(
            P(("groups", "expert"), "dp"),
            P(("groups", "expert"), "dp"),
            P(("groups", "expert"), "dp", None),
            P(("groups", "expert"), "dp", None),
            P(("groups", "expert"), None, "dp"),
        ),
        check_vma=False,
    )
```

```python
import functools

import jax
import jax.numpy as jnp
from jax import lax
from jax.experimental import pallas as pl
from jax.experimental.pallas import tpu as pltpu
from jax.sharding import PartitionSpec as P

BLK = 4
MAXB = 2
SPARE = 2
OWN = BLK * MAXB
GROUP = 4
CHUNK = 128
LOADS = 4
VMEM_LIMIT = 32 * 1024 * 1024

BF16 = jnp.bfloat16
F32 = jnp.float32
I32 = jnp.int32


def matmul(left, right, left_dim, right_dim):
    return lax.dot_general(
        left, right, (((left_dim,), (right_dim,)), ((), ())), preferred_element_type=F32
    )


def params():
    return pltpu.CompilerParams(vmem_limit_bytes=VMEM_LIMIT)


def in_hbm(array):
    return pltpu.with_memory_space_constraint(array, pltpu.HBM)


def spans(extent, size):
    return [(start, min(size, extent - start)) for start in range(0, extent, size)]


def padded(rows):
    return -(-rows // 8) * 8


def distance(index, experts):
    return (experts - index) % experts


def dispatch_kernel(experts, hosts, slots, chunks, pieces, *refs):
    plan_hbm, caps_hbm, ids_hbm, gates_hbm, tok_hbm, grad_hbm = refs[:6]
    send_refs = refs[6 : 6 + pieces]
    scaled_ref, pick_ref, plan_ref, caps_ref, ids_ref, gates_ref, both_ref, wide, sems = refs[6 + pieces :]
    choose, count = ids_ref.shape
    block = padded(2 * slots)
    pairs = [(ids_hbm, ids_ref), (plan_hbm, plan_ref), (caps_hbm, caps_ref), (gates_hbm, gates_ref)]
    for place, source in enumerate((tok_hbm, grad_hbm)):
        for start, size in spans(count, count // LOADS):
            target = both_ref.at[pl.ds(place * count + start, size)]
            pairs.append((source.at[pl.ds(start, size)], target))
    copies = [
        pltpu.make_async_copy(source, target, sems.at[i])
        for i, (source, target) in enumerate(pairs)
    ]
    for copy in copies:
        copy.start()
    me = lax.axis_index("expert")
    row = lax.broadcasted_iota(I32, (block, count), 0)
    col = lax.broadcasted_iota(I32, (block, count), 1)
    is_cot = row >= slots
    slot = jnp.where(is_cot, row - slots, row)
    valid = row < 2 * slots
    is_spare = slot >= OWN
    spare_slot = jnp.maximum(slot - OWN, 0)
    replica = jnp.where(is_spare, 1 + lax.div(spare_slot, SPARE), 0)
    position = jnp.where(is_spare, lax.rem(spare_slot, SPARE), slot)
    token_slot = lax.rem(col, hosts)
    earlier = (
        lax.broadcasted_iota(I32, (count, count), 0) < lax.broadcasted_iota(I32, (count, count), 1)
    )
    earlier = earlier.astype(F32).astype(BF16)
    cots = jnp.concatenate([is_cot.astype(F32)] * experts, axis=0)
    for copy in copies[:4]:
        copy.wait()
    members, weights, limits = [], [], []
    for index in range(experts):
        expert = index if pieces == 1 else me ^ distance(index, experts)
        hot = (plan_ref[0, 0] == expert) | (plan_ref[1, 0] == expert)
        wanted = token_slot * hot.astype(I32)
        here = jnp.zeros((1, count), F32)
        weight = jnp.zeros((1, count), F32)
        for k in range(choose):
            chosen = ids_ref[k : k + 1, :] == expert
            here = jnp.where(chosen, 1.0, here)
            weight = jnp.where(chosen, gates_ref[k : k + 1, :], weight)
        fits = valid & (replica == wanted)
        members.append(jnp.where(fits, jnp.broadcast_to(here, fits.shape), 0.0))
        weights.append(jnp.broadcast_to(weight, fits.shape))
        room = jnp.where(is_spare, SPARE, caps_ref[expert] * BLK)
        limits.append(jnp.where(position < room, position, -1))
    member = jnp.concatenate(members, axis=0)
    weight = jnp.concatenate(weights, axis=0)
    limit = jnp.concatenate(limits, axis=0).astype(F32)
    before = matmul(member.astype(BF16), earlier, 1, 0)
    taken = jnp.where(before == limit, member, 0.0)
    pick_cot = taken * cots
    pick_tok = taken - pick_cot
    picks = jnp.concatenate([pick_tok.astype(BF16), pick_cot.astype(BF16)], axis=1)
    gate = jnp.sum(pick_cot * weight, axis=1, keepdims=True)
    scale = jnp.where(cots[:, :1] > 0.0, gate, 1.0)
    scaled_ref[...] = pick_tok * weight
    pick_ref[...] = pick_cot
    for copy in copies[4:]:
        copy.wait()
    send = scale * matmul(picks, both_ref[...], 1, 0)
    if pieces == 1:
        send_refs[0][...] = send.astype(BF16)
        return
    width = send.shape[1] // chunks
    used = 2 * slots * chunks
    if wide.shape[0] > used:
        wide[used:, :] = jnp.zeros((wide.shape[0] - used, width), F32)
    for i, send_ref in enumerate(send_refs):
        for j in range(chunks):
            rows = send[i * block : i * block + 2 * slots, j * width : (j + 1) * width]
            wide[2 * slots * j : 2 * slots * (j + 1), :] = rows
        send_ref[...] = wide[...].astype(BF16)


def dispatch(plan, caps, ids, gates, tokens, grads, experts, slots, chunks, pieces):
    count, feature = tokens.shape
    vmem = pl.BlockSpec(memory_space=pltpu.VMEM)
    block = padded(2 * slots)
    packed = (padded(2 * slots * chunks), feature // chunks)
    sent = (experts * block, feature) if pieces == 1 else packed
    outs = pl.pallas_call(
        functools.partial(dispatch_kernel, experts, plan.shape[1], slots, chunks, pieces),
        out_shape=(jax.ShapeDtypeStruct(sent, BF16),) * pieces
        + (jax.ShapeDtypeStruct((experts * block, count), F32),) * 2,
        in_specs=[pl.BlockSpec(memory_space=pltpu.HBM)] * 6,
        out_specs=(vmem,) * (pieces + 2),
        scratch_shapes=[
            pltpu.SMEM(plan.shape, I32),
            pltpu.SMEM(caps.shape, I32),
            pltpu.VMEM(ids.shape, I32),
            pltpu.VMEM(gates.shape, F32),
            pltpu.VMEM((2 * count, feature), BF16),
            pltpu.VMEM(packed, F32),
            pltpu.SemaphoreType.DMA((4 + 2 * LOADS,)),
        ],
        compiler_params=params(),
        name="dispatch",
    )(*(in_hbm(array) for array in (plan, caps, ids, gates, tokens, grads)))
    return outs[:pieces], outs[pieces:]


def load_kernel(
    gate_hbm, up_hbm, down_hbm, scaled_ref, pick_ref, gate_ref, up_ref, down_ref, merge_ref, sems
):
    copies = []
    for source, target in ((gate_hbm, gate_ref), (up_hbm, up_ref), (down_hbm, down_ref)):
        for start, size in spans(source.shape[0], source.shape[0] // LOADS):
            rows = pl.ds(start, size)
            copies.append(
                pltpu.make_async_copy(source.at[rows], target.at[rows], sems.at[len(copies)])
            )
    for copy in copies:
        copy.start()
    scaled = scaled_ref[...].T
    count = scaled.shape[0]
    high = scaled.astype(BF16)
    merge_ref[:count, :] = high
    merge_ref[count : 2 * count, :] = (scaled - high.astype(F32)).astype(BF16)
    merge_ref[2 * count :, :] = pick_ref[...].T.astype(BF16)
    for copy in copies:
        copy.wait()


def load_weights(gate, up, down, scaled, pick):
    hbm = pl.BlockSpec(memory_space=pltpu.HBM)
    vmem = pl.BlockSpec(memory_space=pltpu.VMEM)
    assert all(w.shape[0] % (16 * LOADS) == 0 for w in (gate, up, down))
    merge = jax.ShapeDtypeStruct((3 * pick.shape[1], pick.shape[0]), BF16)
    return pl.pallas_call(
        load_kernel,
        out_shape=tuple(pltpu.VMEM(w.shape, BF16) for w in (gate, up, down)) + (merge,),
        in_specs=[hbm, hbm, hbm, vmem, vmem],
        out_specs=(vmem,) * 4,
        scratch_shapes=[pltpu.SemaphoreType.DMA((3 * LOADS,))],
        compiler_params=params(),
        cost_estimate=pl.CostEstimate(
            flops=0, bytes_accessed=2 * 3 * gate.size * 2, transcendentals=0
        ),
        name="load_weights",
    )(in_hbm(gate), in_hbm(up), in_hbm(down), scaled, pick)


def half_columns(which, width):
    half = width // 2
    side = lax.rem(lax.axis_index("dp") + which, 2)
    return pl.ds(pl.multiple_of(side * half, half), half)


def half_partials(which, rows, cots, gate_ref, up_ref, down_ref, part_ref):
    width = gate_ref.shape[1]
    half = width // 2
    units = half_columns(which, width)
    both = jnp.concatenate([gate_ref[:, units], up_ref[:, units]], axis=1)
    part_ref[:, : 2 * half] = matmul(rows, both, 1, 0).astype(BF16)
    part_ref[:, 2 * half :] = matmul(cots, down_ref[units, :], 1, 1).astype(BF16)


def give_kernel(slots, chunks, pieces, *refs):
    recv_refs = refs[:pieces]
    gate_ref, up_ref, down_ref, rows_ref, cots_ref, give_ref, wide, flat = refs[pieces:]
    group, block, width = wide.shape
    for s in range(group):
        recv_ref, start = (recv_refs[0], s * block) if pieces == 1 else (recv_refs[s], 0)
        wide[s] = recv_ref[start : start + block, :].astype(F32)
        for j in range(chunks):
            columns = pl.ds(j * width, width)
            for kind in range(2):
                place = (2 * j + kind) * slots
                flat[kind, s * slots : (s + 1) * slots, columns] = wide[s, place : place + slots, :]
    rows = flat[0].astype(BF16)
    cots = flat[1].astype(BF16)
    rows_ref[...] = rows
    cots_ref[...] = cots
    half_partials(1, rows, cots, gate_ref, up_ref, down_ref, give_ref)


def keep_kernel(rows_ref, cots_ref, gate_ref, up_ref, down_ref, keep_ref):
    half_partials(0, rows_ref[...], cots_ref[...], gate_ref, up_ref, down_ref, keep_ref)


def add_kernel(left_ref, right_ref, sum_ref):
    sum_ref[...] = (left_ref[...].astype(F32) + right_ref[...].astype(F32)).astype(BF16)


def activate_kernel(near_ref, far_ref, mine_ref):
    half = mine_ref.shape[1] // 3
    total = near_ref[...].astype(F32) + far_ref[...].astype(F32)
    gate_pre, up_pre, hidden_grad = (total[:, i * half : (i + 1) * half] for i in range(3))
    sigma = jax.nn.sigmoid(gate_pre)
    active = gate_pre * sigma
    slope = sigma * (1.0 + gate_pre * (1.0 - sigma))
    mine_ref[:, :half] = (active * up_pre).astype(BF16)
    mine_ref[:, half : 2 * half] = (hidden_grad * up_pre * slope).astype(BF16)
    mine_ref[:, 2 * half :] = (hidden_grad * active).astype(BF16)


def half_outputs(which, acts_ref, gate_ref, up_ref, down_ref):
    width = gate_ref.shape[1]
    half = width // 2
    units = half_columns(which, width)
    outs = matmul(acts_ref[:, :half], down_ref[units, :], 1, 0)
    both = jnp.concatenate([gate_ref[:, units], up_ref[:, units]], axis=1)
    return outs, matmul(acts_ref[:, half:], both, 1, 1)


def own_kernel(mine_ref, gate_ref, up_ref, down_ref, outs_ref, ins_ref):
    outs_ref[...], ins_ref[...] = half_outputs(0, mine_ref, gate_ref, up_ref, down_ref)


def back_kernel(slots, chunks, pieces, *refs):
    theirs_ref, outs_ref, ins_ref, gate_ref, up_ref, down_ref = refs[:6]
    back_refs = refs[6 : 6 + pieces]
    flat, wide = refs[6 + pieces :]
    group, block, width = wide.shape
    outs, ins = half_outputs(1, theirs_ref, gate_ref, up_ref, down_ref)
    flat[0] = outs_ref[...] + outs
    flat[1] = ins_ref[...] + ins
    used = 2 * slots * chunks
    if block > used:
        wide[:, used:, :] = jnp.zeros((group, block - used, width), F32)
    for s in range(group):
        for j in range(chunks):
            columns = pl.ds(j * width, width)
            for kind in range(2):
                place = (2 * j + kind) * slots
                wide[s, place : place + slots, :] = flat[kind, s * slots : (s + 1) * slots, columns]
        back_ref, start = (back_refs[0], s * block) if pieces == 1 else (back_refs[s], 0)
        back_ref[start : start + block, :] = wide[s].astype(BF16)


def by_rows(kernel, name, steps, arrays, weights, outs, scratch=(), flops=0):
    def tiled(shape):
        return pl.BlockSpec((shape[0] // steps, shape[1]), lambda i: (i, 0))

    def whole(shape):
        return pl.BlockSpec(shape, lambda i: (0, 0))

    moved = sum(array.size * array.dtype.itemsize for array in (*arrays, *weights))
    results = pl.pallas_call(
        kernel,
        grid=(steps,),
        out_shape=tuple(jax.ShapeDtypeStruct(shape, dtype) for shape, dtype in outs),
        in_specs=[tiled(array.shape) for array in arrays] + [whole(w.shape) for w in weights],
        out_specs=tuple(tiled(shape) for shape, _ in outs),
        scratch_shapes=list(scratch),
        compiler_params=params(),
        cost_estimate=pl.CostEstimate(flops=flops, bytes_accessed=moved, transcendentals=0),
        name=name,
    )(*arrays, *weights)
    return results if len(outs) > 1 else results[0]


def grads_kernel(
    rows_ref, cots_ref, mine_ref, theirs_ref, gate_hbm, up_hbm, down_hbm, gate_ref, up_ref, down_ref, sems
):
    width = gate_ref.shape[1]
    half = width // 2
    copies = []

    def send(source, target, rows):
        copies.append(
            pltpu.make_async_copy(source.at[rows], target.at[rows], sems.at[len(copies)])
        )
        copies[-1].start()

    sides = [(mine_ref, half_columns(0, width)), (theirs_ref, half_columns(1, width))]
    for acts_ref, units in sides:
        for start, size in spans(half, CHUNK):
            rows = pl.ds(pl.multiple_of(units.start + start, 16), size)
            hidden = acts_ref[:, start : start + size]
            down_ref[rows, :] = matmul(hidden, cots_ref[...], 0, 0).astype(BF16)
            send(down_ref, down_hbm, rows)
    for start, size in spans(gate_ref.shape[0], CHUNK):
        rows = pl.ds(start, size)
        for acts_ref, units in sides:
            grads = matmul(rows_ref[:, rows], acts_ref[:, half:], 0, 0).astype(BF16)
            gate_ref[rows, units] = grads[:, :half]
            up_ref[rows, units] = grads[:, half:]
        send(gate_ref, gate_hbm, rows)
        send(up_ref, up_hbm, rows)
    for copy in copies:
        copy.wait()


def weight_grads(rows, cots, mine, theirs):
    total, feature = rows.shape
    width = 2 * mine.shape[1] // 3
    vmem = pl.BlockSpec(memory_space=pltpu.VMEM)
    hbm = pl.BlockSpec(memory_space=pltpu.HBM)
    shapes = ((feature, width), (feature, width), (width, feature))
    pieces = 2 * len(spans(feature, CHUNK)) + 2 * len(spans(width // 2, CHUNK))
    return pl.pallas_call(
        grads_kernel,
        out_shape=tuple(jax.ShapeDtypeStruct(shape, BF16) for shape in shapes),
        in_specs=[vmem] * 4,
        out_specs=(hbm,) * 3,
        scratch_shapes=[pltpu.VMEM(shape, BF16) for shape in shapes]
        + [pltpu.SemaphoreType.DMA((pieces,))],
        compiler_params=params(),
        cost_estimate=pl.CostEstimate(
            flops=6 * total * feature * width,
            bytes_accessed=6 * feature * width,
            transcendentals=0,
        ),
        name="weight_grads",
    )(rows, cots, mine, theirs)


def combine_kernel(columns, slots, chunks, pieces, *refs):
    back_refs = refs[:pieces]
    merge_ref, mixed_hbm, token_hbm, mixed_ref, token_ref, wide, flat, sems = refs[pieces:]
    if pieces > 1:
        rows, width, block = 2 * slots, back_refs[0].shape[1], padded(2 * slots)
        for i, back_ref in enumerate(back_refs):
            wide[i] = back_ref[...].astype(F32)
            if block > rows:
                gap = pl.ds(i * block + rows, block - rows)
                flat[gap, :] = jnp.zeros((block - rows, flat.shape[1]), F32)
            for j in range(chunks):
                part = pl.ds(j * width, width)
                flat[i * block : i * block + rows, part] = wide[i, j * rows : (j + 1) * rows, :]
    count = mixed_ref.shape[0]
    copies = []
    for start, size in columns:
        part = pl.ds(start, size)
        back = back_refs[0][:, part] if pieces == 1 else flat[:, part].astype(BF16)
        sums = matmul(merge_ref[...], back, 1, 0)
        mixed_ref[:, part] = (sums[:count] + sums[count : 2 * count]).astype(BF16)
        token_ref[:, part] = sums[2 * count :].astype(BF16)
        for source, target in ((mixed_ref, mixed_hbm), (token_ref, token_hbm)):
            copies.append(
                pltpu.make_async_copy(
                    source.at[:, part], target.at[:, part], sems.at[len(copies)]
                )
            )
            copies[-1].start()
    for copy in copies:
        copy.wait()


def combine(backs, merge, slots, chunks):
    pieces, feature, count = len(backs), chunks * backs[0].shape[1], merge.shape[0] // 3
    columns = spans(feature, 2 * CHUNK if feature % CHUNK == 0 else feature)
    vmem = pl.BlockSpec(memory_space=pltpu.VMEM)
    hbm = pl.BlockSpec(memory_space=pltpu.HBM)
    shape = (count, feature)
    staged = [(pieces, *backs[0].shape), (merge.shape[1], feature)] if pieces > 1 else [(8, 128)] * 2
    return pl.pallas_call(
        functools.partial(combine_kernel, columns, slots, chunks, pieces),
        out_shape=(jax.ShapeDtypeStruct(shape, BF16),) * 2,
        in_specs=[vmem] * (pieces + 1),
        out_specs=(hbm, hbm),
        scratch_shapes=[
            pltpu.VMEM(shape, BF16),
            pltpu.VMEM(shape, BF16),
            *(pltpu.VMEM(extent, F32) for extent in staged),
            pltpu.SemaphoreType.DMA((2 * len(columns),)),
        ],
        compiler_params=params(),
        name="combine",
    )(*backs, merge)


def swapped(array, axis, distance):
    return lax.ppermute(array, axis, [(i, i ^ distance) for i in range(lax.axis_size(axis))])


def over_experts(arrays, experts):
    if len(arrays) == 1:
        array = arrays[0]
        blocks = array.reshape(experts, -1, array.shape[1])
        moved = lax.all_to_all(blocks, "expert", split_axis=0, concat_axis=0, tiled=True)
        return [moved.reshape(array.shape)]
    moved = [swapped(arrays[i], "expert", distance(i, experts)) for i in range(1, experts)]
    return [arrays[0]] + moved


def shards(
    tokens,
    out_grad,
    gate_weights,
    expert_ids,
    replica_plan,
    cap_blocks,
    gate_weight,
    up_weight,
    down_weight,
):
    experts = lax.axis_size("expert")
    hosts = replica_plan.shape[1]
    assert tokens.shape[0] % hosts == 0 and experts % GROUP == 0
    assert all(n >= 4 and n & (n - 1) == 0 for n in (experts, lax.axis_size("dp")))
    slots = OWN + SPARE * (hosts - 1)
    gate, up, down = gate_weight[0], up_weight[0], down_weight[0]
    feature, width = gate.shape
    pieces = experts if experts <= GROUP and feature % CHUNK == 0 else 1
    chunks = feature // CHUNK if pieces > 1 else 1
    block = padded(2 * slots * chunks)
    sends, (scaled, pick) = dispatch(
        replica_plan,
        cap_blocks,
        expert_ids.T,
        gate_weights.T,
        tokens,
        out_grad,
        experts,
        slots,
        chunks,
        pieces,
    )
    recvs = over_experts(sends, experts)
    *weights, merge = load_weights(gate, up, down, scaled, pick)
    steps, total, half = experts // GROUP, experts * slots, 3 * width // 2
    layout = (slots, chunks, pieces)
    flops = 3 * total * feature * width
    scratch = [
        pltpu.VMEM((GROUP, block, feature // chunks), F32),
        pltpu.VMEM((2, GROUP * slots, feature), F32),
    ]
    rows, cots, give = by_rows(
        functools.partial(give_kernel, *layout),
        "give",
        steps,
        recvs,
        weights,
        [((total, feature), BF16), ((total, feature), BF16), ((total, half), BF16)],
        scratch,
        flops,
    )
    got = swapped(give, "dp", 1)
    keep = by_rows(
        keep_kernel, "keep", steps, [rows, cots], weights, [((total, half), BF16)], (), flops
    )
    near = by_rows(add_kernel, "add", steps, [keep, got], [], [((total, half), BF16)])
    step, last = 2, lax.axis_size("dp") // 2
    while step < last:
        far = swapped(near, "dp", step)
        near = by_rows(add_kernel, "add", steps, [near, far], [], [((total, half), BF16)])
        step *= 2
    far = swapped(near, "dp", last)
    mine = by_rows(activate_kernel, "activate", steps, [near, far], [], [((total, half), BF16)])
    theirs = swapped(mine, "dp", 1)
    outs, ins = by_rows(
        own_kernel, "own", steps, [mine], weights, [((total, feature), F32)] * 2, (), flops
    )
    backs = by_rows(
        functools.partial(back_kernel, *layout),
        "back",
        steps,
        [theirs, outs, ins],
        weights,
        [((experts * block // pieces, feature // chunks), BF16)] * pieces,
        scratch[::-1],
        flops,
    )
    returned = over_experts(backs if pieces > 1 else [backs], experts)
    gate_grad, up_grad, down_grad = weight_grads(rows, cots, mine, theirs)
    mixed, token_grad = combine(returned, merge, slots, chunks)
    return mixed, token_grad, gate_grad[None], up_grad[None], down_grad[None]


def solution(mesh):
    return jax.shard_map(
        shards,
        mesh=mesh,
        in_specs=(
            P(("groups", "expert"), "dp"),
            P(("groups", "expert"), "dp"),
            P(("groups", "expert"), None),
            P(("groups", "expert"), None),
            P("groups", None),
            P("groups"),
            P("expert", "dp", None),
            P("expert", "dp", None),
            P("expert", None, "dp"),
        ),
        out_specs=(
            P(("groups", "expert"), "dp"),
            P(("groups", "expert"), "dp"),
            P(("groups", "expert"), "dp", None),
            P(("groups", "expert"), "dp", None),
            P(("groups", "expert"), None, "dp"),
        ),
        check_vma=False,
    )
```

```python
import functools

import jax
import jax.numpy as jnp
from jax import lax
from jax.experimental import pallas as pl
from jax.experimental.pallas import tpu as pltpu
from jax.sharding import PartitionSpec as P

BLK = 4
MAXB = 2
SPARE = 2
OWN = BLK * MAXB
GROUP = 4
CHUNK = 128
LOADS = 4
VMEM_LIMIT = 32 * 1024 * 1024

BF16 = jnp.bfloat16
F32 = jnp.float32
I32 = jnp.int32


def matmul(left, right, left_dim, right_dim):
    return lax.dot_general(
        left, right, (((left_dim,), (right_dim,)), ((), ())), preferred_element_type=F32
    )


def params():
    return pltpu.CompilerParams(vmem_limit_bytes=VMEM_LIMIT)


def in_hbm(array):
    return pltpu.with_memory_space_constraint(array, pltpu.HBM)


def spans(extent, size):
    return [(start, min(size, extent - start)) for start in range(0, extent, size)]


def padded(rows):
    return -(-rows // 8) * 8


def distance(index, experts):
    return (experts - index) % experts


def dispatch_kernel(experts, hosts, slots, chunks, pieces, *refs):
    plan_hbm, caps_hbm, ids_hbm, gates_hbm, tok_hbm, grad_hbm = refs[:6]
    send_refs = refs[6 : 6 + pieces]
    scaled_ref, pick_ref, plan_ref, caps_ref, ids_ref, gates_ref, both_ref, wide, sems = refs[6 + pieces :]
    choose, count = ids_ref.shape
    block = padded(2 * slots)
    pairs = [(ids_hbm, ids_ref), (plan_hbm, plan_ref), (caps_hbm, caps_ref), (gates_hbm, gates_ref)]
    for place, source in enumerate((tok_hbm, grad_hbm)):
        pairs.append((source, both_ref.at[pl.ds(place * count, count)]))
    copies = [
        pltpu.make_async_copy(source, target, sems.at[i])
        for i, (source, target) in enumerate(pairs)
    ]
    for copy in copies:
        copy.start()
    me = lax.axis_index("expert")
    row = lax.broadcasted_iota(I32, (block, count), 0)
    col = lax.broadcasted_iota(I32, (block, count), 1)
    is_cot = row >= slots
    slot = jnp.where(is_cot, row - slots, row)
    valid = row < 2 * slots
    is_spare = slot >= OWN
    spare_slot = jnp.maximum(slot - OWN, 0)
    replica = jnp.where(is_spare, 1 + lax.div(spare_slot, SPARE), 0)
    position = jnp.where(is_spare, lax.rem(spare_slot, SPARE), slot)
    token_slot = lax.rem(col, hosts)
    earlier = (
        lax.broadcasted_iota(I32, (count, count), 0) < lax.broadcasted_iota(I32, (count, count), 1)
    )
    earlier = earlier.astype(F32).astype(BF16)
    cots = jnp.concatenate([is_cot.astype(F32)] * experts, axis=0)
    for copy in copies[:4]:
        copy.wait()
    members, weights, limits = [], [], []
    for index in range(experts):
        expert = index if pieces == 1 else me ^ distance(index, experts)
        hot = (plan_ref[0, 0] == expert) | (plan_ref[1, 0] == expert)
        wanted = token_slot * hot.astype(I32)
        here = jnp.zeros((1, count), F32)
        weight = jnp.zeros((1, count), F32)
        for k in range(choose):
            chosen = ids_ref[k : k + 1, :] == expert
            here = jnp.where(chosen, 1.0, here)
            weight = jnp.where(chosen, gates_ref[k : k + 1, :], weight)
        fits = valid & (replica == wanted)
        members.append(jnp.where(fits, jnp.broadcast_to(here, fits.shape), 0.0))
        weights.append(jnp.broadcast_to(weight, fits.shape))
        room = jnp.where(is_spare, SPARE, caps_ref[expert] * BLK)
        limits.append(jnp.where(position < room, position, -1))
    member = jnp.concatenate(members, axis=0)
    weight = jnp.concatenate(weights, axis=0)
    limit = jnp.concatenate(limits, axis=0).astype(F32)
    before = matmul(member.astype(BF16), earlier, 1, 0)
    taken = jnp.where(before == limit, member, 0.0)
    pick_cot = taken * cots
    pick_tok = taken - pick_cot
    picks = jnp.concatenate([pick_tok.astype(BF16), pick_cot.astype(BF16)], axis=1)
    gate = jnp.sum(pick_cot * weight, axis=1, keepdims=True)
    scale = jnp.where(cots[:, :1] > 0.0, gate, 1.0)
    scaled_ref[...] = pick_tok * weight
    pick_ref[...] = pick_cot
    for copy in copies[4:]:
        copy.wait()
    send = scale * matmul(picks, both_ref[...], 1, 0)
    if pieces == 1:
        send_refs[0][...] = send.astype(BF16)
        return
    width = send.shape[1] // chunks
    used = 2 * slots * chunks
    if wide.shape[0] > used:
        wide[used:, :] = jnp.zeros((wide.shape[0] - used, width), F32)
    for i, send_ref in enumerate(send_refs):
        for j in range(chunks):
            rows = send[i * block : i * block + 2 * slots, j * width : (j + 1) * width]
            wide[2 * slots * j : 2 * slots * (j + 1), :] = rows
        send_ref[...] = wide[...].astype(BF16)


def dispatch(plan, caps, ids, gates, tokens, grads, experts, slots, chunks, pieces):
    count, feature = tokens.shape
    vmem = pl.BlockSpec(memory_space=pltpu.VMEM)
    block = padded(2 * slots)
    packed = (padded(2 * slots * chunks), feature // chunks)
    sent = (experts * block, feature) if pieces == 1 else packed
    outs = pl.pallas_call(
        functools.partial(dispatch_kernel, experts, plan.shape[1], slots, chunks, pieces),
        out_shape=(jax.ShapeDtypeStruct(sent, BF16),) * pieces
        + (jax.ShapeDtypeStruct((experts * block, count), F32),) * 2,
        in_specs=[pl.BlockSpec(memory_space=pltpu.HBM)] * 6,
        out_specs=(vmem,) * (pieces + 2),
        scratch_shapes=[
            pltpu.SMEM(plan.shape, I32),
            pltpu.SMEM(caps.shape, I32),
            pltpu.VMEM(ids.shape, I32),
            pltpu.VMEM(gates.shape, F32),
            pltpu.VMEM((2 * count, feature), BF16),
            pltpu.VMEM(packed, F32),
            pltpu.SemaphoreType.DMA((6,)),
        ],
        compiler_params=params(),
        name="dispatch",
    )(*(in_hbm(array) for array in (plan, caps, ids, gates, tokens, grads)))
    return outs[:pieces], outs[pieces:]


def load_kernel(
    gate_hbm, up_hbm, down_hbm, scaled_ref, pick_ref, gate_ref, up_ref, down_ref, merge_ref, sems
):
    copies = []
    for source, target in ((gate_hbm, gate_ref), (up_hbm, up_ref), (down_hbm, down_ref)):
        for start, size in spans(source.shape[0], source.shape[0] // LOADS):
            rows = pl.ds(start, size)
            copies.append(
                pltpu.make_async_copy(source.at[rows], target.at[rows], sems.at[len(copies)])
            )
    for copy in copies:
        copy.start()
    scaled = scaled_ref[...].T
    count = scaled.shape[0]
    high = scaled.astype(BF16)
    merge_ref[:count, :] = high
    merge_ref[count : 2 * count, :] = (scaled - high.astype(F32)).astype(BF16)
    merge_ref[2 * count :, :] = pick_ref[...].T.astype(BF16)
    for copy in copies:
        copy.wait()


def load_weights(gate, up, down, scaled, pick):
    hbm = pl.BlockSpec(memory_space=pltpu.HBM)
    vmem = pl.BlockSpec(memory_space=pltpu.VMEM)
    assert all(w.shape[0] % (16 * LOADS) == 0 for w in (gate, up, down))
    merge = jax.ShapeDtypeStruct((3 * pick.shape[1], pick.shape[0]), BF16)
    return pl.pallas_call(
        load_kernel,
        out_shape=tuple(pltpu.VMEM(w.shape, BF16) for w in (gate, up, down)) + (merge,),
        in_specs=[hbm, hbm, hbm, vmem, vmem],
        out_specs=(vmem,) * 4,
        scratch_shapes=[pltpu.SemaphoreType.DMA((3 * LOADS,))],
        compiler_params=params(),
        cost_estimate=pl.CostEstimate(
            flops=0, bytes_accessed=2 * 3 * gate.size * 2, transcendentals=0
        ),
        name="load_weights",
    )(in_hbm(gate), in_hbm(up), in_hbm(down), scaled, pick)


def half_columns(which, width):
    half = width // 2
    side = lax.rem(lax.axis_index("dp") + which, 2)
    return pl.ds(pl.multiple_of(side * half, half), half)


def half_partials(which, rows, cots, gate_ref, up_ref, down_ref, part_ref):
    width = gate_ref.shape[1]
    half = width // 2
    units = half_columns(which, width)
    both = jnp.concatenate([gate_ref[:, units], up_ref[:, units]], axis=1)
    part_ref[:, : 2 * half] = matmul(rows, both, 1, 0).astype(BF16)
    part_ref[:, 2 * half :] = matmul(cots, down_ref[units, :], 1, 1).astype(BF16)


def give_kernel(slots, chunks, pieces, *refs):
    recv_refs = refs[:pieces]
    gate_ref, up_ref, down_ref, rows_ref, cots_ref, give_ref, wide, flat = refs[pieces:]
    group, block, width = wide.shape
    for s in range(group):
        recv_ref, start = (recv_refs[0], s * block) if pieces == 1 else (recv_refs[s], 0)
        wide[s] = recv_ref[start : start + block, :].astype(F32)
        for j in range(chunks):
            columns = pl.ds(j * width, width)
            for kind in range(2):
                place = (2 * j + kind) * slots
                flat[kind, s * slots : (s + 1) * slots, columns] = wide[s, place : place + slots, :]
    rows = flat[0].astype(BF16)
    cots = flat[1].astype(BF16)
    rows_ref[...] = rows
    cots_ref[...] = cots
    half_partials(1, rows, cots, gate_ref, up_ref, down_ref, give_ref)


def keep_kernel(rows_ref, cots_ref, gate_ref, up_ref, down_ref, keep_ref):
    half_partials(0, rows_ref[...], cots_ref[...], gate_ref, up_ref, down_ref, keep_ref)


def add_kernel(left_ref, right_ref, sum_ref):
    sum_ref[...] = (left_ref[...].astype(F32) + right_ref[...].astype(F32)).astype(BF16)


def activate_kernel(near_ref, far_ref, mine_ref):
    half = mine_ref.shape[1] // 3
    total = near_ref[...].astype(F32) + far_ref[...].astype(F32)
    gate_pre, up_pre, hidden_grad = (total[:, i * half : (i + 1) * half] for i in range(3))
    sigma = jax.nn.sigmoid(gate_pre)
    active = gate_pre * sigma
    slope = sigma * (1.0 + gate_pre * (1.0 - sigma))
    mine_ref[:, :half] = (active * up_pre).astype(BF16)
    mine_ref[:, half : 2 * half] = (hidden_grad * up_pre * slope).astype(BF16)
    mine_ref[:, 2 * half :] = (hidden_grad * active).astype(BF16)


def half_outputs(which, acts_ref, gate_ref, up_ref, down_ref):
    width = gate_ref.shape[1]
    half = width // 2
    units = half_columns(which, width)
    outs = matmul(acts_ref[:, :half], down_ref[units, :], 1, 0)
    both = jnp.concatenate([gate_ref[:, units], up_ref[:, units]], axis=1)
    return outs, matmul(acts_ref[:, half:], both, 1, 1)


def own_kernel(mine_ref, gate_ref, up_ref, down_ref, outs_ref, ins_ref):
    outs_ref[...], ins_ref[...] = half_outputs(0, mine_ref, gate_ref, up_ref, down_ref)


def back_kernel(slots, chunks, pieces, *refs):
    theirs_ref, outs_ref, ins_ref, gate_ref, up_ref, down_ref = refs[:6]
    back_refs = refs[6 : 6 + pieces]
    flat, wide = refs[6 + pieces :]
    group, block, width = wide.shape
    outs, ins = half_outputs(1, theirs_ref, gate_ref, up_ref, down_ref)
    flat[0] = outs_ref[...] + outs
    flat[1] = ins_ref[...] + ins
    used = 2 * slots * chunks
    if block > used:
        wide[:, used:, :] = jnp.zeros((group, block - used, width), F32)
    for s in range(group):
        for j in range(chunks):
            columns = pl.ds(j * width, width)
            for kind in range(2):
                place = (2 * j + kind) * slots
                wide[s, place : place + slots, :] = flat[kind, s * slots : (s + 1) * slots, columns]
        back_ref, start = (back_refs[0], s * block) if pieces == 1 else (back_refs[s], 0)
        back_ref[start : start + block, :] = wide[s].astype(BF16)


def by_rows(kernel, name, steps, arrays, weights, outs, scratch=(), flops=0):
    def tiled(shape):
        return pl.BlockSpec((shape[0] // steps, shape[1]), lambda i: (i, 0))

    def whole(shape):
        return pl.BlockSpec(shape, lambda i: (0, 0))

    moved = sum(array.size * array.dtype.itemsize for array in (*arrays, *weights))
    results = pl.pallas_call(
        kernel,
        grid=(steps,),
        out_shape=tuple(jax.ShapeDtypeStruct(shape, dtype) for shape, dtype in outs),
        in_specs=[tiled(array.shape) for array in arrays] + [whole(w.shape) for w in weights],
        out_specs=tuple(tiled(shape) for shape, _ in outs),
        scratch_shapes=list(scratch),
        compiler_params=params(),
        cost_estimate=pl.CostEstimate(flops=flops, bytes_accessed=moved, transcendentals=0),
        name=name,
    )(*arrays, *weights)
    return results if len(outs) > 1 else results[0]


def grads_kernel(
    rows_ref, cots_ref, mine_ref, theirs_ref, gate_hbm, up_hbm, down_hbm, gate_ref, up_ref, down_ref, sems
):
    width = gate_ref.shape[1]
    half = width // 2
    copies = []

    def send(source, target, rows):
        copies.append(
            pltpu.make_async_copy(source.at[rows], target.at[rows], sems.at[len(copies)])
        )
        copies[-1].start()

    sides = [(mine_ref, half_columns(0, width)), (theirs_ref, half_columns(1, width))]
    for acts_ref, units in sides:
        for start, size in spans(half, CHUNK):
            rows = pl.ds(pl.multiple_of(units.start + start, 16), size)
            hidden = acts_ref[:, start : start + size]
            down_ref[rows, :] = matmul(hidden, cots_ref[...], 0, 0).astype(BF16)
            send(down_ref, down_hbm, rows)
    for place, out_ref, out_hbm in ((1, gate_ref, gate_hbm), (2, up_ref, up_hbm)):
        for start, size in spans(out_ref.shape[0], CHUNK):
            rows = pl.ds(start, size)
            for acts_ref, units in sides:
                grad = acts_ref[:, place * half : (place + 1) * half]
                out_ref[rows, units] = matmul(rows_ref[:, rows], grad, 0, 0).astype(BF16)
            send(out_ref, out_hbm, rows)
    for copy in copies:
        copy.wait()


def weight_grads(rows, cots, mine, theirs):
    total, feature = rows.shape
    width = 2 * mine.shape[1] // 3
    vmem = pl.BlockSpec(memory_space=pltpu.VMEM)
    hbm = pl.BlockSpec(memory_space=pltpu.HBM)
    shapes = ((feature, width), (feature, width), (width, feature))
    pieces = 2 * len(spans(feature, CHUNK)) + 2 * len(spans(width // 2, CHUNK))
    return pl.pallas_call(
        grads_kernel,
        out_shape=tuple(jax.ShapeDtypeStruct(shape, BF16) for shape in shapes),
        in_specs=[vmem] * 4,
        out_specs=(hbm,) * 3,
        scratch_shapes=[pltpu.VMEM(shape, BF16) for shape in shapes]
        + [pltpu.SemaphoreType.DMA((pieces,))],
        compiler_params=params(),
        cost_estimate=pl.CostEstimate(
            flops=6 * total * feature * width,
            bytes_accessed=6 * feature * width,
            transcendentals=0,
        ),
        name="weight_grads",
    )(rows, cots, mine, theirs)


def combine_kernel(columns, slots, chunks, pieces, *refs):
    back_refs = refs[:pieces]
    merge_ref, mixed_hbm, token_hbm, mixed_ref, token_ref, wide, flat, sems = refs[pieces:]
    if pieces > 1:
        rows, width, block = 2 * slots, back_refs[0].shape[1], padded(2 * slots)
        for i, back_ref in enumerate(back_refs):
            wide[i] = back_ref[...].astype(F32)
            if block > rows:
                gap = pl.ds(i * block + rows, block - rows)
                flat[gap, :] = jnp.zeros((block - rows, flat.shape[1]), F32)
            for j in range(chunks):
                part = pl.ds(j * width, width)
                flat[i * block : i * block + rows, part] = wide[i, j * rows : (j + 1) * rows, :]
    count = mixed_ref.shape[0]
    copies = []
    for start, size in columns:
        part = pl.ds(start, size)
        back = back_refs[0][:, part] if pieces == 1 else flat[:, part].astype(BF16)
        sums = matmul(merge_ref[...], back, 1, 0)
        mixed_ref[:, part] = (sums[:count] + sums[count : 2 * count]).astype(BF16)
        token_ref[:, part] = sums[2 * count :].astype(BF16)
        for source, target in ((mixed_ref, mixed_hbm), (token_ref, token_hbm)):
            copies.append(
                pltpu.make_async_copy(
                    source.at[:, part], target.at[:, part], sems.at[len(copies)]
                )
            )
            copies[-1].start()
    for copy in copies:
        copy.wait()


def combine(backs, merge, slots, chunks):
    pieces, feature, count = len(backs), chunks * backs[0].shape[1], merge.shape[0] // 3
    columns = spans(feature, 2 * CHUNK if feature % CHUNK == 0 else feature)
    vmem = pl.BlockSpec(memory_space=pltpu.VMEM)
    hbm = pl.BlockSpec(memory_space=pltpu.HBM)
    shape = (count, feature)
    staged = [(pieces, *backs[0].shape), (merge.shape[1], feature)] if pieces > 1 else [(8, 128)] * 2
    return pl.pallas_call(
        functools.partial(combine_kernel, columns, slots, chunks, pieces),
        out_shape=(jax.ShapeDtypeStruct(shape, BF16),) * 2,
        in_specs=[vmem] * (pieces + 1),
        out_specs=(hbm, hbm),
        scratch_shapes=[
            pltpu.VMEM(shape, BF16),
            pltpu.VMEM(shape, BF16),
            *(pltpu.VMEM(extent, F32) for extent in staged),
            pltpu.SemaphoreType.DMA((2 * len(columns),)),
        ],
        compiler_params=params(),
        name="combine",
    )(*backs, merge)


def swapped(array, axis, distance):
    return lax.ppermute(array, axis, [(i, i ^ distance) for i in range(lax.axis_size(axis))])


def over_experts(arrays, experts):
    if len(arrays) == 1:
        array = arrays[0]
        blocks = array.reshape(experts, -1, array.shape[1])
        moved = lax.all_to_all(blocks, "expert", split_axis=0, concat_axis=0, tiled=True)
        return [moved.reshape(array.shape)]
    moved = [swapped(arrays[i], "expert", distance(i, experts)) for i in range(1, experts)]
    return [arrays[0]] + moved


def shards(
    tokens,
    out_grad,
    gate_weights,
    expert_ids,
    replica_plan,
    cap_blocks,
    gate_weight,
    up_weight,
    down_weight,
):
    experts = lax.axis_size("expert")
    hosts = replica_plan.shape[1]
    assert tokens.shape[0] % hosts == 0 and experts % GROUP == 0
    assert all(n >= 4 and n & (n - 1) == 0 for n in (experts, lax.axis_size("dp")))
    slots = OWN + SPARE * (hosts - 1)
    gate, up, down = gate_weight[0], up_weight[0], down_weight[0]
    feature, width = gate.shape
    pieces = experts if experts <= GROUP and feature % CHUNK == 0 else 1
    chunks = feature // CHUNK if pieces > 1 else 1
    block = padded(2 * slots * chunks)
    sends, (scaled, pick) = dispatch(
        replica_plan,
        cap_blocks,
        expert_ids.T,
        gate_weights.T,
        tokens,
        out_grad,
        experts,
        slots,
        chunks,
        pieces,
    )
    recvs = over_experts(sends, experts)
    *weights, merge = load_weights(gate, up, down, scaled, pick)
    steps, total, half = experts // GROUP, experts * slots, 3 * width // 2
    layout = (slots, chunks, pieces)
    flops = 3 * total * feature * width
    scratch = [
        pltpu.VMEM((GROUP, block, feature // chunks), F32),
        pltpu.VMEM((2, GROUP * slots, feature), F32),
    ]
    rows, cots, give = by_rows(
        functools.partial(give_kernel, *layout),
        "give",
        steps,
        recvs,
        weights,
        [((total, feature), BF16), ((total, feature), BF16), ((total, half), BF16)],
        scratch,
        flops,
    )
    got = swapped(give, "dp", 1)
    keep = by_rows(
        keep_kernel, "keep", steps, [rows, cots], weights, [((total, half), BF16)], (), flops
    )
    near = by_rows(add_kernel, "add", steps, [keep, got], [], [((total, half), BF16)])
    step, last = 2, lax.axis_size("dp") // 2
    while step < last:
        far = swapped(near, "dp", step)
        near = by_rows(add_kernel, "add", steps, [near, far], [], [((total, half), BF16)])
        step *= 2
    far = swapped(near, "dp", last)
    mine = by_rows(activate_kernel, "activate", steps, [near, far], [], [((total, half), BF16)])
    theirs = swapped(mine, "dp", 1)
    outs, ins = by_rows(
        own_kernel, "own", steps, [mine], weights, [((total, feature), F32)] * 2, (), flops
    )
    backs = by_rows(
        functools.partial(back_kernel, *layout),
        "back",
        steps,
        [theirs, outs, ins],
        weights,
        [((experts * block // pieces, feature // chunks), BF16)] * pieces,
        scratch[::-1],
        flops,
    )
    returned = over_experts(backs if pieces > 1 else [backs], experts)
    gate_grad, up_grad, down_grad = weight_grads(rows, cots, mine, theirs)
    mixed, token_grad = combine(returned, merge, slots, chunks)
    return mixed, token_grad, gate_grad[None], up_grad[None], down_grad[None]


def solution(mesh):
    return jax.shard_map(
        shards,
        mesh=mesh,
        in_specs=(
            P(("groups", "expert"), "dp"),
            P(("groups", "expert"), "dp"),
            P(("groups", "expert"), None),
            P(("groups", "expert"), None),
            P("groups", None),
            P("groups"),
            P("expert", "dp", None),
            P("expert", "dp", None),
            P("expert", None, "dp"),
        ),
        out_specs=(
            P(("groups", "expert"), "dp"),
            P(("groups", "expert"), "dp"),
            P(("groups", "expert"), "dp", None),
            P(("groups", "expert"), "dp", None),
            P(("groups", "expert"), None, "dp"),
        ),
        check_vma=False,
    )
```
